32 devices in a mesh: groups: 2 (over y), ctx: 4 (over z), exp: 2 (over x), tp: 2 (over core).
Axes of the slice: x: 2, y: 2, z: 4, core: 2. Of those that a mesh axis runs over, the one named last changes fastest.
Arguments:
- queries: bfloat16 [1024, 4096], P(('groups', 'ctx'), ('exp', 'tp')), parts along dimension 0, may hold values from -6 to 6
- keys: bfloat16 [1024, 512], P(('groups', 'ctx')), parts along dimension 0, may hold values from -6 to 6
- values: bfloat16 [1024, 512], P(('groups', 'ctx')), parts along dimension 0, may hold values from -6 to 6
- out_weight: bfloat16 [4096, 2048], P(('exp', 'tp')), may hold values from -0.25 to 0.25
- resid: bfloat16 [1024, 2048], P(('groups', 'ctx', 'exp', 'tp')), parts along dimension 0, may hold values from -6 to 6
- expert_ids: int32 [1024, 8], P(('groups', 'ctx', 'exp')), parts along dimension 0, may hold values from 0 to 63, all different within a row; in each aligned block of 64 rows (0 to 63, 64 to 127, ...) at most 8 rows name the same one
- router_probs: float32 [1024, 8], P(('groups', 'ctx', 'exp')), parts along dimension 0, may hold values from 0.05 to 1
- w_gate: bfloat16 [128, 2048, 384], P(('ctx', 'exp'), None, 'tp'), may hold values from -0.125 to 0.125
- w_up: bfloat16 [128, 2048, 384], P(('ctx', 'exp'), None, 'tp'), may hold values from -0.125 to 0.125
- w_down: bfloat16 [128, 384, 2048], P(('ctx', 'exp'), 'tp'), may hold values from -0.4375 to 0.4375
Outputs:
- layer_out: bfloat16 [1024, 2048], P(('groups', 'ctx', 'exp', 'tp')), parts along dimension 0
The draws below stay inside these ranges and needn't reach their ends.
There are 2 independent parts, one for each index of `groups`. The reference program is written for one: setup_inputs(seed, part) draws one part's arguments, and reference() takes and returns one part's arrays. A program takes and returns all parts, laid end to end along the dimension named above; an argument that names none is the same for every part. Nothing has to cross between parts.
Inputs may be any that keep to these rules, and one draw needn't show every extreme that they name: `expert_ids`: each row names 8 different experts. Within the rows held by one index of ctx and exp (aligned blocks of 128 / 2 rows), no expert is named more than 8 times; in some such blocks some expert is named exactly 8 times.
All inputs are finite; a program needn't handle non-finite values.
Results may differ from the reference program's by a relative error of at most 0.01.
Values may be sent and summed in bfloat16 or wider, within the bound.
No kernel may reach another device: no remote copies, remote signals or barrier semaphores. Data moves between devices by JAX's collectives and lax.ppermute only.
A program may use at most 128 MiB of HBM per device.

```python
import math
import jax
import jax.numpy as jnp
import numpy as np
from jax import lax

D = 2048
FF = 768
HEAD_DIMENSION = 128
QUERY_HEADS = 32
KEY_VALUE_HEADS = 4
EXPERTS = 64
TOPK = 8
SEQ_CTX = 128
CAP = 8
SEQUENCE_TOKENS = 512
N_EXP = 2
N_TP = 2


def draw_keys(key, part):
    key = jax.random.fold_in(key, 3)
    sampled_values = jnp.clip(1.5 * jax.random.normal(key, (SEQUENCE_TOKENS, KEY_VALUE_HEADS * HEAD_DIMENSION), jnp.float32), -6.0, 6.0)
    return sampled_values.astype(jnp.bfloat16)


def draw_queries(key, part):
    key = jax.random.fold_in(key, 5)
    sampled_values = jnp.clip(1.5 * jax.random.normal(key, (SEQUENCE_TOKENS, QUERY_HEADS * HEAD_DIMENSION), jnp.float32), -6.0, 6.0)
    return sampled_values.astype(jnp.bfloat16)


def block_scale(stream_key, extent, shards, smallest, largest):
    loudness = 1.0
    for position, shards_of in shards:
        steps = jax.random.uniform(jax.random.fold_in(jax.random.fold_in(stream_key, 6), position), (shards_of,), jnp.float32, smallest / len(shards), largest / len(shards))
        loudness = loudness * jnp.repeat(jnp.exp(steps), extent[position] // shards_of).reshape((-1,) + (1,) * (len(extent) - 1 - position))
    return loudness


def shared_out(rng, own, number, rows, count, top, most, skew):
    ranking = jax.random.permutation(rng, count)
    packed, usual = shares(count, rows * top, most, skew, True), shares(count, rows * top, most, skew, False)
    places = jnp.arange(count)

    def named(tallies, offset_by):
        used = int((tallies > 0).sum())
        fixed = max(1, used // 4)
        shifted = fixed + (places - fixed + offset_by * (used - fixed)) % max(1, count - fixed)
        return jnp.zeros((count,), jnp.int32).at[ranking[jnp.where(places < fixed, places, shifted)]].set(jnp.asarray(tallies, jnp.int32))

    tallies = jnp.where(number % 4 == 0, named(packed, number // 4), named(usual, number - number // 4 - 1))
    mixed = jax.random.permutation(jax.random.fold_in(own, 3), count)
    giver, sink = mixed[0:count // 2 * 2:2], mixed[1:count // 2 * 2:2]
    margin = jnp.minimum(tallies[giver] - 1, most - tallies[sink]) // 2
    margin = jnp.where((giver == ranking[0]) | (sink == ranking[0]) | (tallies[sink] == 0), 0, jnp.maximum(margin, 0))
    shifted = jax.random.randint(jax.random.fold_in(own, 4), (count // 2,), 0, 1 << 20) % (margin + 1)
    tallies = tallies.at[giver].add(-shifted).at[sink].add(shifted)
    labels = jnp.searchsorted(jnp.cumsum(tallies), jnp.arange(rows * top), side="right").astype(jnp.int32)
    grid = labels.reshape(top, rows).T
    grid = grid[jax.random.permutation(jax.random.fold_in(own, 1), rows)]
    offset_by = jax.random.randint(jax.random.fold_in(own, 2), (rows, 1), 0, top)
    return jnp.take_along_axis(grid, (jnp.arange(top)[None, :] + offset_by) % top, axis=1)


def shares(count, total, reach, slope, full):
    weights = [(1 << 20) // math.isqrt(rank ** slope) + 1 for rank in range(1, count + 1)]
    largest = reach if full else min(reach, max(-(-total // count), total * weights[0] // sum(weights)))
    least = 1 if total - largest >= count - 1 else 0
    counts, surplus = [largest] + [least] * (count - 1), total - largest - least * (count - 1)
    while surplus > 0:
        free = [i for i in range(1, count) if counts[i] < largest] or [i for i in range(1, count) if counts[i] < reach]
        whole, budget = sum([weights[i] for i in free]), surplus
        for i in free:
            extra = min(reach - counts[i], max(1, budget * weights[i] // whole), surplus)
            counts[i] = counts[i] + extra
            surplus = surplus - extra
    return np.array(counts)


def noise(key, dims, scale, limit, shards=(), kind=jnp.bfloat16):
    values = scale * jax.random.normal(key, dims, jnp.float32)
    if shards:
        values = values * block_scale(key, dims, shards, -0.22, 0.18)
    return jnp.clip(values, -limit, limit).astype(kind)


def setup_inputs(seed: int = 0, part: int = 0) -> dict:
    splits = jax.random.split(jax.random.key(seed), 11)
    own_keys = jax.random.split(jax.random.fold_in(splits[10], part), 11)
    queries = draw_queries(jax.random.fold_in(jax.random.fold_in(splits[10], part), 71), part)
    keys = draw_keys(jax.random.fold_in(jax.random.fold_in(splits[10], part), 71), part)
    values = noise(own_keys[2], (SEQUENCE_TOKENS, KEY_VALUE_HEADS * HEAD_DIMENSION), 1.0, 6.0, ((0, 4),))
    out_weight = noise(splits[3], (QUERY_HEADS * HEAD_DIMENSION, D), (4 * HEAD_DIMENSION) ** -0.5, 0.25, ((0, 4),))
    resid = noise(own_keys[4], (SEQUENCE_TOKENS, D), 1.0, 6.0, ((0, 16),))
    expert_ids_keys = jax.random.split(jax.random.fold_in(own_keys[5], 1), SEQUENCE_TOKENS // (SEQ_CTX // N_EXP))
    expert_ids_turns = jax.random.permutation(jax.random.fold_in(own_keys[5], 3), SEQUENCE_TOKENS // (SEQ_CTX // N_EXP))
    expert_ids = jax.vmap(lambda own, number: shared_out(jax.random.fold_in(own_keys[5], 2), own, number, SEQ_CTX // N_EXP, EXPERTS, TOPK, CAP, 2))(expert_ids_keys, expert_ids_turns).reshape((SEQUENCE_TOKENS, TOPK))
    router_probs = jnp.clip(jnp.exp(math.log(1.0) - 2.9957323 * jax.random.uniform(own_keys[6], (SEQUENCE_TOKENS, TOPK), jnp.float32) ** block_scale(own_keys[6], (SEQUENCE_TOKENS, TOPK), ((0, 8),), -0.2, 0.2)), 0.05, 1.0)
    w_gate = noise(splits[7], (2 * EXPERTS, D, FF // 2), D ** -0.5, 0.125, ((0, 8), (2, 2)))
    w_up = noise(splits[8], (2 * EXPERTS, D, FF // 2), D ** -0.5, 0.125, ((0, 8), (2, 2)))
    w_down = noise(splits[9], (2 * EXPERTS, FF // 2, D), (FF // 4) ** -0.5, 0.4375, ((0, 8), (1, 2)))
    return dict(queries=queries, keys=keys, values=values, out_weight=out_weight, resid=resid, expert_ids=expert_ids, router_probs=router_probs, w_gate=w_gate, w_up=w_up, w_down=w_down)


def attention_heads(queries, keys, values):
    group_width = QUERY_HEADS // KEY_VALUE_HEADS
    query_all = queries.reshape(SEQUENCE_TOKENS, QUERY_HEADS, HEAD_DIMENSION)
    key_matrix = keys.reshape(SEQUENCE_TOKENS, KEY_VALUE_HEADS, HEAD_DIMENSION)
    value_matrix = values.reshape(SEQUENCE_TOKENS, KEY_VALUE_HEADS, HEAD_DIMENSION)
    places = jnp.arange(SEQUENCE_TOKENS, dtype=jnp.int32)
    causal = places[None, :] <= places[:, None]
    score_scale = 1.0 / math.sqrt(HEAD_DIMENSION)

    def one_head(head_index):
        query_rows = lax.dynamic_index_in_dim(query_all, head_index, 1, keepdims=False)
        shared = head_index // group_width
        key_rows = lax.dynamic_index_in_dim(key_matrix, shared, 1, keepdims=False)
        value_rows = lax.dynamic_index_in_dim(value_matrix, shared, 1, keepdims=False)
        scores = jnp.dot(query_rows, key_rows.T, preferred_element_type=jnp.float32) * score_scale
        scores = jnp.where(causal, scores, -jnp.inf)
        row_max = lax.optimization_barrier(jnp.max(scores, axis=1, keepdims=True))
        weights = jnp.exp(scores - row_max)
        weights = weights / lax.optimization_barrier(jnp.sum(weights, axis=1, keepdims=True))
        return jnp.dot(weights, value_rows.astype(jnp.float32), precision=lax.Precision.HIGHEST)
    per_head = lax.map(one_head, jnp.arange(QUERY_HEADS, dtype=jnp.int32))
    return jnp.transpose(per_head, (1, 0, 2)).reshape(SEQUENCE_TOKENS, QUERY_HEADS * HEAD_DIMENSION).astype(jnp.bfloat16)

def reference(queries, keys, values, out_weight, resid, expert_ids, router_probs, w_gate, w_up, w_down):
    attended = attention_heads(queries, keys, values)
    groups = N_EXP * N_TP
    width = QUERY_HEADS * HEAD_DIMENSION // groups
    grouped_att = attended.reshape(SEQUENCE_TOKENS, groups, width)
    grouped_weight = out_weight.reshape(groups, width, D)

    def add_group(total, index):
        columns = lax.dynamic_index_in_dim(grouped_att, index, 1, keepdims=False)
        rows_w = lax.dynamic_index_in_dim(grouped_weight, index, 0, keepdims=False)
        term = jnp.dot(columns, rows_w, preferred_element_type=jnp.float32)
        rounded = lax.optimization_barrier(term.astype(jnp.bfloat16))
        return (total + rounded.astype(jnp.float32), None)
    projected, _ = lax.scan(add_group, jnp.zeros((SEQUENCE_TOKENS, D), jnp.float32), jnp.arange(groups, dtype=jnp.int32))
    hidden = resid.astype(jnp.float32) + projected
    mean_square = lax.optimization_barrier(jnp.mean(hidden * hidden, axis=1, keepdims=True))
    normed = (hidden * lax.rsqrt(mean_square + 1e-06)).astype(jnp.bfloat16)
    gate_weights = router_probs / lax.optimization_barrier(jnp.sum(router_probs, axis=1, keepdims=True))
    block_rows = SEQ_CTX // N_EXP
    nblocks = SEQUENCE_TOKENS // block_rows
    quarter = FF // 4
    flat_ids = expert_ids.reshape(nblocks, block_rows * TOPK)
    onehot = (flat_ids[:, :, None] == jnp.arange(EXPERTS, dtype=jnp.int32)[None, None, :]).astype(jnp.int32)
    slots = lax.optimization_barrier(jnp.sum(onehot * (jnp.cumsum(onehot, axis=1) - 1), axis=2)).astype(jnp.int32)
    block_ids = jnp.broadcast_to(jnp.arange(nblocks, dtype=jnp.int32)[:, None], flat_ids.shape)
    token_of = block_ids * block_rows + jnp.arange(block_rows * TOPK, dtype=jnp.int32)[None, :] // TOPK
    buffer = jnp.zeros((EXPERTS, nblocks, CAP, D), jnp.bfloat16).at[flat_ids, block_ids, slots].set(normed[token_of])

    def one_expert(expert):
        expert_rows = lax.dynamic_index_in_dim(buffer, expert, 0, keepdims=False).reshape(nblocks * CAP, D)
        results = []
        for half_index in range(2):
            gate_rows = lax.dynamic_index_in_dim(w_gate, 2 * expert + half_index, 0, keepdims=False)
            up_rows = lax.dynamic_index_in_dim(w_up, 2 * expert + half_index, 0, keepdims=False)
            down_rows = lax.dynamic_index_in_dim(w_down, 2 * expert + half_index, 0, keepdims=False)
            for quarter_index in range(2):
                low = quarter_index * quarter
                gate_out = jnp.dot(expert_rows, gate_rows[:, low:low + quarter], preferred_element_type=jnp.float32)
                up_out = jnp.dot(expert_rows, up_rows[:, low:low + quarter], preferred_element_type=jnp.float32)
                activated = (jax.nn.silu(gate_out) * up_out).astype(jnp.bfloat16)
                results.append(jnp.dot(activated, down_rows[low:low + quarter, :], preferred_element_type=jnp.float32).astype(jnp.bfloat16))
        return jnp.stack(results).reshape(2, 2, nblocks * CAP, D)
    outputs = lax.map(one_expert, jnp.arange(EXPERTS, dtype=jnp.int32))
    picked = outputs[flat_ids, :, :, block_ids * CAP + slots]
    picked = picked.reshape(SEQUENCE_TOKENS, TOPK, 2, 2, D).astype(jnp.float32)
    routed = jnp.einsum('tk,tkhqd->td', gate_weights, picked, precision=lax.Precision.HIGHEST)
    return (hidden + routed).astype(jnp.bfloat16)
```

```python
import functools
import math

import jax
import jax.numpy as jnp
from jax import lax
from jax.experimental import pallas as pl
from jax.experimental.pallas import tpu as pltpu
from jax.sharding import PartitionSpec as P

HEAD_DIMENSION = 128
QUERY_HEADS = 32
KEY_VALUE_HEADS = 4
EXPERTS = 64
TOPK = 8
MIB = 1 << 20
BF = jnp.bfloat16
F32 = jnp.float32


def shift(x, axis, steps):
    size = lax.axis_size(axis)
    steps = steps % size
    if steps == 0:
        return x
    return lax.ppermute(x, axis, [(i, (i + steps) % size) for i in range(size)])


def attention_kernel(n_ctx, n_exp, n_tp, rows, heads, relative, place, q_ref, *refs):
    kv_refs, w_ref, o_ref = refs[:n_ctx], refs[n_ctx], refs[n_ctx + 1]
    k_all, v_all, att, att_rel = refs[n_ctx + 2 :]
    ctx, exp, tp = place[0], place[1], place[2]
    for z in range(n_ctx):
        k_all[z * rows : (z + 1) * rows, :] = kv_refs[z][:rows, :HEAD_DIMENSION]
        v_all[z * rows : (z + 1) * rows, :] = kv_refs[z][:rows, HEAD_DIMENSION:]
    column = lax.broadcasted_iota(jnp.int32, (rows, n_ctx * rows), 1)
    row = lax.broadcasted_iota(jnp.int32, (rows, n_ctx * rows), 0)
    allowed = (column <= row) | ((column >= rows) & (column < (ctx + 1) * rows))
    scale = 1.0 / math.sqrt(HEAD_DIMENSION)
    for h in range(heads):
        q = q_ref[:, h * HEAD_DIMENSION : (h + 1) * HEAD_DIMENSION]
        s = lax.dot_general(q, k_all[...], (((1,), (1,)), ((), ())), preferred_element_type=F32)
        s = jnp.where(allowed, s * scale, -1e30)
        weights = jnp.exp(s - jnp.max(s, axis=1, keepdims=True))
        total = jnp.sum(weights, axis=1, keepdims=True)
        out = jnp.dot(weights.astype(BF), v_all[...], preferred_element_type=F32)
        att[:, h * HEAD_DIMENSION : (h + 1) * HEAD_DIMENSION] = (out / total).astype(BF)
    part = rows // (n_exp * n_tp)
    if not relative:
        o_ref[...] = jnp.dot(att[...], w_ref[...], preferred_element_type=F32).astype(BF)
        return
    for t in range(n_tp):
        for x in range(n_exp):
            owner = lax.rem(exp - x + n_exp, n_exp) * n_tp + lax.rem(tp - t + n_tp, n_tp)
            source = pl.ds(pl.multiple_of(owner * part, part), part)
            at = (t * n_exp + x) * part
            att_rel[at : at + part, :] = att[source, :]
    o_ref[...] = jnp.dot(att_rel[...], w_ref[...], preferred_element_type=F32).astype(BF)


def attend_project(queries, pieces, out_weight, place, n_exp, n_tp, relative):
    rows, width = queries.shape
    n_ctx = len(pieces)
    model = out_weight.shape[1]
    vmem = pl.BlockSpec(memory_space=pltpu.VMEM)
    return pl.pallas_call(
        functools.partial(
            attention_kernel, n_ctx, n_exp, n_tp, rows, width // HEAD_DIMENSION, relative
        ),
        out_shape=jax.ShapeDtypeStruct((rows, model), BF),
        in_specs=[pl.BlockSpec(memory_space=pltpu.SMEM)] + [vmem] * (n_ctx + 2),
        out_specs=vmem,
        scratch_shapes=[
            pltpu.VMEM((n_ctx * rows, HEAD_DIMENSION), BF),
            pltpu.VMEM((n_ctx * rows, HEAD_DIMENSION), BF),
            pltpu.VMEM((rows, width), BF),
            pltpu.VMEM((rows, width), BF),
        ],
        compiler_params=pltpu.CompilerParams(vmem_limit_bytes=32 * MIB),
        cost_estimate=pl.CostEstimate(
            flops=2 * rows * width * (2 * n_ctx * rows + model),
            bytes_accessed=2 * (rows * width + width * model + rows * model),
            transcendentals=rows * n_ctx * rows * (width // HEAD_DIMENSION),
        ),
        name="attend_project",
    )(place, queries, *pieces, out_weight)


def expert_kernel(n_pieces, tokens, slots, halves, key_ref, weight_ref, *refs):
    pieces = refs[:n_pieces]
    wg_ref, wu_ref, wd_ref, mine_ref, other_ref = refs[n_pieces : n_pieces + 5]
    x_all, pick_all, out_all = refs[n_pieces + 5 :]
    step = pl.program_id(0)
    last = pl.num_programs(0) - 1
    part = tokens // n_pieces

    @pl.when(step == 0)
    def _():
        for i, piece in enumerate(pieces):
            x_all[i * part : (i + 1) * part, :] = piece[...]

    slot = lax.broadcasted_iota(jnp.int32, (slots, tokens), 0)
    chosen = slot == key_ref[pl.ds(step, 1), :]
    pick = jnp.where(chosen, 1.0, 0.0).astype(BF)
    scale = jnp.sum(jnp.where(chosen, weight_ref[pl.ds(step, 1), :], 0.0), axis=1, keepdims=True)
    x = jnp.dot(pick, x_all[...], preferred_element_type=F32).astype(BF)
    out = None
    for h in range(halves):
        gate = jnp.dot(x, wg_ref[h], preferred_element_type=F32)
        up = jnp.dot(x, wu_ref[h], preferred_element_type=F32)
        act = (gate * jax.nn.sigmoid(gate) * up).astype(BF)
        term = jnp.dot(act, wd_ref[h], preferred_element_type=F32)
        out = term if out is None else out + term
    here = pl.ds(pl.multiple_of(step * slots, slots), slots)
    pick_all[here, :] = pick
    out_all[here, :] = (out * scale).astype(BF)

    @pl.when(step == last)
    def _():
        routed = lax.dot_general(
            pick_all[...], out_all[...], (((0,), (0,)), ((), ())), preferred_element_type=F32
        ).astype(BF)
        half = tokens // 2
        mine_ref[...] = routed[:half]
        other_ref[...] = routed[half:]


def run_experts(keys, weights, pieces, w_gate, w_up, w_down, slots):
    n_exp, tokens = keys.shape
    rows, model, hidden = w_gate.shape
    halves = rows // n_exp
    part = tokens // len(pieces)

    def whole(shape):
        return pl.BlockSpec(shape, lambda e: (0,) * len(shape), pipeline_mode=pl.Buffered(1))

    out = jax.ShapeDtypeStruct((tokens // 2, model), BF)
    return pl.pallas_call(
        functools.partial(expert_kernel, len(pieces), tokens, slots, halves),
        grid=(n_exp,),
        out_shape=(out, out),
        in_specs=[whole((n_exp, tokens))] * 2
        + [whole((part, model))] * len(pieces)
        + [
            pl.BlockSpec((halves, model, hidden), lambda e: (e, 0, 0)),
            pl.BlockSpec((halves, model, hidden), lambda e: (e, 0, 0)),
            pl.BlockSpec((halves, hidden, model), lambda e: (e, 0, 0)),
        ],
        out_specs=[whole((tokens // 2, model))] * 2,
        scratch_shapes=[
            pltpu.VMEM((tokens, model), BF),
            pltpu.VMEM((n_exp * slots, tokens), BF),
            pltpu.VMEM((n_exp * slots, model), BF),
        ],
        compiler_params=pltpu.CompilerParams(vmem_limit_bytes=48 * MIB),
        cost_estimate=pl.CostEstimate(
            flops=2 * n_exp * slots * model * (3 * halves * hidden + 2 * tokens),
            bytes_accessed=6 * rows * model * hidden + 4 * tokens * model,
            transcendentals=n_exp * slots * halves * hidden,
        ),
        name="experts",
    )(keys, weights, *pieces, w_gate, w_up, w_down)


def experts_plain(keys, weights, x, w_gate, w_up, w_down, slots):
    n_exp = keys.shape[0]
    rows, model, hidden = w_gate.shape
    pick = (keys[:, None, :] == jnp.arange(slots, dtype=jnp.int32)[None, :, None]).astype(BF)
    scale = jnp.sum(pick.astype(F32) * weights[:, None, :], axis=2)
    chosen = jnp.einsum("est,td->esd", pick, x, preferred_element_type=F32).astype(BF)
    chosen = jnp.repeat(chosen, rows // n_exp, axis=0)
    gate = jnp.einsum("rsd,rdf->rsf", chosen, w_gate, preferred_element_type=F32)
    up = jnp.einsum("rsd,rdf->rsf", chosen, w_up, preferred_element_type=F32)
    act = (jax.nn.silu(gate) * up).astype(BF)
    out = jnp.einsum("rsf,rfd->rsd", act, w_down, preferred_element_type=F32)
    out = jnp.sum(out.reshape(n_exp, rows // n_exp, slots, model), axis=1)
    out = (out * scale[:, :, None]).astype(BF)
    return jnp.einsum("est,esd->td", pick, out, preferred_element_type=F32).astype(BF)


def on_device(
    queries, keys, values, out_weight, resid, expert_ids, router_probs, w_gate, w_up, w_down
):
    n_ctx, n_exp, n_tp = (lax.axis_size(a) for a in ("ctx", "exp", "tp"))
    ctx, exp, tp = (lax.axis_index(a) for a in ("ctx", "exp", "tp"))
    place = jnp.stack([ctx, exp, tp]).astype(jnp.int32)
    rows = queries.shape[0]
    part, model = resid.shape
    block = expert_ids.shape[0]
    heads_here = queries.shape[1] // HEAD_DIMENSION
    small = n_ctx * n_exp <= 8 and part % 16 == 0

    shared = (exp * n_tp + tp) * heads_here // (QUERY_HEADS // KEY_VALUE_HEADS)
    key_head = lax.dynamic_slice_in_dim(keys, shared * HEAD_DIMENSION, HEAD_DIMENSION, 1)
    value_head = lax.dynamic_slice_in_dim(values, shared * HEAD_DIMENSION, HEAD_DIMENSION, 1)
    gate_weights = router_probs / jnp.sum(router_probs, axis=1, keepdims=True)
    high = lax.reduce_precision(gate_weights, 8, 7)
    low = gate_weights - high
    routing = jnp.concatenate(
        [expert_ids.astype(F32).T, high.T, low.T], axis=1
    ).astype(BF)
    routing = jnp.pad(routing, ((0, 16 - TOPK), (0, 2 * HEAD_DIMENSION - 3 * block)))
    kv = jnp.concatenate([jnp.concatenate([key_head, value_head], axis=1), routing], axis=0)
    kv_pieces = [shift(kv, "ctx", z) for z in range(n_ctx)]
    routing = jnp.stack([piece[rows : rows + TOPK, : 3 * block] for piece in kv_pieces])
    routing = jnp.stack([shift(routing, "exp", x) for x in range(n_exp)], axis=1)

    routing = routing.reshape(n_ctx, n_exp, TOPK, 3, n_tp, part)
    routing = jnp.stack(
        [
            lax.dynamic_index_in_dim(routing, (tp - t) % n_tp, 4, keepdims=False)
            for t in range(n_tp)
        ],
        axis=4,
    )
    routing = routing.transpose(3, 2, 4, 0, 1, 5).astype(F32)
    ids = routing[0].astype(jnp.int32)
    probs = routing[1] + routing[2]
    rows_here = w_gate.shape[0]
    experts_here = max(1, rows_here // 2)
    device = ctx * n_exp + exp
    first = device * rows_here // 2
    local = first + jnp.arange(experts_here, dtype=jnp.int32)
    hit = ids[None] == local.reshape(-1, 1, 1, 1, 1, 1)
    named = jnp.any(hit, axis=1)
    weight = jnp.sum(jnp.where(hit, probs[None], 0.0), axis=1)
    cap = min(8, block)
    flat = named.transpose(0, 2, 3, 1, 4).reshape(-1, block)
    before = jnp.arange(block)[:, None] < jnp.arange(block)[None, :]
    rank = jnp.dot(flat.astype(BF), before.astype(BF), preferred_element_type=F32)
    rank = rank.astype(jnp.int32).reshape(experts_here, n_ctx, n_exp, n_tp, part)
    rank = rank.transpose(0, 3, 1, 2, 4)
    blocks = jnp.arange(n_ctx * n_exp, dtype=jnp.int32).reshape(1, 1, n_ctx, n_exp, 1)
    cells = jnp.where(named, blocks * cap + rank, -1).reshape(experts_here, -1)
    weight = weight.reshape(experts_here, -1)
    slots = n_ctx * n_exp * cap

    projected = attend_project(
        queries, kv_pieces, out_weight, place, n_exp, n_tp, small
    )
    hidden = resid.astype(F32)
    if small:
        projected = projected.reshape(n_tp, n_exp * part, model)
        summed = projected[0].astype(F32)
        for t in range(1, n_tp):
            summed = summed + shift(projected[t], "tp", -t).astype(F32)
        summed = summed.astype(BF).reshape(n_exp, part, model)
        hidden = hidden + summed[0].astype(F32)
        for x in range(1, n_exp):
            hidden = hidden + shift(summed[x], "exp", -x).astype(F32)
    else:
        hidden = hidden + lax.psum_scatter(
            projected, ("exp", "tp"), scatter_dimension=0, tiled=True
        ).astype(F32)
    mean_square = jnp.mean(hidden * hidden, axis=1, keepdims=True)
    normed = (hidden * lax.rsqrt(mean_square + 1e-06)).astype(BF)

    if small:
        along_z = [shift(normed, "ctx", z) for z in range(n_ctx)]
        chip = [shift(piece, "exp", x) for piece in along_z for x in range(n_exp)]
        pieces = [shift(piece, "tp", t) for t in range(n_tp) for piece in chip]
        mine, other = run_experts(cells, weight, pieces, w_gate, w_up, w_down, slots)
        both = mine.astype(F32) + shift(other, "tp", -1).astype(F32)
        both = both.astype(BF).reshape(n_ctx, n_exp, part, model)
        routed = None
        for z in range(n_ctx):
            line = both[z, 0].astype(F32)
            for x in range(1, n_exp):
                line = line + shift(both[z, x], "exp", -x).astype(F32)
            if z:
                line = shift(line.astype(BF), "ctx", -z).astype(F32)
            routed = line if routed is None else routed + line
    else:
        tokens = n_ctx * n_exp * n_tp * part
        x = lax.all_gather(normed, ("ctx", "exp", "tp"), axis=0, tiled=True)

        def absolute(table):
            table = table.reshape(experts_here, n_tp, n_ctx, n_exp, part)
            for axis, size, me in ((1, n_tp, tp), (2, n_ctx, ctx), (3, n_exp, exp)):
                order = (me - jnp.arange(size, dtype=jnp.int32)) % size
                table = jnp.take(table, order, axis=axis)
            return table.transpose(0, 2, 3, 1, 4).reshape(experts_here, tokens)

        partial = experts_plain(
            absolute(cells), absolute(weight), x, w_gate, w_up, w_down, slots
        )
        routed = lax.psum_scatter(
            partial, ("ctx", "exp", "tp"), scatter_dimension=0, tiled=True
        ).astype(F32)
    return (hidden + routed).astype(BF)


def solution(mesh):
    in_specs = (
        P(("groups", "ctx"), ("exp", "tp")),
        P(("groups", "ctx"), None),
        P(("groups", "ctx"), None),
        P(("exp", "tp"), None),
        P(("groups", "ctx", "exp", "tp"), None),
        P(("groups", "ctx", "exp"), None),
        P(("groups", "ctx", "exp"), None),
        P(("ctx", "exp"), None, "tp"),
        P(("ctx", "exp"), None, "tp"),
        P(("ctx", "exp"), "tp", None),
    )
    out_specs = P(("groups", "ctx", "exp", "tp"), None)
    return jax.shard_map(
        on_device, mesh=mesh, in_specs=in_specs, out_specs=out_specs, check_vma=False
    )
```

```python
import functools
import math

import jax
import jax.numpy as jnp
from jax import lax
from jax.experimental import pallas as pl
from jax.experimental.pallas import tpu as pltpu
from jax.sharding import PartitionSpec as P

HEAD_DIMENSION = 128
QUERY_HEADS = 32
KEY_VALUE_HEADS = 4
EXPERTS = 64
TOPK = 8
MIB = 1 << 20
BF = jnp.bfloat16
F32 = jnp.float32


def shift(x, axis, steps):
    size = lax.axis_size(axis)
    steps = steps % size
    if steps == 0:
        return x
    return lax.ppermute(x, axis, [(i, (i + steps) % size) for i in range(size)])


def dot_rows(a, b):
    return lax.dot_general(a, b, (((1,), (1,)), ((), ())), preferred_element_type=F32)


def attention_kernel(n_ctx, n_exp, n_tp, rows, heads, relative, place, q_ref, *refs):
    kv_refs, w_ref, o_ref = refs[:n_ctx], refs[n_ctx], refs[n_ctx + 1]
    k_all, v_all, att, att_rel, w_all, w_sem = refs[n_ctx + 2 :]
    fetch = pltpu.make_async_copy(w_ref, w_all, w_sem)
    fetch.start()
    ctx, exp, tp = place[0], place[1], place[2]
    for z in range(n_ctx):
        k_all[z * rows : (z + 1) * rows, :] = kv_refs[z][:rows, :HEAD_DIMENSION]
        v_all[z * rows : (z + 1) * rows, :] = kv_refs[z][:rows, HEAD_DIMENSION:]
    column = lax.broadcasted_iota(jnp.int32, (rows, n_ctx * rows), 1)
    row = lax.broadcasted_iota(jnp.int32, (rows, n_ctx * rows), 0)
    allowed = (column <= row) | ((column >= rows) & (column < (ctx + 1) * rows))
    scale = 1.0 / math.sqrt(HEAD_DIMENSION)
    for h in range(heads):
        q = q_ref[:, h * HEAD_DIMENSION : (h + 1) * HEAD_DIMENSION]
        s = dot_rows(q, k_all[...])
        s = jnp.where(allowed, s * scale, -1e30)
        weights = jnp.exp(s - jnp.max(s, axis=1, keepdims=True))
        total = jnp.sum(weights, axis=1, keepdims=True)
        out = jnp.dot(weights.astype(BF), v_all[...], preferred_element_type=F32)
        att[:, h * HEAD_DIMENSION : (h + 1) * HEAD_DIMENSION] = (out / total).astype(BF)
    part = rows // (n_exp * n_tp)
    if not relative:
        fetch.wait()
        o_ref[...] = jnp.dot(att[...], w_all[...], preferred_element_type=F32).astype(BF)
        return
    for t in range(n_tp):
        for x in range(n_exp):
            owner = lax.rem(exp - x + n_exp, n_exp) * n_tp + lax.rem(tp - t + n_tp, n_tp)
            source = pl.ds(pl.multiple_of(owner * part, part), part)
            at = (t * n_exp + x) * part
            att_rel[at : at + part, :] = att[source, :]
    fetch.wait()
    o_ref[...] = jnp.dot(att_rel[...], w_all[...], preferred_element_type=F32).astype(BF)


def attend_project(queries, pieces, out_weight, place, n_exp, n_tp, relative):
    rows, width = queries.shape
    n_ctx = len(pieces)
    model = out_weight.shape[1]
    vmem = pl.BlockSpec(memory_space=pltpu.VMEM)
    return pl.pallas_call(
        functools.partial(
            attention_kernel, n_ctx, n_exp, n_tp, rows, width // HEAD_DIMENSION, relative
        ),
        out_shape=jax.ShapeDtypeStruct((rows, model), BF),
        in_specs=[pl.BlockSpec(memory_space=pltpu.SMEM)] + [vmem] * (n_ctx + 1)
        + [pl.BlockSpec(memory_space=pltpu.HBM)],
        out_specs=vmem,
        scratch_shapes=[
            pltpu.VMEM((n_ctx * rows, HEAD_DIMENSION), BF),
            pltpu.VMEM((n_ctx * rows, HEAD_DIMENSION), BF),
            pltpu.VMEM((rows, width), BF),
            pltpu.VMEM((rows, width), BF),
            pltpu.VMEM((width, model), BF),
            pltpu.SemaphoreType.DMA,
        ],
        compiler_params=pltpu.CompilerParams(vmem_limit_bytes=32 * MIB),
        cost_estimate=pl.CostEstimate(
            flops=2 * rows * width * (2 * n_ctx * rows + model),
            bytes_accessed=2 * (rows * width + width * model + rows * model),
            transcendentals=rows * n_ctx * rows * (width // HEAD_DIMENSION),
        ),
        name="attend_project",
    )(place, queries, *pieces, out_weight)


def expert_kernel(n_pieces, tokens, slots, halves, key_ref, weight_ref, *refs):
    pieces = refs[:n_pieces]
    wg_ref, wu_ref, wd_ref, mine_ref, other_ref = refs[n_pieces : n_pieces + 5]
    x_all, pick_all, out_all = refs[n_pieces + 5 :]
    step = pl.program_id(0)
    last = pl.num_programs(0) - 1
    part = tokens // n_pieces

    @pl.when(step == 0)
    def _():
        for i, piece in enumerate(pieces):
            x_all[i * part : (i + 1) * part, :] = piece[...]

    slot = lax.broadcasted_iota(jnp.int32, (slots, tokens), 0)
    chosen = slot == key_ref[pl.ds(step, 1), :]
    pick = jnp.where(chosen, 1.0, 0.0).astype(BF)
    scale = jnp.sum(jnp.where(chosen, weight_ref[pl.ds(step, 1), :], 0.0), axis=1, keepdims=True)
    x = jnp.dot(pick, x_all[...], preferred_element_type=F32).astype(BF)
    out = None
    for h in range(halves):
        gate = dot_rows(x, wg_ref[h])
        up = dot_rows(x, wu_ref[h])
        act = (gate * jax.nn.sigmoid(gate) * up).astype(BF)
        term = jnp.dot(act, wd_ref[h], preferred_element_type=F32)
        out = term if out is None else out + term
    here = pl.ds(pl.multiple_of(step * slots, slots), slots)
    pick_all[here, :] = pick
    out_all[here, :] = (out * scale).astype(BF)

    @pl.when(step == last)
    def _():
        routed = lax.dot_general(
            pick_all[...], out_all[...], (((0,), (0,)), ((), ())), preferred_element_type=F32
        ).astype(BF)
        half = tokens // 2
        mine_ref[...] = routed[:half]
        other_ref[...] = routed[half:]


def run_experts(keys, weights, pieces, w_gate, w_up, w_down, slots):
    n_exp, tokens = keys.shape
    rows, hidden, model = w_down.shape
    halves = rows // n_exp
    part = tokens // len(pieces)
    w_gate = jnp.swapaxes(w_gate, 1, 2)
    w_up = jnp.swapaxes(w_up, 1, 2)

    def whole(shape):
        return pl.BlockSpec(shape, lambda e: (0,) * len(shape), pipeline_mode=pl.Buffered(1))

    out = jax.ShapeDtypeStruct((tokens // 2, model), BF)
    return pl.pallas_call(
        functools.partial(expert_kernel, len(pieces), tokens, slots, halves),
        grid=(n_exp,),
        out_shape=(out, out),
        in_specs=[whole((n_exp, tokens))] * 2
        + [whole((part, model))] * len(pieces)
        + [
            pl.BlockSpec((halves, hidden, model), lambda e: (e, 0, 0)),
            pl.BlockSpec((halves, hidden, model), lambda e: (e, 0, 0)),
            pl.BlockSpec((halves, hidden, model), lambda e: (e, 0, 0)),
        ],
        out_specs=[whole((tokens // 2, model))] * 2,
        scratch_shapes=[
            pltpu.VMEM((tokens, model), BF),
            pltpu.VMEM((n_exp * slots, tokens), BF),
            pltpu.VMEM((n_exp * slots, model), BF),
        ],
        compiler_params=pltpu.CompilerParams(vmem_limit_bytes=48 * MIB),
        cost_estimate=pl.CostEstimate(
            flops=2 * n_exp * slots * model * (3 * halves * hidden + 2 * tokens),
            bytes_accessed=6 * rows * model * hidden + 4 * tokens * model,
            transcendentals=n_exp * slots * halves * hidden,
        ),
        name="experts",
    )(keys, weights, *pieces, w_gate, w_up, w_down)


def experts_plain(keys, weights, x, w_gate, w_up, w_down, slots):
    n_exp = keys.shape[0]
    rows, model, hidden = w_gate.shape
    pick = (keys[:, None, :] == jnp.arange(slots, dtype=jnp.int32)[None, :, None]).astype(BF)
    scale = jnp.sum(pick.astype(F32) * weights[:, None, :], axis=2)
    chosen = jnp.einsum("est,td->esd", pick, x, preferred_element_type=F32).astype(BF)
    chosen = jnp.repeat(chosen, rows // n_exp, axis=0)
    gate = jnp.einsum("rsd,rdf->rsf", chosen, w_gate, preferred_element_type=F32)
    up = jnp.einsum("rsd,rdf->rsf", chosen, w_up, preferred_element_type=F32)
    act = (jax.nn.silu(gate) * up).astype(BF)
    out = jnp.einsum("rsf,rfd->rsd", act, w_down, preferred_element_type=F32)
    out = jnp.sum(out.reshape(n_exp, rows // n_exp, slots, model), axis=1)
    out = (out * scale[:, :, None]).astype(BF)
    return jnp.einsum("est,esd->td", pick, out, preferred_element_type=F32).astype(BF)


def on_device(
    queries, keys, values, out_weight, resid, expert_ids, router_probs, w_gate, w_up, w_down
):
    n_ctx, n_exp, n_tp = (lax.axis_size(a) for a in ("ctx", "exp", "tp"))
    ctx, exp, tp = (lax.axis_index(a) for a in ("ctx", "exp", "tp"))
    place = jnp.stack([ctx, exp, tp]).astype(jnp.int32)
    rows = queries.shape[0]
    part, model = resid.shape
    block = expert_ids.shape[0]
    heads_here = queries.shape[1] // HEAD_DIMENSION
    small = n_ctx * n_exp <= 8 and part % 16 == 0

    shared = (exp * n_tp + tp) * heads_here // (QUERY_HEADS // KEY_VALUE_HEADS)
    key_head = lax.dynamic_slice_in_dim(keys, shared * HEAD_DIMENSION, HEAD_DIMENSION, 1)
    value_head = lax.dynamic_slice_in_dim(values, shared * HEAD_DIMENSION, HEAD_DIMENSION, 1)
    gate_weights = router_probs / jnp.sum(router_probs, axis=1, keepdims=True)
    high = lax.reduce_precision(gate_weights, 8, 7)
    low = gate_weights - high
    routing = jnp.concatenate(
        [expert_ids.astype(F32).T, high.T, low.T], axis=1
    ).astype(BF)
    routing = jnp.pad(routing, ((0, 16 - TOPK), (0, 2 * HEAD_DIMENSION - 3 * block)))
    kv = jnp.concatenate([jnp.concatenate([key_head, value_head], axis=1), routing], axis=0)
    kv_pieces = [shift(kv, "ctx", z) for z in range(n_ctx)]
    routing = jnp.stack([piece[rows : rows + TOPK, : 3 * block] for piece in kv_pieces])
    routing = jnp.stack([shift(routing, "exp", x) for x in range(n_exp)], axis=1)

    routing = routing.reshape(n_ctx, n_exp, TOPK, 3, n_tp, part)
    routing = jnp.stack(
        [
            lax.dynamic_index_in_dim(routing, (tp - t) % n_tp, 4, keepdims=False)
            for t in range(n_tp)
        ],
        axis=4,
    )
    routing = routing.transpose(3, 2, 4, 0, 1, 5).astype(F32)
    ids = routing[0].astype(jnp.int32)
    probs = routing[1] + routing[2]
    rows_here = w_gate.shape[0]
    experts_here = max(1, rows_here // 2)
    device = ctx * n_exp + exp
    first = device * rows_here // 2
    local = first + jnp.arange(experts_here, dtype=jnp.int32)
    hit = ids[None] == local.reshape(-1, 1, 1, 1, 1, 1)
    named = jnp.any(hit, axis=1)
    weight = jnp.sum(jnp.where(hit, probs[None], 0.0), axis=1)
    cap = min(8, block)
    flat = named.transpose(0, 2, 3, 1, 4).reshape(-1, block)
    before = jnp.arange(block)[:, None] < jnp.arange(block)[None, :]
    rank = jnp.dot(flat.astype(BF), before.astype(BF), preferred_element_type=F32)
    rank = rank.astype(jnp.int32).reshape(experts_here, n_ctx, n_exp, n_tp, part)
    rank = rank.transpose(0, 3, 1, 2, 4)
    blocks = jnp.arange(n_ctx * n_exp, dtype=jnp.int32).reshape(1, 1, n_ctx, n_exp, 1)
    cells = jnp.where(named, blocks * cap + rank, -1).reshape(experts_here, -1)
    weight = weight.reshape(experts_here, -1)
    slots = n_ctx * n_exp * cap

    projected = attend_project(
        queries, kv_pieces, out_weight, place, n_exp, n_tp, small
    )
    hidden = resid.astype(F32)
    if small:
        projected = projected.reshape(n_tp, n_exp * part, model)
        summed = projected[0].astype(F32)
        for t in range(1, n_tp):
            summed = summed + shift(projected[t], "tp", -t).astype(F32)
        summed = summed.astype(BF).reshape(n_exp, part, model)
        hidden = hidden + summed[0].astype(F32)
        for x in range(1, n_exp):
            hidden = hidden + shift(summed[x], "exp", -x).astype(F32)
    else:
        hidden = hidden + lax.psum_scatter(
            projected, ("exp", "tp"), scatter_dimension=0, tiled=True
        ).astype(F32)
    mean_square = jnp.mean(hidden * hidden, axis=1, keepdims=True)
    normed = (hidden * lax.rsqrt(mean_square + 1e-06)).astype(BF)

    if small:
        along_z = [shift(normed, "ctx", z) for z in range(n_ctx)]
        chip = [shift(piece, "exp", x) for piece in along_z for x in range(n_exp)]
        pieces = [shift(piece, "tp", t) for t in range(n_tp) for piece in chip]
        mine, other = run_experts(cells, weight, pieces, w_gate, w_up, w_down, slots)
        both = mine.astype(F32) + shift(other, "tp", -1).astype(F32)
        both = both.astype(BF).reshape(n_ctx, n_exp, part, model)
        routed = None
        for z in range(n_ctx):
            line = both[z, 0].astype(F32)
            for x in range(1, n_exp):
                line = line + shift(both[z, x], "exp", -x).astype(F32)
            if z:
                line = shift(line.astype(BF), "ctx", -z).astype(F32)
            routed = line if routed is None else routed + line
    else:
        tokens = n_ctx * n_exp * n_tp * part
        x = lax.all_gather(normed, ("ctx", "exp", "tp"), axis=0, tiled=True)

        def absolute(table):
            table = table.reshape(experts_here, n_tp, n_ctx, n_exp, part)
            for axis, size, me in ((1, n_tp, tp), (2, n_ctx, ctx), (3, n_exp, exp)):
                order = (me - jnp.arange(size, dtype=jnp.int32)) % size
                table = jnp.take(table, order, axis=axis)
            return table.transpose(0, 2, 3, 1, 4).reshape(experts_here, tokens)

        partial = experts_plain(
            absolute(cells), absolute(weight), x, w_gate, w_up, w_down, slots
        )
        routed = lax.psum_scatter(
            partial, ("ctx", "exp", "tp"), scatter_dimension=0, tiled=True
        ).astype(F32)
    return (hidden + routed).astype(BF)


def solution(mesh):
    in_specs = (
        P(("groups", "ctx"), ("exp", "tp")),
        P(("groups", "ctx"), None),
        P(("groups", "ctx"), None),
        P(("exp", "tp"), None),
        P(("groups", "ctx", "exp", "tp"), None),
        P(("groups", "ctx", "exp"), None),
        P(("groups", "ctx", "exp"), None),
        P(("ctx", "exp"), None, "tp"),
        P(("ctx", "exp"), None, "tp"),
        P(("ctx", "exp"), "tp", None),
    )
    out_specs = P(("groups", "ctx", "exp", "tp"), None)
    return jax.shard_map(
        on_device, mesh=mesh, in_specs=in_specs, out_specs=out_specs, check_vma=False
    )
```

```python
import functools
import math

import jax
import jax.numpy as jnp
from jax import lax
from jax.experimental import pallas as pl
from jax.experimental.pallas import tpu as pltpu
from jax.sharding import PartitionSpec as P

HEAD_DIMENSION = 128
QUERY_HEADS = 32
KEY_VALUE_HEADS = 4
EXPERTS = 64
TOPK = 8
MIB = 1 << 20
BF = jnp.bfloat16
F32 = jnp.float32


def flip(x, axis, bit):
    return lax.ppermute(x, axis, [(i, i ^ bit) for i in range(lax.axis_size(axis))])


def from_earlier(x, axis, steps):
    size = lax.axis_size(axis)
    return lax.ppermute(x, axis, [(i, i + steps) for i in range(size - steps)])


def dot_rows(a, b):
    return lax.dot_general(a, b, (((1,), (1,)), ((), ())), preferred_element_type=F32)


def attention_kernel(n_ctx, n_exp, n_tp, rows, heads, relative, place, *refs):
    kv_refs, (q_hbm, w_hbm, o_ref) = refs[:n_ctx], refs[n_ctx : n_ctx + 3]
    k_all, v_all, q_all, att, att_rel, w_all, q_sem, w_sem = refs[n_ctx + 3 :]
    fetch_q = []
    for h in range(heads):
        columns = slice(h * HEAD_DIMENSION, (h + 1) * HEAD_DIMENSION)
        fetch_q.append(
            pltpu.make_async_copy(q_hbm.at[:, columns], q_all.at[:, columns], q_sem.at[h])
        )
        fetch_q[h].start()
    fetch_w = pltpu.make_async_copy(w_hbm, w_all, w_sem)
    fetch_w.start()
    ctx, exp, tp = place[0], place[1], place[2]
    for z in range(n_ctx):
        k_all[z * rows : (z + 1) * rows, :] = kv_refs[z][:, :HEAD_DIMENSION]
        v_all[z * rows : (z + 1) * rows, :] = kv_refs[z][:, HEAD_DIMENSION:]
    column = lax.broadcasted_iota(jnp.int32, (rows, n_ctx * rows), 1)
    row = lax.broadcasted_iota(jnp.int32, (rows, n_ctx * rows), 0)
    allowed = (column <= row) | ((column >= rows) & (column < (ctx + 1) * rows))
    scale = 1.0 / math.sqrt(HEAD_DIMENSION)
    for h in range(heads):
        columns = slice(h * HEAD_DIMENSION, (h + 1) * HEAD_DIMENSION)
        fetch_q[h].wait()
        s = dot_rows(q_all[:, columns], k_all[...])
        s = jnp.where(allowed, s * scale, -1e30)
        weights = jnp.exp(s - jnp.max(s, axis=1, keepdims=True))
        total = jnp.sum(weights, axis=1, keepdims=True)
        out = jnp.dot(weights.astype(BF), v_all[...], preferred_element_type=F32)
        att[:, columns] = (out / total).astype(BF)
    if relative:
        part = rows // (n_exp * n_tp)
        for t in range(n_tp):
            for x in range(n_exp):
                owner = lax.rem(exp + x, n_exp) * n_tp + lax.rem(tp + t, n_tp)
                source = pl.ds(pl.multiple_of(owner * part, part), part)
                at = (t * n_exp + x) * part
                att_rel[at : at + part, :] = att[source, :]
        att = att_rel
    fetch_w.wait()
    o_ref[...] = jnp.dot(att[...], w_all[...], preferred_element_type=F32).astype(BF)


def attend_project(queries, pieces, out_weight, place, n_exp, n_tp, relative):
    rows, width = queries.shape
    n_ctx, heads = len(pieces), width // HEAD_DIMENSION
    model = out_weight.shape[1]
    vmem = pl.BlockSpec(memory_space=pltpu.VMEM)
    hbm = pl.BlockSpec(memory_space=pltpu.HBM)
    return pl.pallas_call(
        functools.partial(attention_kernel, n_ctx, n_exp, n_tp, rows, heads, relative),
        out_shape=jax.ShapeDtypeStruct((rows, model), BF),
        in_specs=[pl.BlockSpec(memory_space=pltpu.SMEM)] + [vmem] * n_ctx + [hbm] * 2,
        out_specs=vmem,
        scratch_shapes=[
            pltpu.VMEM((n_ctx * rows, HEAD_DIMENSION), BF),
            pltpu.VMEM((n_ctx * rows, HEAD_DIMENSION), BF),
            pltpu.VMEM((rows, width), BF),
            pltpu.VMEM((rows, width), BF),
            pltpu.VMEM((rows, width), BF),
            pltpu.VMEM((width, model), BF),
            pltpu.SemaphoreType.DMA((heads,)),
            pltpu.SemaphoreType.DMA,
        ],
        compiler_params=pltpu.CompilerParams(vmem_limit_bytes=32 * MIB),
        cost_estimate=pl.CostEstimate(
            flops=2 * rows * width * (2 * n_ctx * rows + model),
            bytes_accessed=2 * (rows * width + width * model + rows * model),
            transcendentals=rows * n_ctx * rows * heads,
        ),
        name="attend_project",
    )(
        place,
        *pieces,
        pltpu.with_memory_space_constraint(queries, pltpu.HBM),
        pltpu.with_memory_space_constraint(out_weight, pltpu.HBM),
    )


def expert_kernel(n_pieces, depth, key_ref, weight_ref, *refs):
    pieces, (wg_hbm, wu_hbm, wd_hbm) = refs[:n_pieces], refs[n_pieces : n_pieces + 3]
    outs = refs[n_pieces + 3 : n_pieces + 7]
    x_all, pick_all, scale_all, out_all, wgu, wd, act, sems = refs[n_pieces + 7 :]
    experts, tokens = key_ref.shape
    slots = pick_all.shape[0] // experts
    _, _, halves, hidden, model = wgu.shape
    part = tokens // n_pieces

    def copies(e):
        slot = lax.rem(e, depth)
        rows = pl.ds(e * halves, halves)
        return (
            pltpu.make_async_copy(wg_hbm.at[rows], wgu.at[slot, 0], sems.at[0, slot]),
            pltpu.make_async_copy(wu_hbm.at[rows], wgu.at[slot, 1], sems.at[1, slot]),
            pltpu.make_async_copy(wd_hbm.at[rows], wd.at[slot], sems.at[2, slot]),
        )

    def start(e):
        for copy in copies(e):
            copy.start()

    def wait(e):
        for copy in copies(e):
            copy.wait()

    def gate_up(e):
        x = out_all[pl.ds(pl.multiple_of(e * slots, slots), slots), :]
        weight = wgu[lax.rem(e, depth)].reshape(2 * halves * hidden, model)
        both = dot_rows(weight, x)
        gate, up = both[: halves * hidden], both[halves * hidden :]
        return (gate * jax.nn.sigmoid(gate) * up).astype(BF)

    def down(e):
        here = pl.ds(pl.multiple_of(e * slots, slots), slots)
        weight = wd[lax.rem(e, depth)].reshape(halves * hidden, model)
        out = lax.dot_general(
            act[lax.rem(e, 2)], weight, (((0,), (0,)), ((), ())), preferred_element_type=F32
        )
        return here, (out * scale_all[here, :]).astype(BF)

    for e in range(min(depth - 1, experts)):
        start(e)
    for i, piece in enumerate(pieces):
        x_all[i * part : (i + 1) * part, :] = piece[...]
    slot = lax.broadcasted_iota(jnp.int32, (slots, tokens), 0)
    for e in range(experts):
        chosen = slot == key_ref[e : e + 1, :]
        here = slice(e * slots, (e + 1) * slots)
        pick_all[here, :] = jnp.where(chosen, 1.0, 0.0).astype(BF)
        scale_all[here, :] = jnp.sum(
            jnp.where(chosen, weight_ref[e : e + 1, :], 0.0), axis=1, keepdims=True
        )
    out_all[...] = jnp.dot(pick_all[...], x_all[...], preferred_element_type=F32).astype(BF)
    wait(0)
    act[0] = gate_up(0)

    @pl.loop(0, experts - 1)
    def _(e):
        @pl.when(e + depth - 1 < experts)
        def _():
            start(e + depth - 1)

        wait(e + 1)
        following = gate_up(e + 1)
        here, out = down(e)
        act[lax.rem(e + 1, 2)] = following
        out_all[here, :] = out

    here, out = down(experts - 1)
    out_all[here, :] = out
    quarter = tokens // 4
    for i, o_ref in enumerate(outs):
        o_ref[...] = lax.dot_general(
            pick_all[:, i * quarter : (i + 1) * quarter],
            out_all[...],
            (((0,), (0,)), ((), ())),
            preferred_element_type=F32,
        ).astype(BF)


def run_experts(keys, weights, pieces, w_gate, w_up, w_down, slots):
    experts, tokens = keys.shape
    rows, hidden, model = w_down.shape
    halves = rows // experts
    depth = min(4, experts)
    vmem = pl.BlockSpec(memory_space=pltpu.VMEM)
    hbm = pl.BlockSpec(memory_space=pltpu.HBM)

    def stays(x):
        return pltpu.with_memory_space_constraint(x, pltpu.HBM)

    out = jax.ShapeDtypeStruct((tokens // 4, model), BF)
    return pl.pallas_call(
        functools.partial(expert_kernel, len(pieces), depth),
        out_shape=(out,) * 4,
        in_specs=[vmem] * (2 + len(pieces)) + [hbm] * 3,
        out_specs=(vmem,) * 4,
        scratch_shapes=[
            pltpu.VMEM((tokens, model), BF),
            pltpu.VMEM((experts * slots, tokens), BF),
            pltpu.VMEM((experts * slots, 1), F32),
            pltpu.VMEM((experts * slots, model), BF),
            pltpu.VMEM((depth, 2, halves, hidden, model), BF),
            pltpu.VMEM((depth, halves, hidden, model), BF),
            pltpu.VMEM((2, halves * hidden, slots), BF),
            pltpu.SemaphoreType.DMA((3, depth)),
        ],
        compiler_params=pltpu.CompilerParams(vmem_limit_bytes=44 * MIB),
        cost_estimate=pl.CostEstimate(
            flops=2 * experts * slots * model * (3 * halves * hidden + 2 * tokens),
            bytes_accessed=6 * rows * model * hidden + 4 * tokens * model,
            transcendentals=experts * slots * halves * hidden,
        ),
        name="experts",
    )(
        keys,
        weights,
        *pieces,
        stays(jnp.swapaxes(w_gate, 1, 2)),
        stays(jnp.swapaxes(w_up, 1, 2)),
        stays(w_down),
    )


def experts_plain(keys, weights, x, w_gate, w_up, w_down, slots):
    n_exp = keys.shape[0]
    rows, model, hidden = w_gate.shape
    pick = (keys[:, None, :] == jnp.arange(slots, dtype=jnp.int32)[None, :, None]).astype(BF)
    scale = jnp.sum(pick.astype(F32) * weights[:, None, :], axis=2)
    chosen = jnp.einsum("est,td->esd", pick, x, preferred_element_type=F32).astype(BF)
    chosen = jnp.repeat(chosen, rows // n_exp, axis=0)
    gate = jnp.einsum("rsd,rdf->rsf", chosen, w_gate, preferred_element_type=F32)
    up = jnp.einsum("rsd,rdf->rsf", chosen, w_up, preferred_element_type=F32)
    act = (jax.nn.silu(gate) * up).astype(BF)
    out = jnp.einsum("rsf,rfd->rsd", act, w_down, preferred_element_type=F32)
    out = jnp.sum(out.reshape(n_exp, rows // n_exp, slots, model), axis=1)
    out = (out * scale[:, :, None]).astype(BF)
    return jnp.einsum("est,esd->td", pick, out, preferred_element_type=F32).astype(BF)


def routing_tables(routing, n_ctx, n_exp, n_tp, first, experts_here, cap):
    part = routing.shape[-1]
    routing = routing.transpose(2, 3, 4, 1, 0, 5).astype(F32)
    ids = routing[0].astype(jnp.int32)
    probs = routing[1] + routing[2]
    local = first + jnp.arange(experts_here, dtype=jnp.int32)
    hit = ids[None] == local.reshape(-1, 1, 1, 1, 1, 1)
    named = jnp.any(hit, axis=1)
    weight = jnp.sum(jnp.where(hit, probs[None], 0.0), axis=1)
    block = n_tp * part
    flat = named.transpose(0, 2, 3, 1, 4).reshape(-1, block)
    before = jnp.arange(block)[:, None] < jnp.arange(block)[None, :]
    rank = jnp.dot(flat.astype(BF), before.astype(BF), preferred_element_type=F32)
    rank = rank.astype(jnp.int32).reshape(experts_here, n_exp, n_ctx, n_tp, part)
    rank = rank.transpose(0, 3, 1, 2, 4)
    blocks = jnp.arange(n_ctx * n_exp, dtype=jnp.int32).reshape(1, 1, n_exp, n_ctx, 1)
    cells = jnp.where(named, blocks * cap + rank, -1).reshape(experts_here, -1)
    return cells, weight.reshape(experts_here, -1)


def sums_back(mine, mine_across, other, other_across, part):
    def add(a, *others):
        total = a.astype(F32)
        for b in others:
            total = total + b.astype(F32)
        return total.astype(BF)

    across = add(mine_across, flip(other_across, "tp", 1))
    here = add(mine, flip(other, "tp", 1))
    across = [across[z * part : (z + 1) * part] for z in range(4)]
    here = [here[z * part : (z + 1) * part] for z in range(4)]
    far_across = add(across[2], flip(across[3], "ctx", 1))
    own = flip(across[0], "exp", 1)
    near = flip(across[1], "exp", 1)
    last = flip(here[3], "ctx", 1)
    far_across, here[1] = lax.optimization_barrier((far_across, here[1]))
    far = flip(far_across, "exp", 1)
    near = add(here[1], near)
    near, here[2] = lax.optimization_barrier((near, here[2]))
    near = flip(near, "ctx", 1)
    far = flip(add(here[2], last, far), "ctx", 2)
    return here[0].astype(F32) + own.astype(F32) + near.astype(F32) + far.astype(F32)


def on_device(
    queries, keys, values, out_weight, resid, expert_ids, router_probs, w_gate, w_up, w_down
):
    n_ctx, n_exp, n_tp = (lax.axis_size(a) for a in ("ctx", "exp", "tp"))
    ctx, exp, tp = (lax.axis_index(a) for a in ("ctx", "exp", "tp"))
    place = jnp.stack([ctx, exp, tp]).astype(jnp.int32)
    part, model = resid.shape
    block = expert_ids.shape[0]
    heads_here = queries.shape[1] // HEAD_DIMENSION
    rows_here = w_gate.shape[0]
    experts_here = max(1, rows_here // 2)
    first = (ctx * n_exp + exp) * rows_here // 2
    cap = min(8, block)
    slots = n_ctx * n_exp * cap
    small = (n_ctx, n_exp, n_tp) == (4, 2, 2) and part % 16 == 0 and rows_here % 2 == 0

    shared = (exp * n_tp + tp) * heads_here // (QUERY_HEADS // KEY_VALUE_HEADS)
    key_head = lax.dynamic_slice_in_dim(keys, shared * HEAD_DIMENSION, HEAD_DIMENSION, 1)
    value_head = lax.dynamic_slice_in_dim(values, shared * HEAD_DIMENSION, HEAD_DIMENSION, 1)
    kv = jnp.concatenate([key_head, value_head], axis=1)
    kv_pieces = [kv] + [from_earlier(kv, "ctx", z) for z in range(1, n_ctx)]

    gate_weights = router_probs / jnp.sum(router_probs, axis=1, keepdims=True)
    high = lax.reduce_precision(gate_weights, 8, 7)
    routing = jnp.stack([expert_ids.astype(F32).T, high.T, (gate_weights - high).T]).astype(BF)
    if small:
        routing = routing.reshape(3 * TOPK, block)
        for axis, bit in (("exp", 1), ("ctx", 1), ("ctx", 2)):
            routing = jnp.concatenate([routing, flip(routing, axis, bit)])
        routing = routing.reshape(n_ctx, n_exp, 3, TOPK, n_tp, part)
        routing = jnp.where(tp == 0, routing, routing[:, :, :, :, ::-1])
    else:
        routing = lax.all_gather(routing, ("ctx", "exp"), axis=0)
        routing = routing.reshape(n_ctx, n_exp, 3, TOPK, n_tp, part)
    cells, weight = routing_tables(routing, n_ctx, n_exp, n_tp, first, experts_here, cap)

    projected = attend_project(
        queries, kv_pieces, out_weight, place, n_exp, n_tp, small
    )
    hidden = resid.astype(F32)
    if small:
        mine, other = projected[: n_exp * part], projected[n_exp * part :]
        summed = (mine.astype(F32) + flip(other, "tp", 1).astype(F32)).astype(BF)
        hidden = hidden + summed[:part].astype(F32)
        hidden = hidden + flip(summed[part:], "exp", 1).astype(F32)
    else:
        hidden = hidden + lax.psum_scatter(
            projected, ("exp", "tp"), scatter_dimension=0, tiled=True
        ).astype(F32)
    mean_square = jnp.mean(hidden * hidden, axis=1, keepdims=True)
    normed = (hidden * lax.rsqrt(mean_square + 1e-06)).astype(BF)

    if small:
        far = flip(normed, "ctx", 2)
        across = flip(normed, "exp", 1)
        near = flip(normed, "ctx", 1)
        far_across = flip(far, "exp", 1)
        near_across = flip(near, "exp", 1)
        last = flip(far, "ctx", 1)
        last_across = flip(far_across, "ctx", 1)
        chip = [normed, near, far, last, across, near_across, far_across, last_across]
        pieces = chip + [flip(piece, "tp", 1) for piece in chip]
        sums = run_experts(cells, weight, pieces, w_gate, w_up, w_down, slots)
        return (hidden + sums_back(*sums, part)).astype(BF)
    x = lax.all_gather(normed, ("ctx", "exp", "tp"), axis=0, tiled=True)

    def by_place(table):
        table = table.reshape(experts_here, n_tp, n_exp, n_ctx, part)
        return table.transpose(0, 3, 2, 1, 4).reshape(experts_here, x.shape[0])

    partial = experts_plain(by_place(cells), by_place(weight), x, w_gate, w_up, w_down, slots)
    routed = lax.psum_scatter(partial, ("ctx", "exp", "tp"), scatter_dimension=0, tiled=True)
    return (hidden + routed.astype(F32)).astype(BF)


def solution(mesh):
    in_specs = (
        P(("groups", "ctx"), ("exp", "tp")),
        P(("groups", "ctx"), None),
        P(("groups", "ctx"), None),
        P(("exp", "tp"), None),
        P(("groups", "ctx", "exp", "tp"), None),
        P(("groups", "ctx", "exp"), None),
        P(("groups", "ctx", "exp"), None),
        P(("ctx", "exp"), None, "tp"),
        P(("ctx", "exp"), None, "tp"),
        P(("ctx", "exp"), "tp", None),
    )
    out_specs = P(("groups", "ctx", "exp", "tp"), None)
    return jax.shard_map(
        on_device, mesh=mesh, in_specs=in_specs, out_specs=out_specs, check_vma=False
    )
```

```python
import functools
import math

import jax
import jax.numpy as jnp
from jax import lax
from jax.experimental import pallas as pl
from jax.experimental.pallas import tpu as pltpu
from jax.sharding import PartitionSpec as P

HEAD_DIMENSION = 128
QUERY_HEADS = 32
KEY_VALUE_HEADS = 4
EXPERTS = 64
TOPK = 8
MIB = 1 << 20
LANES = 128
BF = jnp.bfloat16
F32 = jnp.float32


def attend_blocks(blocks, key_head, value_head, heads_here):
    score_scale = 1.0 / math.sqrt(HEAD_DIMENSION)

    def make_state(query_rows):
        row_total = query_rows.shape[0]
        return (
            jnp.full((row_total, heads_here), -1e30, jnp.float32),
            jnp.zeros((row_total, heads_here), jnp.float32),
            jnp.zeros((row_total, heads_here, HEAD_DIMENSION), jnp.float32),
        )

    initial = tuple((make_state(query_rows) for query_rows, query_places in blocks))

    def fold_keys(carry, piece, first):
        key_piece, value_piece = piece
        key_places = jnp.arange(key_piece.shape[0], dtype=jnp.int32)
        updated = []
        for (query_rows, query_places), state in zip(blocks, carry):

            def refresh(state, query_rows=query_rows, query_places=query_places):
                running_max, running_sum, accum = state
                shaped = query_rows.reshape(query_rows.shape[0], heads_here, HEAD_DIMENSION)
                scores = (
                    jnp.einsum("qhd,kd->qhk", shaped, key_piece, preferred_element_type=jnp.float32)
                    * score_scale
                )
                allowed = key_places[None, None, :] <= query_places[:, None, None]
                scores = jnp.where(allowed, scores, -1e30)
                new_max = jnp.maximum(running_max, jnp.max(scores, axis=2))
                weights = jnp.where(allowed, jnp.exp(scores - new_max[:, :, None]), 0.0)
                running_sum = jnp.sum(weights, axis=2)
                accum = jnp.einsum(
                    "qhk,kd->qhd",
                    weights,
                    value_piece.astype(jnp.float32),
                    precision=lax.Precision.HIGHEST,
                )
                return (new_max, running_sum, accum)

            needed = first <= query_places[-1]
            updated.append(lax.cond(needed, refresh, lambda state: state, state))
        return tuple(updated)

    final = fold_keys(
        initial,
        (
            lax.all_gather(key_head, "ctx", axis=0, tiled=True),
            lax.all_gather(value_head, "ctx", axis=0, tiled=True),
        ),
        jnp.int32(0),
    )
    results = []
    for (query_rows, query_places), state in zip(blocks, final):
        running_max, running_sum, accum = state
        results.append(
            (accum / running_sum[:, :, None])
            .reshape(query_rows.shape[0], heads_here * HEAD_DIMENSION)
            .astype(jnp.bfloat16)
        )
    return results


def run_experts(inputs, w_gate, w_up, w_down):
    gate_out = jnp.einsum("rnd,rdf->rnf", inputs, w_gate, preferred_element_type=jnp.float32)
    up_out = jnp.einsum("rnd,rdf->rnf", inputs, w_up, preferred_element_type=jnp.float32)
    activated = (jax.nn.silu(gate_out) * up_out).astype(jnp.bfloat16)
    return jnp.einsum("rnf,rfd->rnd", activated, w_down, preferred_element_type=jnp.float32).astype(
        jnp.bfloat16
    )


def on_device_any_size(
    queries, keys, values, out_weight, resid, expert_ids, router_probs, w_gate, w_up, w_down
):
    rows_ctx = queries.shape[0]
    heads_here = queries.shape[1] // HEAD_DIMENSION
    group_width = QUERY_HEADS // KEY_VALUE_HEADS
    head_rank = lax.axis_index(("exp", "tp"))
    shared = head_rank * heads_here // group_width
    key_head = lax.dynamic_slice_in_dim(keys, shared * HEAD_DIMENSION, HEAD_DIMENSION, 1)
    value_head = lax.dynamic_slice_in_dim(values, shared * HEAD_DIMENSION, HEAD_DIMENSION, 1)
    cycle_rank = lax.axis_index("ctx")
    own_places = cycle_rank * rows_ctx + jnp.arange(rows_ctx, dtype=jnp.int32)
    attended = attend_blocks([(queries, own_places)], key_head, value_head, heads_here)[0]
    projected = lax.psum_scatter(
        jnp.dot(attended, out_weight, preferred_element_type=jnp.float32).astype(jnp.bfloat16),
        ("exp", "tp"),
        scatter_dimension=0,
        tiled=True,
    ).astype(jnp.float32)
    hidden = resid.astype(jnp.float32) + projected
    mean_square = jnp.mean(hidden * hidden, axis=1, keepdims=True)
    normed = (hidden * lax.rsqrt(mean_square + 1e-06)).astype(jnp.bfloat16)
    pair_rows = lax.all_gather(normed, "tp", axis=0, tiled=True)
    slot_count = min(8, expert_ids.shape[0])
    gate_weights = router_probs / jnp.sum(router_probs, axis=1, keepdims=True)
    flat_ids = expert_ids.reshape(-1)
    assigned = flat_ids.shape[0]
    onehot = (flat_ids[:, None] == jnp.arange(EXPERTS, dtype=jnp.int32)[None, :]).astype(jnp.int32)
    slots = jnp.sum(onehot * (jnp.cumsum(onehot, axis=0) - 1), axis=1)
    token_of = jnp.arange(assigned, dtype=jnp.int32) // TOPK
    peer_count = lax.axis_size(("ctx", "exp"))
    rows_here = w_gate.shape[0]
    cell_parts = []
    for half_index in range(2):
        half_rows_id = 2 * flat_ids + half_index
        target = half_rows_id // rows_here
        local_row = half_rows_id % rows_here
        cell_parts.append((local_row * slot_count + slots) * peer_count + target)
    cells = jnp.concatenate(cell_parts)
    table = (
        jnp.full((rows_here * slot_count * peer_count,), -1, jnp.int32)
        .at[cells]
        .set(jnp.concatenate([token_of, token_of]))
    )
    send_buffer = jnp.where(
        table[:, None] >= 0, pair_rows[jnp.maximum(table, 0)], jnp.zeros((), jnp.bfloat16)
    )
    model_width = pair_rows.shape[1]
    received = lax.all_to_all(
        send_buffer.reshape(rows_here * slot_count, peer_count, model_width),
        ("ctx", "exp"),
        split_axis=1,
        concat_axis=1,
        tiled=True,
    )
    expert_out = run_experts(
        received.reshape(rows_here, slot_count * peer_count, model_width), w_gate, w_up, w_down
    )
    returned = lax.all_to_all(
        expert_out.reshape(rows_here * slot_count, peer_count, model_width),
        ("ctx", "exp"),
        split_axis=1,
        concat_axis=1,
        tiled=True,
    )
    returned_flat = returned.reshape(rows_here * slot_count * peer_count, model_width)
    gathered = returned_flat[cells].reshape(2, expert_ids.shape[0], TOPK, model_width)
    routed_part = jnp.einsum(
        "hakd,ak->ad", gathered.astype(jnp.float32), gate_weights, precision=lax.Precision.HIGHEST
    )
    routed = lax.psum_scatter(
        routed_part.astype(jnp.bfloat16), "tp", scatter_dimension=0, tiled=True
    ).astype(jnp.float32)
    return (hidden + routed).astype(jnp.bfloat16)


def flip(x, axis, bit):
    return lax.ppermute(x, axis, [(i, i ^ bit) for i in range(lax.axis_size(axis))])


def from_earlier(x, axis, steps):
    size = lax.axis_size(axis)
    return lax.ppermute(x, axis, [(i, i + steps) for i in range(size - steps)])


def in_hbm(x):
    return pltpu.with_memory_space_constraint(x, pltpu.HBM)


def dot_rows(a, b):
    return lax.dot_general(a, b, (((1,), (1,)), ((), ())), preferred_element_type=F32)


def attention_kernel(sizes, place, *refs):
    n_ctx, n_exp, n_tp, heads, part = sizes
    rows = n_exp * n_tp * part
    kv_refs, refs = refs[:n_ctx], refs[n_ctx:]
    ids_ref, probs_ref, resid_hbm, q_hbm, w_hbm = refs[:5]
    base_ref, across_ref, other_ref, routing_ref = refs[5:9]
    k_all, v_all, q_all, att, att_rel, w_all, resid, packed, q_sem, sems = refs[9:]
    fetch_q = []
    for h in range(heads):
        columns = slice(h * HEAD_DIMENSION, (h + 1) * HEAD_DIMENSION)
        fetch_q.append(
            pltpu.make_async_copy(q_hbm.at[:, columns], q_all.at[:, columns], q_sem.at[h])
        )
        fetch_q[h].start()
    fetch_w = pltpu.make_async_copy(w_hbm, w_all, sems.at[0])
    fetch_w.start()
    fetch_resid = pltpu.make_async_copy(resid_hbm, resid, sems.at[1])
    fetch_resid.start()
    ctx, exp, tp = place[0], place[1], place[2]

    block = n_tp * part
    ids = ids_ref[...]
    probs = probs_ref[...]
    expert = lax.broadcasted_iota(jnp.int32, (EXPERTS, block), 0)
    named = jnp.zeros((EXPERTS, block), F32)
    for k in range(TOPK):
        named = named + jnp.where(expert == ids[k : k + 1, :], 1.0, 0.0)
    before = lax.broadcasted_iota(jnp.int32, (block, block), 0) < lax.broadcasted_iota(
        jnp.int32, (block, block), 1
    )
    count = jnp.dot(
        named.astype(BF), jnp.where(before, 1.0, 0.0).astype(BF), preferred_element_type=F32
    )
    ranks = [
        jnp.sum(jnp.where(expert == ids[k : k + 1, :], count, 0.0), axis=0, keepdims=True)
        for k in range(TOPK)
    ]
    gates = probs / jnp.sum(probs, axis=0, keepdims=True)
    high = gates.astype(BF).astype(F32)
    fields = jnp.concatenate([ids.astype(F32)] + ranks + [high, gates - high], axis=0)
    packed[...] = jnp.zeros_like(packed)
    packed[: 4 * TOPK, :block] = fields
    packed[...] = packed[...].T
    routing_ref[...] = packed[pl.ds(pl.multiple_of(tp * part, part), part), :].astype(BF)

    for z in range(n_ctx):
        k_all[z * rows : (z + 1) * rows, :] = kv_refs[z][:, :HEAD_DIMENSION]
        v_all[z * rows : (z + 1) * rows, :HEAD_DIMENSION] = kv_refs[z][:, HEAD_DIMENSION:]
    v_all[:, HEAD_DIMENSION:] = jnp.ones((n_ctx * rows, HEAD_DIMENSION), BF)
    column = lax.broadcasted_iota(jnp.int32, (rows, n_ctx * rows), 1)
    row = lax.broadcasted_iota(jnp.int32, (rows, n_ctx * rows), 0)
    allowed = (column <= row) | ((column >= rows) & (column < (ctx + 1) * rows))
    scale = 1.0 / math.sqrt(HEAD_DIMENSION)
    for h in range(heads):
        columns = slice(h * HEAD_DIMENSION, (h + 1) * HEAD_DIMENSION)
        fetch_q[h].wait()
        s = dot_rows(q_all[:, columns], k_all[...])
        s = jnp.where(allowed, s * scale, -1e30)
        weights = jnp.exp(s - jnp.max(s, axis=1, keepdims=True))
        out = jnp.dot(weights.astype(BF), v_all[...], preferred_element_type=F32)
        att[:, columns] = (out[:, :HEAD_DIMENSION] / out[:, HEAD_DIMENSION:]).astype(BF)
    for t in range(n_tp):
        for x in range(n_exp):
            owner = lax.rem(exp + x, n_exp) * n_tp + lax.rem(tp + t, n_tp)
            source = pl.ds(pl.multiple_of(owner * part, part), part)
            at = (t * n_exp + x) * part
            att_rel[at : at + part, :] = att[source, :]
    fetch_w.wait()
    projected = jnp.dot(att_rel[...], w_all[...], preferred_element_type=F32)
    fetch_resid.wait()
    base_ref[...] = resid[...].astype(F32) + projected[:part]
    across_ref[...] = projected[part : 2 * part].astype(BF)
    other_ref[...] = projected[2 * part :].astype(BF)


def attend_project(place, pieces, expert_ids, router_probs, resid, queries, out_weight, n_exp, n_tp):
    rows, width = queries.shape
    n_ctx, heads = len(pieces), width // HEAD_DIMENSION
    part, model = resid.shape
    block = expert_ids.shape[0]
    vmem = pl.BlockSpec(memory_space=pltpu.VMEM)
    hbm = pl.BlockSpec(memory_space=pltpu.HBM)
    return pl.pallas_call(
        functools.partial(attention_kernel, (n_ctx, n_exp, n_tp, heads, part)),
        out_shape=(
            jax.ShapeDtypeStruct((part, model), F32),
            jax.ShapeDtypeStruct((part, model), BF),
            jax.ShapeDtypeStruct((2 * part, model), BF),
            jax.ShapeDtypeStruct((part, LANES), BF),
        ),
        in_specs=[pl.BlockSpec(memory_space=pltpu.SMEM)] + [vmem] * (n_ctx + 2) + [hbm] * 3,
        out_specs=(vmem,) * 4,
        scratch_shapes=[
            pltpu.VMEM((n_ctx * rows, HEAD_DIMENSION), BF),
            pltpu.VMEM((n_ctx * rows, 2 * HEAD_DIMENSION), BF),
            pltpu.VMEM((rows, width), BF),
            pltpu.VMEM((rows, width), BF),
            pltpu.VMEM((rows, width), BF),
            pltpu.VMEM((width, model), BF),
            pltpu.VMEM((part, model), BF),
            pltpu.VMEM((LANES, LANES), F32),
            pltpu.SemaphoreType.DMA((heads,)),
            pltpu.SemaphoreType.DMA((2,)),
        ],
        compiler_params=pltpu.CompilerParams(vmem_limit_bytes=32 * MIB),
        cost_estimate=pl.CostEstimate(
            flops=2 * rows * width * (2 * n_ctx * rows + model),
            bytes_accessed=2 * (rows * width + width * model + rows * model),
            transcendentals=rows * n_ctx * rows * heads,
        ),
        name="attend_project",
    )(place, *pieces, expert_ids.T, router_probs.T, *map(in_hbm, (resid, queries, out_weight)))


def expert_kernel(n_pieces, depth, experts, first_ref, *refs):
    pieces, (wg_hbm, wu_hbm, wd_hbm) = refs[:n_pieces], refs[n_pieces : n_pieces + 3]
    outs = refs[n_pieces + 3 : n_pieces + 7]
    x_all, packed, pick_all, scale_all, out_all, wgu, wd, act, sems = refs[n_pieces + 7 :]
    tokens = x_all.shape[0]
    slots = pick_all.shape[0] // experts
    _, _, halves, hidden, model = wgu.shape
    part = tokens // n_pieces
    blocks = n_pieces // 2

    def copies(e):
        slot = lax.rem(e, depth)
        rows = pl.ds(e * halves, halves)
        return (
            pltpu.make_async_copy(wg_hbm.at[rows], wgu.at[slot, 0], sems.at[0, slot]),
            pltpu.make_async_copy(wu_hbm.at[rows], wgu.at[slot, 1], sems.at[1, slot]),
            pltpu.make_async_copy(wd_hbm.at[rows], wd.at[slot], sems.at[2, slot]),
        )

    def start(e):
        for copy in copies(e):
            copy.start()

    def wait(e):
        for copy in copies(e):
            copy.wait()

    def gate_up(e):
        x = out_all[pl.ds(pl.multiple_of(e * slots, slots), slots), :]
        weight = wgu[lax.rem(e, depth)].reshape(2 * halves * hidden, model)
        both = dot_rows(weight, x)
        gate, up = both[: halves * hidden], both[halves * hidden :]
        return (gate * jax.nn.sigmoid(gate) * up).astype(BF)

    def down(e):
        here = pl.ds(pl.multiple_of(e * slots, slots), slots)
        weight = wd[lax.rem(e, depth)].reshape(halves * hidden, model)
        out = lax.dot_general(
            act[lax.rem(e, 2)], weight, (((0,), (0,)), ((), ())), preferred_element_type=F32
        )
        return here, (out * scale_all[here, :]).astype(BF)

    for e in range(min(depth - 1, experts)):
        start(e)
    for i, piece in enumerate(pieces):
        x_all[i * part : (i + 1) * part, :] = piece[:, :model]
        packed[i * part : (i + 1) * part, :] = piece[:, model:].astype(F32)
    fields = packed[...].T
    ids, ranks = fields[:TOPK], fields[TOPK : 2 * TOPK]
    gates = fields[2 * TOPK : 3 * TOPK] + fields[3 * TOPK : 4 * TOPK]
    token = lax.broadcasted_iota(jnp.int32, (TOPK, tokens), 1)
    places = ranks.astype(jnp.int32) + lax.rem(token // part, blocks) * (slots // blocks)
    slot = lax.broadcasted_iota(jnp.int32, (slots, tokens), 0)
    for e in range(experts):
        hit = ids.astype(jnp.int32) == first_ref[0] + e
        chosen = slot == jnp.max(jnp.where(hit, places, -1), axis=0, keepdims=True)
        gate = jnp.sum(jnp.where(hit, gates, 0.0), axis=0, keepdims=True)
        here = slice(e * slots, (e + 1) * slots)
        pick_all[here, :] = jnp.where(chosen, 1.0, 0.0).astype(BF)
        scale_all[here, :] = jnp.sum(jnp.where(chosen, gate, 0.0), axis=1, keepdims=True)
    out_all[...] = jnp.dot(pick_all[...], x_all[...], preferred_element_type=F32).astype(BF)
    wait(0)
    act[0] = gate_up(0)

    @pl.loop(0, experts - 1)
    def _(e):
        @pl.when(e + depth - 1 < experts)
        def _():
            start(e + depth - 1)

        wait(e + 1)
        following = gate_up(e + 1)
        here, out = down(e)
        act[lax.rem(e + 1, 2)] = following
        out_all[here, :] = out

    here, out = down(experts - 1)
    out_all[here, :] = out
    quarter = tokens // 4
    for i, o_ref in enumerate(outs):
        o_ref[...] = lax.dot_general(
            pick_all[:, i * quarter : (i + 1) * quarter],
            out_all[...],
            (((0,), (0,)), ((), ())),
            preferred_element_type=F32,
        ).astype(BF)


def cube_experts(first, pieces, w_gate, w_up, w_down, slots):
    rows, hidden, model = w_down.shape
    halves = 2
    experts = rows // halves
    tokens = len(pieces) * pieces[0].shape[0]
    depth = min(4, experts)
    vmem = pl.BlockSpec(memory_space=pltpu.VMEM)
    hbm = pl.BlockSpec(memory_space=pltpu.HBM)

    out = jax.ShapeDtypeStruct((tokens // 4, model), BF)
    return pl.pallas_call(
        functools.partial(expert_kernel, len(pieces), depth, experts),
        out_shape=(out,) * 4,
        in_specs=[pl.BlockSpec(memory_space=pltpu.SMEM)] + [vmem] * len(pieces) + [hbm] * 3,
        out_specs=(vmem,) * 4,
        scratch_shapes=[
            pltpu.VMEM((tokens, model), BF),
            pltpu.VMEM((tokens, LANES), F32),
            pltpu.VMEM((experts * slots, tokens), BF),
            pltpu.VMEM((experts * slots, 1), F32),
            pltpu.VMEM((experts * slots, model), BF),
            pltpu.VMEM((depth, 2, halves, hidden, model), BF),
            pltpu.VMEM((depth, halves, hidden, model), BF),
            pltpu.VMEM((2, halves * hidden, slots), BF),
            pltpu.SemaphoreType.DMA((3, depth)),
        ],
        compiler_params=pltpu.CompilerParams(vmem_limit_bytes=44 * MIB),
        cost_estimate=pl.CostEstimate(
            flops=2 * experts * slots * model * (3 * halves * hidden + 2 * tokens),
            bytes_accessed=6 * rows * model * hidden + 4 * tokens * model,
            transcendentals=experts * slots * halves * hidden,
        ),
        name="experts",
    )(
        first,
        *pieces,
        in_hbm(jnp.swapaxes(w_gate, 1, 2)),
        in_hbm(jnp.swapaxes(w_up, 1, 2)),
        in_hbm(w_down),
    )


def sums_back(mine, mine_across, other, other_across, part):
    def add(a, *others):
        total = a.astype(F32)
        for b in others:
            total = total + b.astype(F32)
        return total.astype(BF)

    across = add(mine_across, flip(other_across, "tp", 1))
    here = add(mine, flip(other, "tp", 1))
    across = [across[z * part : (z + 1) * part] for z in range(4)]
    here = [here[z * part : (z + 1) * part] for z in range(4)]
    far_across = add(across[2], flip(across[3], "ctx", 1))
    own = flip(across[0], "exp", 1)
    near = flip(across[1], "exp", 1)
    last = flip(here[3], "ctx", 1)
    far_across, here[1] = lax.optimization_barrier((far_across, here[1]))
    far = flip(far_across, "exp", 1)
    near = add(here[1], near)
    near, here[2] = lax.optimization_barrier((near, here[2]))
    near = flip(near, "ctx", 1)
    far = flip(add(here[2], last, far), "ctx", 2)
    return here[0].astype(F32) + own.astype(F32) + near.astype(F32) + far.astype(F32)


def on_device(
    queries, keys, values, out_weight, resid, expert_ids, router_probs, w_gate, w_up, w_down
):
    n_ctx, n_exp, n_tp = (lax.axis_size(a) for a in ("ctx", "exp", "tp"))
    part = resid.shape[0]
    rows_here = w_gate.shape[0]
    block = expert_ids.shape[0]
    cube = (n_ctx, n_exp, n_tp) == (4, 2, 2) and block == n_tp * part <= LANES
    if not cube or part % 16 or rows_here * n_ctx * n_exp != 2 * EXPERTS:
        return on_device_any_size(
            queries, keys, values, out_weight, resid, expert_ids, router_probs, w_gate, w_up, w_down
        )
    ctx, exp, tp = (lax.axis_index(a) for a in ("ctx", "exp", "tp"))
    place = jnp.stack([ctx, exp, tp]).astype(jnp.int32)
    heads_here = queries.shape[1] // HEAD_DIMENSION
    first = (ctx * n_exp + exp) * rows_here // 2
    slots = n_ctx * n_exp * min(8, block)

    shared = (exp * n_tp + tp) * heads_here // (QUERY_HEADS // KEY_VALUE_HEADS)
    key_head = lax.dynamic_slice_in_dim(keys, shared * HEAD_DIMENSION, HEAD_DIMENSION, 1)
    value_head = lax.dynamic_slice_in_dim(values, shared * HEAD_DIMENSION, HEAD_DIMENSION, 1)
    kv = jnp.concatenate([key_head, value_head], axis=1)
    kv_pieces = [kv] + [from_earlier(kv, "ctx", z) for z in range(1, n_ctx)]
    base, across, other, routing = attend_project(
        place, kv_pieces, expert_ids, router_probs, resid, queries, out_weight, n_exp, n_tp
    )

    other = flip(other, "tp", 1).astype(F32)
    across = flip((across.astype(F32) + other[part:]).astype(BF), "exp", 1)
    hidden = base + other[:part] + across.astype(F32)
    mean_square = jnp.mean(hidden * hidden, axis=1, keepdims=True)
    normed = (hidden * lax.rsqrt(mean_square + 1e-06)).astype(BF)
    normed = jnp.concatenate([normed, routing], axis=1)

    far = flip(normed, "ctx", 2)
    across = flip(normed, "exp", 1)
    near = flip(normed, "ctx", 1)
    far_across = flip(far, "exp", 1)
    near_across = flip(near, "exp", 1)
    last = flip(far, "ctx", 1)
    last_across = flip(far_across, "ctx", 1)
    chip = [normed, near, far, last, across, near_across, far_across, last_across]
    pieces = chip + [flip(piece, "tp", 1) for piece in chip]
    sums = cube_experts(
        first.astype(jnp.int32).reshape(1), pieces, w_gate, w_up, w_down, slots
    )
    return (hidden + sums_back(*sums, part)).astype(BF)


def solution(mesh):
    in_specs = (
        P(("groups", "ctx"), ("exp", "tp")),
        P(("groups", "ctx"), None),
        P(("groups", "ctx"), None),
        P(("exp", "tp"), None),
        P(("groups", "ctx", "exp", "tp"), None),
        P(("groups", "ctx", "exp"), None),
        P(("groups", "ctx", "exp"), None),
        P(("ctx", "exp"), None, "tp"),
        P(("ctx", "exp"), None, "tp"),
        P(("ctx", "exp"), "tp", None),
    )
    out_specs = P(("groups", "ctx", "exp", "tp"), None)
    return jax.shard_map(
        on_device, mesh=mesh, in_specs=in_specs, out_specs=out_specs, check_vma=False
    )
```

```python
import functools
import math

import jax
import jax.numpy as jnp
from jax import lax
from jax.experimental import pallas as pl
from jax.experimental.pallas import tpu as pltpu
from jax.sharding import PartitionSpec as P

HEAD_DIMENSION = 128
QUERY_HEADS = 32
KEY_VALUE_HEADS = 4
EXPERTS = 64
TOPK = 8
MIB = 1 << 20
LANES = 128
BF = jnp.bfloat16
F32 = jnp.float32


def attend_blocks(blocks, key_head, value_head, heads_here):
    score_scale = 1.0 / math.sqrt(HEAD_DIMENSION)

    def make_state(query_rows):
        row_total = query_rows.shape[0]
        return (
            jnp.full((row_total, heads_here), -1e30, jnp.float32),
            jnp.zeros((row_total, heads_here), jnp.float32),
            jnp.zeros((row_total, heads_here, HEAD_DIMENSION), jnp.float32),
        )

    initial = tuple((make_state(query_rows) for query_rows, query_places in blocks))

    def fold_keys(carry, piece, first):
        key_piece, value_piece = piece
        key_places = jnp.arange(key_piece.shape[0], dtype=jnp.int32)
        updated = []
        for (query_rows, query_places), state in zip(blocks, carry):

            def refresh(state, query_rows=query_rows, query_places=query_places):
                running_max, running_sum, accum = state
                shaped = query_rows.reshape(query_rows.shape[0], heads_here, HEAD_DIMENSION)
                scores = (
                    jnp.einsum("qhd,kd->qhk", shaped, key_piece, preferred_element_type=jnp.float32)
                    * score_scale
                )
                allowed = key_places[None, None, :] <= query_places[:, None, None]
                scores = jnp.where(allowed, scores, -1e30)
                new_max = jnp.maximum(running_max, jnp.max(scores, axis=2))
                weights = jnp.where(allowed, jnp.exp(scores - new_max[:, :, None]), 0.0)
                running_sum = jnp.sum(weights, axis=2)
                accum = jnp.einsum(
                    "qhk,kd->qhd",
                    weights,
                    value_piece.astype(jnp.float32),
                    precision=lax.Precision.HIGHEST,
                )
                return (new_max, running_sum, accum)

            needed = first <= query_places[-1]
            updated.append(lax.cond(needed, refresh, lambda state: state, state))
        return tuple(updated)

    final = fold_keys(
        initial,
        (
            lax.all_gather(key_head, "ctx", axis=0, tiled=True),
            lax.all_gather(value_head, "ctx", axis=0, tiled=True),
        ),
        jnp.int32(0),
    )
    results = []
    for (query_rows, query_places), state in zip(blocks, final):
        running_max, running_sum, accum = state
        results.append(
            (accum / running_sum[:, :, None])
            .reshape(query_rows.shape[0], heads_here * HEAD_DIMENSION)
            .astype(jnp.bfloat16)
        )
    return results


def run_experts(inputs, w_gate, w_up, w_down):
    gate_out = jnp.einsum("rnd,rdf->rnf", inputs, w_gate, preferred_element_type=jnp.float32)
    up_out = jnp.einsum("rnd,rdf->rnf", inputs, w_up, preferred_element_type=jnp.float32)
    activated = (jax.nn.silu(gate_out) * up_out).astype(jnp.bfloat16)
    return jnp.einsum("rnf,rfd->rnd", activated, w_down, preferred_element_type=jnp.float32).astype(
        jnp.bfloat16
    )


def on_device_any_size(
    queries, keys, values, out_weight, resid, expert_ids, router_probs, w_gate, w_up, w_down
):
    rows_ctx = queries.shape[0]
    heads_here = queries.shape[1] // HEAD_DIMENSION
    group_width = QUERY_HEADS // KEY_VALUE_HEADS
    head_rank = lax.axis_index(("exp", "tp"))
    shared = head_rank * heads_here // group_width
    key_head = lax.dynamic_slice_in_dim(keys, shared * HEAD_DIMENSION, HEAD_DIMENSION, 1)
    value_head = lax.dynamic_slice_in_dim(values, shared * HEAD_DIMENSION, HEAD_DIMENSION, 1)
    cycle_rank = lax.axis_index("ctx")
    own_places = cycle_rank * rows_ctx + jnp.arange(rows_ctx, dtype=jnp.int32)
    attended = attend_blocks([(queries, own_places)], key_head, value_head, heads_here)[0]
    projected = lax.psum_scatter(
        jnp.dot(attended, out_weight, preferred_element_type=jnp.float32).astype(jnp.bfloat16),
        ("exp", "tp"),
        scatter_dimension=0,
        tiled=True,
    ).astype(jnp.float32)
    hidden = resid.astype(jnp.float32) + projected
    mean_square = jnp.mean(hidden * hidden, axis=1, keepdims=True)
    normed = (hidden * lax.rsqrt(mean_square + 1e-06)).astype(jnp.bfloat16)
    pair_rows = lax.all_gather(normed, "tp", axis=0, tiled=True)
    slot_count = min(8, expert_ids.shape[0])
    gate_weights = router_probs / jnp.sum(router_probs, axis=1, keepdims=True)
    flat_ids = expert_ids.reshape(-1)
    assigned = flat_ids.shape[0]
    onehot = (flat_ids[:, None] == jnp.arange(EXPERTS, dtype=jnp.int32)[None, :]).astype(jnp.int32)
    slots = jnp.sum(onehot * (jnp.cumsum(onehot, axis=0) - 1), axis=1)
    token_of = jnp.arange(assigned, dtype=jnp.int32) // TOPK
    peer_count = lax.axis_size(("ctx", "exp"))
    rows_here = w_gate.shape[0]
    cell_parts = []
    for half_index in range(2):
        half_rows_id = 2 * flat_ids + half_index
        target = half_rows_id // rows_here
        local_row = half_rows_id % rows_here
        cell_parts.append((local_row * slot_count + slots) * peer_count + target)
    cells = jnp.concatenate(cell_parts)
    table = (
        jnp.full((rows_here * slot_count * peer_count,), -1, jnp.int32)
        .at[cells]
        .set(jnp.concatenate([token_of, token_of]))
    )
    send_buffer = jnp.where(
        table[:, None] >= 0, pair_rows[jnp.maximum(table, 0)], jnp.zeros((), jnp.bfloat16)
    )
    model_width = pair_rows.shape[1]
    received = lax.all_to_all(
        send_buffer.reshape(rows_here * slot_count, peer_count, model_width),
        ("ctx", "exp"),
        split_axis=1,
        concat_axis=1,
        tiled=True,
    )
    expert_out = run_experts(
        received.reshape(rows_here, slot_count * peer_count, model_width), w_gate, w_up, w_down
    )
    returned = lax.all_to_all(
        expert_out.reshape(rows_here * slot_count, peer_count, model_width),
        ("ctx", "exp"),
        split_axis=1,
        concat_axis=1,
        tiled=True,
    )
    returned_flat = returned.reshape(rows_here * slot_count * peer_count, model_width)
    gathered = returned_flat[cells].reshape(2, expert_ids.shape[0], TOPK, model_width)
    routed_part = jnp.einsum(
        "hakd,ak->ad", gathered.astype(jnp.float32), gate_weights, precision=lax.Precision.HIGHEST
    )
    routed = lax.psum_scatter(
        routed_part.astype(jnp.bfloat16), "tp", scatter_dimension=0, tiled=True
    ).astype(jnp.float32)
    return (hidden + routed).astype(jnp.bfloat16)


def flip(x, axis, bit):
    return lax.ppermute(x, axis, [(i, i ^ bit) for i in range(lax.axis_size(axis))])


def from_earlier(x, axis, steps):
    size = lax.axis_size(axis)
    return lax.ppermute(x, axis, [(i, i + steps) for i in range(size - steps)])


def in_hbm(x):
    return pltpu.with_memory_space_constraint(x, pltpu.HBM)


def dot_rows(a, b):
    return lax.dot_general(a, b, (((1,), (1,)), ((), ())), preferred_element_type=F32)


def own_block_kernel(sizes, place, kv_ref, ids_hbm, probs_hbm, q_hbm, w_hbm, resid_hbm, *refs):
    n_exp, n_tp, heads, part = sizes
    rows = n_exp * n_tp * part
    q_ref, w_ref, resid_ref, out_ref, sum_ref, max_ref, routing_ref = refs[:7]
    v_ext, ids_ref, probs_ref, packed, q_sem, sems = refs[7:]
    fetch = [
        pltpu.make_async_copy(ids_hbm, ids_ref, sems.at[0]),
        pltpu.make_async_copy(probs_hbm, probs_ref, sems.at[1]),
        pltpu.make_async_copy(resid_hbm, resid_ref, sems.at[2]),
        pltpu.make_async_copy(w_hbm, w_ref, sems.at[3]),
    ]
    fetch_q = pltpu.make_async_copy(q_hbm, q_ref, q_sem)
    fetch_q.start()
    for copy in fetch:
        copy.start()
    tp = place[2]
    v_ext[:, :HEAD_DIMENSION] = kv_ref[:, HEAD_DIMENSION:]
    v_ext[:, HEAD_DIMENSION:] = jnp.ones((rows, HEAD_DIMENSION), BF)
    keys = kv_ref[:, :HEAD_DIMENSION]
    allowed = lax.broadcasted_iota(jnp.int32, (rows, rows), 1) <= lax.broadcasted_iota(
        jnp.int32, (rows, rows), 0
    )
    scale = 1.0 / math.sqrt(HEAD_DIMENSION)
    fetch_q.wait()
    for h in range(heads):
        columns = slice(h * HEAD_DIMENSION, (h + 1) * HEAD_DIMENSION)
        s = jnp.where(allowed, dot_rows(q_ref[:, columns], keys) * scale, -1e30)
        top = jnp.max(s, axis=1, keepdims=True)
        out = jnp.dot(jnp.exp(s - top).astype(BF), v_ext[...], preferred_element_type=F32)
        out_ref[:, columns] = out[:, :HEAD_DIMENSION]
        sum_ref[:, columns] = out[:, HEAD_DIMENSION:]
        max_ref[:, h : h + 1] = top

    fetch[0].wait()
    fetch[1].wait()
    block = n_tp * part
    ids = ids_ref[...]
    probs = probs_ref[...]
    expert = lax.broadcasted_iota(jnp.int32, (EXPERTS, block), 0)
    named = jnp.zeros((EXPERTS, block), F32)
    for k in range(TOPK):
        named = named + jnp.where(expert == ids[k : k + 1, :], 1.0, 0.0)
    before = lax.broadcasted_iota(jnp.int32, (block, block), 0) < lax.broadcasted_iota(
        jnp.int32, (block, block), 1
    )
    count = jnp.dot(
        named.astype(BF), jnp.where(before, 1.0, 0.0).astype(BF), preferred_element_type=F32
    )
    ranks = [
        jnp.sum(jnp.where(expert == ids[k : k + 1, :], count, 0.0), axis=0, keepdims=True)
        for k in range(TOPK)
    ]
    gates = probs / jnp.sum(probs, axis=0, keepdims=True)
    high = gates.astype(BF).astype(F32)
    fields = jnp.concatenate([ids.astype(F32)] + ranks + [high, gates - high], axis=0)
    packed[...] = jnp.zeros_like(packed)
    packed[: 4 * TOPK, :block] = fields
    packed[...] = packed[...].T
    routing_ref[...] = packed[pl.ds(pl.multiple_of(tp * part, part), part), :].astype(BF)
    fetch[2].wait()
    fetch[3].wait()


def own_block(place, kv, expert_ids, router_probs, queries, out_weight, resid, n_exp, n_tp):
    rows, width = queries.shape
    heads = width // HEAD_DIMENSION
    part, model = resid.shape
    block = expert_ids.shape[0]
    vmem = pl.BlockSpec(memory_space=pltpu.VMEM)
    hbm = pl.BlockSpec(memory_space=pltpu.HBM)
    return pl.pallas_call(
        functools.partial(own_block_kernel, (n_exp, n_tp, heads, part)),
        out_shape=(
            jax.ShapeDtypeStruct((rows, width), BF),
            jax.ShapeDtypeStruct((width, model), BF),
            jax.ShapeDtypeStruct((part, model), BF),
            jax.ShapeDtypeStruct((rows, width), F32),
            jax.ShapeDtypeStruct((rows, width), F32),
            jax.ShapeDtypeStruct((rows, LANES), F32),
            jax.ShapeDtypeStruct((part, LANES), BF),
        ),
        in_specs=[pl.BlockSpec(memory_space=pltpu.SMEM), vmem] + [hbm] * 5,
        out_specs=(vmem,) * 7,
        scratch_shapes=[
            pltpu.VMEM((rows, 2 * HEAD_DIMENSION), BF),
            pltpu.VMEM((TOPK, block), jnp.int32),
            pltpu.VMEM((TOPK, block), F32),
            pltpu.VMEM((LANES, LANES), F32),
            pltpu.SemaphoreType.DMA,
            pltpu.SemaphoreType.DMA((4,)),
        ],
        compiler_params=pltpu.CompilerParams(vmem_limit_bytes=20 * MIB),
        cost_estimate=pl.CostEstimate(
            flops=6 * rows * width * rows,
            bytes_accessed=2 * (rows * width + width * model + rows * model),
            transcendentals=rows * rows * heads,
        ),
        name="own_block",
    )(place, kv, *map(in_hbm, (expert_ids.T, router_probs.T, queries, out_weight, resid)))


def attention_kernel(sizes, place, *refs):
    n_ctx, n_exp, n_tp, heads, part = sizes
    rows = n_exp * n_tp * part
    kv_refs, refs = refs[: n_ctx - 1], refs[n_ctx - 1 :]
    q_ref, w_ref, resid_ref, out_ref, sum_ref, max_ref = refs[:6]
    base_ref, across_ref, other_ref = refs[6:9]
    k_all, v_all, att, att_rel = refs[9:]
    ctx, exp, tp = place[0], place[1], place[2]
    for z in range(n_ctx - 1):
        k_all[z * rows : (z + 1) * rows, :] = kv_refs[z][:, :HEAD_DIMENSION]
        v_all[z * rows : (z + 1) * rows, :HEAD_DIMENSION] = kv_refs[z][:, HEAD_DIMENSION:]
    v_all[:, HEAD_DIMENSION:] = jnp.ones(((n_ctx - 1) * rows, HEAD_DIMENSION), BF)
    allowed = lax.broadcasted_iota(jnp.int32, (1, (n_ctx - 1) * rows), 1) < ctx * rows
    scale = 1.0 / math.sqrt(HEAD_DIMENSION)
    for h in range(heads):
        columns = slice(h * HEAD_DIMENSION, (h + 1) * HEAD_DIMENSION)
        s = jnp.where(allowed, dot_rows(q_ref[:, columns], k_all[...]) * scale, -1e30)
        own_top = max_ref[:, h : h + 1]
        top = jnp.maximum(own_top, jnp.max(s, axis=1, keepdims=True))
        keep = jnp.exp(own_top - top)
        out = jnp.dot(jnp.exp(s - top).astype(BF), v_all[...], preferred_element_type=F32)
        total = sum_ref[:, columns] * keep + out[:, HEAD_DIMENSION:]
        out = out_ref[:, columns] * keep + out[:, :HEAD_DIMENSION]
        att[:, columns] = (out / total).astype(BF)
    for t in range(n_tp):
        for x in range(n_exp):
            owner = lax.rem(exp + x, n_exp) * n_tp + lax.rem(tp + t, n_tp)
            source = pl.ds(pl.multiple_of(owner * part, part), part)
            at = (t * n_exp + x) * part
            att_rel[at : at + part, :] = att[source, :]
    projected = jnp.dot(att_rel[...], w_ref[...], preferred_element_type=F32)
    base_ref[...] = resid_ref[...].astype(F32) + projected[:part]
    across_ref[...] = projected[part : 2 * part].astype(BF)
    other_ref[...] = projected[2 * part :].astype(BF)


def attend_project(place, pieces, own, n_exp, n_tp):
    queries, out_weight, resid = own[:3]
    rows, width = queries.shape
    n_ctx, heads = len(pieces) + 1, width // HEAD_DIMENSION
    part, model = resid.shape
    vmem = pl.BlockSpec(memory_space=pltpu.VMEM)
    return pl.pallas_call(
        functools.partial(attention_kernel, (n_ctx, n_exp, n_tp, heads, part)),
        out_shape=(
            jax.ShapeDtypeStruct((part, model), F32),
            jax.ShapeDtypeStruct((part, model), BF),
            jax.ShapeDtypeStruct((2 * part, model), BF),
        ),
        in_specs=[pl.BlockSpec(memory_space=pltpu.SMEM)] + [vmem] * (n_ctx - 1 + len(own)),
        out_specs=(vmem,) * 3,
        scratch_shapes=[
            pltpu.VMEM(((n_ctx - 1) * rows, HEAD_DIMENSION), BF),
            pltpu.VMEM(((n_ctx - 1) * rows, 2 * HEAD_DIMENSION), BF),
            pltpu.VMEM((rows, width), BF),
            pltpu.VMEM((rows, width), BF),
        ],
        compiler_params=pltpu.CompilerParams(vmem_limit_bytes=20 * MIB),
        cost_estimate=pl.CostEstimate(
            flops=2 * rows * width * (3 * (n_ctx - 1) * rows + model),
            bytes_accessed=2 * (rows * width + width * model + rows * model),
            transcendentals=rows * n_ctx * rows * heads,
        ),
        name="attend_project",
    )(place, *pieces, *own)


def expert_kernel(n_pieces, order, sizes, depth, experts, first_ref, *refs):
    pieces, (wg_hbm, wu_hbm, wd_hbm) = refs[:n_pieces], refs[n_pieces : n_pieces + 3]
    outs = refs[n_pieces + 3 : n_pieces + 7]
    x_all, packed, pick_all, scale_all, out_all, wgu, wd, act, sems = refs[n_pieces + 7 :]
    tokens = x_all.shape[0]
    slots = pick_all.shape[0] // experts
    _, _, halves, hidden, model = wgu.shape
    part, blocks = sizes

    def copies(e):
        slot = lax.rem(e, depth)
        rows = pl.ds(e * halves, halves)
        return (
            pltpu.make_async_copy(wg_hbm.at[rows], wgu.at[slot, 0], sems.at[0, slot]),
            pltpu.make_async_copy(wu_hbm.at[rows], wgu.at[slot, 1], sems.at[1, slot]),
            pltpu.make_async_copy(wd_hbm.at[rows], wd.at[slot], sems.at[2, slot]),
        )

    def start(e):
        for copy in copies(e):
            copy.start()

    def wait(e):
        for copy in copies(e):
            copy.wait()

    def gate_up(e):
        x = out_all[pl.ds(pl.multiple_of(e * slots, slots), slots), :]
        weight = wgu[lax.rem(e, depth)].reshape(2 * halves * hidden, model)
        both = dot_rows(weight, x)
        gate, up = both[: halves * hidden], both[halves * hidden :]
        return (gate * jax.nn.sigmoid(gate) * up).astype(BF)

    def down(e):
        here = pl.ds(pl.multiple_of(e * slots, slots), slots)
        weight = wd[lax.rem(e, depth)].reshape(halves * hidden, model)
        out = lax.dot_general(
            act[lax.rem(e, 2)], weight, (((0,), (0,)), ((), ())), preferred_element_type=F32
        )
        return here, (out * scale_all[here, :]).astype(BF)

    for e in range(min(depth - 1, experts)):
        start(e)
    for i, (piece, at) in enumerate(order):
        rows = slice(at * part, (at + 1) * part)
        x_all[i * part : (i + 1) * part, :] = pieces[piece][rows, :model]
        packed[i * part : (i + 1) * part, :] = pieces[piece][rows, model:].astype(F32)
    fields = packed[...].T
    ids, ranks = fields[:TOPK], fields[TOPK : 2 * TOPK]
    gates = fields[2 * TOPK : 3 * TOPK] + fields[3 * TOPK : 4 * TOPK]
    token = lax.broadcasted_iota(jnp.int32, (TOPK, tokens), 1)
    places = ranks.astype(jnp.int32) + lax.rem(token // part, blocks) * (slots // blocks)
    slot = lax.broadcasted_iota(jnp.int32, (slots, tokens), 0)
    for e in range(experts):
        hit = ids.astype(jnp.int32) == first_ref[0] + e
        chosen = slot == jnp.max(jnp.where(hit, places, -1), axis=0, keepdims=True)
        gate = jnp.sum(jnp.where(hit, gates, 0.0), axis=0, keepdims=True)
        here = slice(e * slots, (e + 1) * slots)
        pick_all[here, :] = jnp.where(chosen, 1.0, 0.0).astype(BF)
        scale_all[here, :] = jnp.sum(jnp.where(chosen, gate, 0.0), axis=1, keepdims=True)
    out_all[...] = jnp.dot(pick_all[...], x_all[...], preferred_element_type=F32).astype(BF)
    wait(0)
    act[0] = gate_up(0)

    @pl.loop(0, experts - 1)
    def _(e):
        @pl.when(e + depth - 1 < experts)
        def _():
            start(e + depth - 1)

        wait(e + 1)
        following = gate_up(e + 1)
        here, out = down(e)
        act[lax.rem(e + 1, 2)] = following
        out_all[here, :] = out

    here, out = down(experts - 1)
    out_all[here, :] = out
    quarter = tokens // 4
    for i, o_ref in enumerate(outs):
        o_ref[...] = lax.dot_general(
            pick_all[:, i * quarter : (i + 1) * quarter],
            out_all[...],
            (((0,), (0,)), ((), ())),
            preferred_element_type=F32,
        ).astype(BF)


def cube_experts(first, pieces, order, part, w_gate, w_up, w_down, slots):
    rows, hidden, model = w_down.shape
    halves = 2
    experts = rows // halves
    tokens = len(order) * part
    depth = min(4, experts)
    vmem = pl.BlockSpec(memory_space=pltpu.VMEM)
    hbm = pl.BlockSpec(memory_space=pltpu.HBM)

    out = jax.ShapeDtypeStruct((tokens // 4, model), BF)
    return pl.pallas_call(
        functools.partial(
            expert_kernel, len(pieces), order, (part, len(order) // 2), depth, experts
        ),
        out_shape=(out,) * 4,
        in_specs=[pl.BlockSpec(memory_space=pltpu.SMEM)] + [vmem] * len(pieces) + [hbm] * 3,
        out_specs=(vmem,) * 4,
        scratch_shapes=[
            pltpu.VMEM((tokens, model), BF),
            pltpu.VMEM((tokens, LANES), F32),
            pltpu.VMEM((experts * slots, tokens), BF),
            pltpu.VMEM((experts * slots, 1), F32),
            pltpu.VMEM((experts * slots, model), BF),
            pltpu.VMEM((depth, 2, halves, hidden, model), BF),
            pltpu.VMEM((depth, halves, hidden, model), BF),
            pltpu.VMEM((2, halves * hidden, slots), BF),
            pltpu.SemaphoreType.DMA((3, depth)),
        ],
        compiler_params=pltpu.CompilerParams(vmem_limit_bytes=44 * MIB),
        cost_estimate=pl.CostEstimate(
            flops=2 * experts * slots * model * (3 * halves * hidden + 2 * tokens),
            bytes_accessed=6 * rows * model * hidden + 4 * tokens * model,
            transcendentals=experts * slots * halves * hidden,
        ),
        name="experts",
    )(
        first,
        *pieces,
        in_hbm(jnp.swapaxes(w_gate, 1, 2)),
        in_hbm(jnp.swapaxes(w_up, 1, 2)),
        in_hbm(w_down),
    )


def sums_back(mine, mine_across, other, other_across, part):
    def add(a, *others):
        total = a.astype(F32)
        for b in others:
            total = total + b.astype(F32)
        return total.astype(BF)

    across = add(mine_across, flip(other_across, "tp", 1))
    here = add(mine, flip(other, "tp", 1))
    across = [across[z * part : (z + 1) * part] for z in range(4)]
    here = [here[z * part : (z + 1) * part] for z in range(4)]
    near = flip(across[1], "exp", 1)
    far_across = add(across[2], flip(across[3], "ctx", 1))
    far_across, here[3], here[1] = lax.optimization_barrier((far_across, here[3], here[1]))
    far = flip(far_across, "exp", 1)
    last = flip(here[3], "ctx", 1)
    near = add(here[1], near)
    near, here[2], across[0] = lax.optimization_barrier((near, here[2], across[0]))
    near = flip(near, "ctx", 1)
    own = flip(across[0], "exp", 1)
    far = flip(add(here[2], last, far), "ctx", 2)
    return here[0].astype(F32) + own.astype(F32) + near.astype(F32) + far.astype(F32)


def on_device(
    queries, keys, values, out_weight, resid, expert_ids, router_probs, w_gate, w_up, w_down
):
    n_ctx, n_exp, n_tp = (lax.axis_size(a) for a in ("ctx", "exp", "tp"))
    part = resid.shape[0]
    rows_here = w_gate.shape[0]
    block = expert_ids.shape[0]
    cube = (n_ctx, n_exp, n_tp) == (4, 2, 2) and block == n_tp * part <= LANES
    if not cube or part % 16 or rows_here * n_ctx * n_exp != 2 * EXPERTS:
        return on_device_any_size(
            queries, keys, values, out_weight, resid, expert_ids, router_probs, w_gate, w_up, w_down
        )
    ctx, exp, tp = (lax.axis_index(a) for a in ("ctx", "exp", "tp"))
    place = jnp.stack([ctx, exp, tp]).astype(jnp.int32)
    heads_here = queries.shape[1] // HEAD_DIMENSION
    first = (ctx * n_exp + exp) * rows_here // 2
    slots = n_ctx * n_exp * min(8, block)

    shared = (exp * n_tp + tp) * heads_here // (QUERY_HEADS // KEY_VALUE_HEADS)
    key_head = lax.dynamic_slice_in_dim(keys, shared * HEAD_DIMENSION, HEAD_DIMENSION, 1)
    value_head = lax.dynamic_slice_in_dim(values, shared * HEAD_DIMENSION, HEAD_DIMENSION, 1)
    kv = jnp.concatenate([key_head, value_head], axis=1)
    kv_pieces = [from_earlier(kv, "ctx", z) for z in range(1, n_ctx)]
    *own, routing = own_block(
        place, kv, expert_ids, router_probs, queries, out_weight, resid, n_exp, n_tp
    )
    base, across, other = attend_project(place, kv_pieces, own, n_exp, n_tp)

    other = flip(other, "tp", 1).astype(F32)
    across = flip((across.astype(F32) + other[part:]).astype(BF), "exp", 1)
    hidden = base + other[:part] + across.astype(F32)
    mean_square = jnp.mean(hidden * hidden, axis=1, keepdims=True)
    normed = (hidden * lax.rsqrt(mean_square + 1e-06)).astype(BF)
    normed = jnp.concatenate([normed, routing], axis=1)

    far = flip(normed, "ctx", 2)
    across = flip(normed, "exp", 1)
    near = flip(normed, "ctx", 1)
    far_across = flip(far, "exp", 1)
    near_across = flip(near, "exp", 1)
    last = flip(far, "ctx", 1)
    early = jnp.concatenate([normed, near, far, across, near_across, far_across])
    early, far_onward = lax.optimization_barrier((early, far_across))
    last_across = flip(far_onward, "ctx", 1)
    early_other = flip(early, "tp", 1)
    late_other = flip(jnp.concatenate([last, last_across]), "tp", 1)
    pieces = [normed, near, far, last, across, near_across, far_across, last_across]
    order = [(i, 0) for i in range(8)] + [
        (8, 0), (8, 1), (8, 2), (9, 0), (8, 3), (8, 4), (8, 5), (9, 1)
    ]
    sums = cube_experts(
        first.astype(jnp.int32).reshape(1), pieces + [early_other, late_other], order, part,
        w_gate, w_up, w_down, slots,
    )
    return (hidden + sums_back(*sums, part)).astype(BF)


def solution(mesh):
    in_specs = (
        P(("groups", "ctx"), ("exp", "tp")),
        P(("groups", "ctx"), None),
        P(("groups", "ctx"), None),
        P(("exp", "tp"), None),
        P(("groups", "ctx", "exp", "tp"), None),
        P(("groups", "ctx", "exp"), None),
        P(("groups", "ctx", "exp"), None),
        P(("ctx", "exp"), None, "tp"),
        P(("ctx", "exp"), None, "tp"),
        P(("ctx", "exp"), "tp", None),
    )
    out_specs = P(("groups", "ctx", "exp", "tp"), None)
    return jax.shard_map(
        on_device, mesh=mesh, in_specs=in_specs, out_specs=out_specs, check_vma=False
    )
```

```python
import functools
import math

import jax
import jax.numpy as jnp
from jax import lax
from jax.experimental import pallas as pl
from jax.experimental.pallas import tpu as pltpu
from jax.sharding import PartitionSpec as P

HEAD_DIMENSION = 128
QUERY_HEADS = 32
KEY_VALUE_HEADS = 4
EXPERTS = 64
TOPK = 8
MIB = 1 << 20
LANES = 128
BF = jnp.bfloat16
F32 = jnp.float32


def attend_blocks(blocks, key_head, value_head, heads_here):
    score_scale = 1.0 / math.sqrt(HEAD_DIMENSION)

    def make_state(query_rows):
        row_total = query_rows.shape[0]
        return (
            jnp.full((row_total, heads_here), -1e30, jnp.float32),
            jnp.zeros((row_total, heads_here), jnp.float32),
            jnp.zeros((row_total, heads_here, HEAD_DIMENSION), jnp.float32),
        )

    initial = tuple((make_state(query_rows) for query_rows, query_places in blocks))

    def fold_keys(carry, piece, first):
        key_piece, value_piece = piece
        key_places = jnp.arange(key_piece.shape[0], dtype=jnp.int32)
        updated = []
        for (query_rows, query_places), state in zip(blocks, carry):

            def refresh(state, query_rows=query_rows, query_places=query_places):
                running_max, running_sum, accum = state
                shaped = query_rows.reshape(query_rows.shape[0], heads_here, HEAD_DIMENSION)
                scores = (
                    jnp.einsum("qhd,kd->qhk", shaped, key_piece, preferred_element_type=jnp.float32)
                    * score_scale
                )
                allowed = key_places[None, None, :] <= query_places[:, None, None]
                scores = jnp.where(allowed, scores, -1e30)
                new_max = jnp.maximum(running_max, jnp.max(scores, axis=2))
                weights = jnp.where(allowed, jnp.exp(scores - new_max[:, :, None]), 0.0)
                running_sum = jnp.sum(weights, axis=2)
                accum = jnp.einsum(
                    "qhk,kd->qhd",
                    weights,
                    value_piece.astype(jnp.float32),
                    precision=lax.Precision.HIGHEST,
                )
                return (new_max, running_sum, accum)

            needed = first <= query_places[-1]
            updated.append(lax.cond(needed, refresh, lambda state: state, state))
        return tuple(updated)

    final = fold_keys(
        initial,
        (
            lax.all_gather(key_head, "ctx", axis=0, tiled=True),
            lax.all_gather(value_head, "ctx", axis=0, tiled=True),
        ),
        jnp.int32(0),
    )
    results = []
    for (query_rows, query_places), state in zip(blocks, final):
        running_max, running_sum, accum = state
        results.append(
            (accum / running_sum[:, :, None])
            .reshape(query_rows.shape[0], heads_here * HEAD_DIMENSION)
            .astype(jnp.bfloat16)
        )
    return results


def run_experts(inputs, w_gate, w_up, w_down):
    gate_out = jnp.einsum("rnd,rdf->rnf", inputs, w_gate, preferred_element_type=jnp.float32)
    up_out = jnp.einsum("rnd,rdf->rnf", inputs, w_up, preferred_element_type=jnp.float32)
    activated = (jax.nn.silu(gate_out) * up_out).astype(jnp.bfloat16)
    return jnp.einsum("rnf,rfd->rnd", activated, w_down, preferred_element_type=jnp.float32).astype(
        jnp.bfloat16
    )


def on_device_any_size(
    queries, keys, values, out_weight, resid, expert_ids, router_probs, w_gate, w_up, w_down
):
    rows_ctx = queries.shape[0]
    heads_here = queries.shape[1] // HEAD_DIMENSION
    group_width = QUERY_HEADS // KEY_VALUE_HEADS
    head_rank = lax.axis_index(("exp", "tp"))
    shared = head_rank * heads_here // group_width
    key_head = lax.dynamic_slice_in_dim(keys, shared * HEAD_DIMENSION, HEAD_DIMENSION, 1)
    value_head = lax.dynamic_slice_in_dim(values, shared * HEAD_DIMENSION, HEAD_DIMENSION, 1)
    cycle_rank = lax.axis_index("ctx")
    own_places = cycle_rank * rows_ctx + jnp.arange(rows_ctx, dtype=jnp.int32)
    attended = attend_blocks([(queries, own_places)], key_head, value_head, heads_here)[0]
    projected = lax.psum_scatter(
        jnp.dot(attended, out_weight, preferred_element_type=jnp.float32).astype(jnp.bfloat16),
        ("exp", "tp"),
        scatter_dimension=0,
        tiled=True,
    ).astype(jnp.float32)
    hidden = resid.astype(jnp.float32) + projected
    mean_square = jnp.mean(hidden * hidden, axis=1, keepdims=True)
    normed = (hidden * lax.rsqrt(mean_square + 1e-06)).astype(jnp.bfloat16)
    pair_rows = lax.all_gather(normed, "tp", axis=0, tiled=True)
    slot_count = min(8, expert_ids.shape[0])
    gate_weights = router_probs / jnp.sum(router_probs, axis=1, keepdims=True)
    flat_ids = expert_ids.reshape(-1)
    assigned = flat_ids.shape[0]
    onehot = (flat_ids[:, None] == jnp.arange(EXPERTS, dtype=jnp.int32)[None, :]).astype(jnp.int32)
    slots = jnp.sum(onehot * (jnp.cumsum(onehot, axis=0) - 1), axis=1)
    token_of = jnp.arange(assigned, dtype=jnp.int32) // TOPK
    peer_count = lax.axis_size(("ctx", "exp"))
    rows_here = w_gate.shape[0]
    cell_parts = []
    for half_index in range(2):
        half_rows_id = 2 * flat_ids + half_index
        target = half_rows_id // rows_here
        local_row = half_rows_id % rows_here
        cell_parts.append((local_row * slot_count + slots) * peer_count + target)
    cells = jnp.concatenate(cell_parts)
    table = (
        jnp.full((rows_here * slot_count * peer_count,), -1, jnp.int32)
        .at[cells]
        .set(jnp.concatenate([token_of, token_of]))
    )
    send_buffer = jnp.where(
        table[:, None] >= 0, pair_rows[jnp.maximum(table, 0)], jnp.zeros((), jnp.bfloat16)
    )
    model_width = pair_rows.shape[1]
    received = lax.all_to_all(
        send_buffer.reshape(rows_here * slot_count, peer_count, model_width),
        ("ctx", "exp"),
        split_axis=1,
        concat_axis=1,
        tiled=True,
    )
    expert_out = run_experts(
        received.reshape(rows_here, slot_count * peer_count, model_width), w_gate, w_up, w_down
    )
    returned = lax.all_to_all(
        expert_out.reshape(rows_here * slot_count, peer_count, model_width),
        ("ctx", "exp"),
        split_axis=1,
        concat_axis=1,
        tiled=True,
    )
    returned_flat = returned.reshape(rows_here * slot_count * peer_count, model_width)
    gathered = returned_flat[cells].reshape(2, expert_ids.shape[0], TOPK, model_width)
    routed_part = jnp.einsum(
        "hakd,ak->ad", gathered.astype(jnp.float32), gate_weights, precision=lax.Precision.HIGHEST
    )
    routed = lax.psum_scatter(
        routed_part.astype(jnp.bfloat16), "tp", scatter_dimension=0, tiled=True
    ).astype(jnp.float32)
    return (hidden + routed).astype(jnp.bfloat16)


def flip(x, axis, bit):
    return lax.ppermute(x, axis, [(i, i ^ bit) for i in range(lax.axis_size(axis))])


def flip_both(x):
    n_exp = lax.axis_size("exp")
    mask = n_exp + 1
    size = lax.axis_size("ctx") * n_exp
    return lax.ppermute(x, ("ctx", "exp"), [(i, i ^ mask) for i in range(size)])


def from_earlier(x, axis, steps):
    size = lax.axis_size(axis)
    return lax.ppermute(x, axis, [(i, i + steps) for i in range(size - steps)])


def in_hbm(x):
    return pltpu.with_memory_space_constraint(x, pltpu.HBM)


def dot_rows(a, b):
    return lax.dot_general(a, b, (((1,), (1,)), ((), ())), preferred_element_type=F32)


def own_block_kernel(sizes, place, kv_ref, ids_hbm, probs_hbm, q_hbm, w_hbm, resid_hbm, *refs):
    n_exp, n_tp, heads, part = sizes
    rows = n_exp * n_tp * part
    q_ref, w_ref, resid_ref, out_ref, sum_ref, max_ref, routing_ref = refs[:7]
    v_ext, ids_ref, probs_ref, packed, q_sem, sems = refs[7:]
    fetch = [
        pltpu.make_async_copy(ids_hbm, ids_ref, sems.at[0]),
        pltpu.make_async_copy(probs_hbm, probs_ref, sems.at[1]),
        pltpu.make_async_copy(resid_hbm, resid_ref, sems.at[2]),
        pltpu.make_async_copy(w_hbm, w_ref, sems.at[3]),
    ]
    fetch_q = pltpu.make_async_copy(q_hbm, q_ref, q_sem)
    fetch_q.start()
    for copy in fetch:
        copy.start()
    tp = place[2]
    v_ext[:, :HEAD_DIMENSION] = kv_ref[:, HEAD_DIMENSION:]
    v_ext[:, HEAD_DIMENSION:] = jnp.ones((rows, HEAD_DIMENSION), BF)
    keys = kv_ref[:, :HEAD_DIMENSION]
    allowed = lax.broadcasted_iota(jnp.int32, (rows, rows), 1) <= lax.broadcasted_iota(
        jnp.int32, (rows, rows), 0
    )
    scale = 1.0 / math.sqrt(HEAD_DIMENSION)
    fetch_q.wait()
    for h in range(heads):
        columns = slice(h * HEAD_DIMENSION, (h + 1) * HEAD_DIMENSION)
        s = jnp.where(allowed, dot_rows(q_ref[:, columns], keys) * scale, -1e30)
        top = jnp.max(s, axis=1, keepdims=True)
        out = jnp.dot(jnp.exp(s - top).astype(BF), v_ext[...], preferred_element_type=F32)
        out_ref[:, columns] = out[:, :HEAD_DIMENSION]
        sum_ref[:, columns] = out[:, HEAD_DIMENSION:]
        max_ref[:, h : h + 1] = top

    fetch[0].wait()
    fetch[1].wait()
    block = n_tp * part
    ids = ids_ref[...]
    probs = probs_ref[...]
    expert = lax.broadcasted_iota(jnp.int32, (EXPERTS, block), 0)
    named = jnp.zeros((EXPERTS, block), F32)
    for k in range(TOPK):
        named = named + jnp.where(expert == ids[k : k + 1, :], 1.0, 0.0)
    before = lax.broadcasted_iota(jnp.int32, (block, block), 0) < lax.broadcasted_iota(
        jnp.int32, (block, block), 1
    )
    count = jnp.dot(
        named.astype(BF), jnp.where(before, 1.0, 0.0).astype(BF), preferred_element_type=F32
    )
    ranks = [
        jnp.sum(jnp.where(expert == ids[k : k + 1, :], count, 0.0), axis=0, keepdims=True)
        for k in range(TOPK)
    ]
    gates = probs / jnp.sum(probs, axis=0, keepdims=True)
    high = gates.astype(BF).astype(F32)
    fields = jnp.concatenate([ids.astype(F32)] + ranks + [high, gates - high], axis=0)
    packed[...] = jnp.zeros_like(packed)
    packed[: 4 * TOPK, :block] = fields
    packed[...] = packed[...].T
    routing_ref[...] = packed[pl.ds(pl.multiple_of(tp * part, part), part), :].astype(BF)
    fetch[2].wait()
    fetch[3].wait()


def own_block(place, kv, expert_ids, router_probs, queries, out_weight, resid, n_exp, n_tp):
    rows, width = queries.shape
    heads = width // HEAD_DIMENSION
    part, model = resid.shape
    block = expert_ids.shape[0]
    vmem = pl.BlockSpec(memory_space=pltpu.VMEM)
    hbm = pl.BlockSpec(memory_space=pltpu.HBM)
    return pl.pallas_call(
        functools.partial(own_block_kernel, (n_exp, n_tp, heads, part)),
        out_shape=(
            jax.ShapeDtypeStruct((rows, width), BF),
            jax.ShapeDtypeStruct((width, model), BF),
            jax.ShapeDtypeStruct((part, model), BF),
            jax.ShapeDtypeStruct((rows, width), F32),
            jax.ShapeDtypeStruct((rows, width), F32),
            jax.ShapeDtypeStruct((rows, LANES), F32),
            jax.ShapeDtypeStruct((part, LANES), BF),
        ),
        in_specs=[pl.BlockSpec(memory_space=pltpu.SMEM), vmem] + [hbm] * 5,
        out_specs=(vmem,) * 7,
        scratch_shapes=[
            pltpu.VMEM((rows, 2 * HEAD_DIMENSION), BF),
            pltpu.VMEM((TOPK, block), jnp.int32),
            pltpu.VMEM((TOPK, block), F32),
            pltpu.VMEM((LANES, LANES), F32),
            pltpu.SemaphoreType.DMA,
            pltpu.SemaphoreType.DMA((4,)),
        ],
        compiler_params=pltpu.CompilerParams(vmem_limit_bytes=20 * MIB),
        cost_estimate=pl.CostEstimate(
            flops=6 * rows * width * rows,
            bytes_accessed=2 * (rows * width + width * model + rows * model),
            transcendentals=rows * rows * heads,
        ),
        name="own_block",
    )(place, kv, *map(in_hbm, (expert_ids.T, router_probs.T, queries, out_weight, resid)))


def attention_kernel(sizes, place, *refs):
    n_ctx, n_exp, n_tp, heads, part = sizes
    rows = n_exp * n_tp * part
    kv_refs, refs = refs[: n_ctx - 1], refs[n_ctx - 1 :]
    q_ref, w_ref, resid_ref, out_ref, sum_ref, max_ref = refs[:6]
    base_ref, across_ref, other_ref = refs[6:9]
    k_all, v_all, att, att_rel = refs[9:]
    ctx, exp, tp = place[0], place[1], place[2]
    for z in range(n_ctx - 1):
        k_all[z * rows : (z + 1) * rows, :] = kv_refs[z][:, :HEAD_DIMENSION]
        v_all[z * rows : (z + 1) * rows, :HEAD_DIMENSION] = kv_refs[z][:, HEAD_DIMENSION:]
    v_all[:, HEAD_DIMENSION:] = jnp.ones(((n_ctx - 1) * rows, HEAD_DIMENSION), BF)
    allowed = lax.broadcasted_iota(jnp.int32, (1, (n_ctx - 1) * rows), 1) < ctx * rows
    scale = 1.0 / math.sqrt(HEAD_DIMENSION)
    for h in range(heads):
        columns = slice(h * HEAD_DIMENSION, (h + 1) * HEAD_DIMENSION)
        s = jnp.where(allowed, dot_rows(q_ref[:, columns], k_all[...]) * scale, -1e30)
        own_top = max_ref[:, h : h + 1]
        top = jnp.maximum(own_top, jnp.max(s, axis=1, keepdims=True))
        keep = jnp.exp(own_top - top)
        out = jnp.dot(jnp.exp(s - top).astype(BF), v_all[...], preferred_element_type=F32)
        total = sum_ref[:, columns] * keep + out[:, HEAD_DIMENSION:]
        out = out_ref[:, columns] * keep + out[:, :HEAD_DIMENSION]
        att[:, columns] = (out / total).astype(BF)
    for t in range(n_tp):
        for x in range(n_exp):
            owner = lax.rem(exp + x, n_exp) * n_tp + lax.rem(tp + t, n_tp)
            source = pl.ds(pl.multiple_of(owner * part, part), part)
            at = (t * n_exp + x) * part
            att_rel[at : at + part, :] = att[source, :]
    projected = jnp.dot(att_rel[...], w_ref[...], preferred_element_type=F32)
    base_ref[...] = resid_ref[...].astype(F32) + projected[:part]
    across_ref[...] = projected[part : 2 * part].astype(BF)
    other_ref[...] = projected[2 * part :].astype(BF)


def attend_project(place, pieces, own, n_exp, n_tp):
    queries, out_weight, resid = own[:3]
    rows, width = queries.shape
    n_ctx, heads = len(pieces) + 1, width // HEAD_DIMENSION
    part, model = resid.shape
    vmem = pl.BlockSpec(memory_space=pltpu.VMEM)
    return pl.pallas_call(
        functools.partial(attention_kernel, (n_ctx, n_exp, n_tp, heads, part)),
        out_shape=(
            jax.ShapeDtypeStruct((part, model), F32),
            jax.ShapeDtypeStruct((part, model), BF),
            jax.ShapeDtypeStruct((2 * part, model), BF),
        ),
        in_specs=[pl.BlockSpec(memory_space=pltpu.SMEM)] + [vmem] * (n_ctx - 1 + len(own)),
        out_specs=(vmem,) * 3,
        scratch_shapes=[
            pltpu.VMEM(((n_ctx - 1) * rows, HEAD_DIMENSION), BF),
            pltpu.VMEM(((n_ctx - 1) * rows, 2 * HEAD_DIMENSION), BF),
            pltpu.VMEM((rows, width), BF),
            pltpu.VMEM((rows, width), BF),
        ],
        compiler_params=pltpu.CompilerParams(vmem_limit_bytes=20 * MIB),
        cost_estimate=pl.CostEstimate(
            flops=2 * rows * width * (3 * (n_ctx - 1) * rows + model),
            bytes_accessed=2 * (rows * width + width * model + rows * model),
            transcendentals=rows * n_ctx * rows * heads,
        ),
        name="attend_project",
    )(place, *pieces, *own)


def expert_kernel(n_pieces, depth, experts, first_ref, *refs):
    pieces, (wg_hbm, wu_hbm, wd_hbm) = refs[:n_pieces], refs[n_pieces : n_pieces + 3]
    outs = refs[n_pieces + 3 : n_pieces + 7]
    x_all, packed, pick_all, scale_all, out_all, wgu, wd, act, sems = refs[n_pieces + 7 :]
    tokens = x_all.shape[0]
    slots = pick_all.shape[0] // experts
    _, _, halves, hidden, model = wgu.shape
    part = tokens // n_pieces
    blocks = n_pieces // 2

    def copies(e):
        slot = lax.rem(e, depth)
        rows = pl.ds(e * halves, halves)
        return (
            pltpu.make_async_copy(wg_hbm.at[rows], wgu.at[slot, 0], sems.at[0, slot]),
            pltpu.make_async_copy(wu_hbm.at[rows], wgu.at[slot, 1], sems.at[1, slot]),
            pltpu.make_async_copy(wd_hbm.at[rows], wd.at[slot], sems.at[2, slot]),
        )

    def start(e):
        for copy in copies(e):
            copy.start()

    def wait(e):
        for copy in copies(e):
            copy.wait()

    def gate_up(e):
        x = out_all[pl.ds(pl.multiple_of(e * slots, slots), slots), :]
        weight = wgu[lax.rem(e, depth)].reshape(2 * halves * hidden, model)
        both = dot_rows(weight, x)
        gate, up = both[: halves * hidden], both[halves * hidden :]
        return (gate * jax.nn.sigmoid(gate) * up).astype(BF)

    def down(e):
        here = pl.ds(pl.multiple_of(e * slots, slots), slots)
        weight = wd[lax.rem(e, depth)].reshape(halves * hidden, model)
        out = lax.dot_general(
            act[lax.rem(e, 2)], weight, (((0,), (0,)), ((), ())), preferred_element_type=F32
        )
        return here, (out * scale_all[here, :]).astype(BF)

    for e in range(min(depth - 1, experts)):
        start(e)
    for i, piece in enumerate(pieces):
        x_all[i * part : (i + 1) * part, :] = piece[:, :model]
        packed[i * part : (i + 1) * part, :] = piece[:, model:].astype(F32)
    fields = packed[...].T
    ids, ranks = fields[:TOPK], fields[TOPK : 2 * TOPK]
    gates = fields[2 * TOPK : 3 * TOPK] + fields[3 * TOPK : 4 * TOPK]
    token = lax.broadcasted_iota(jnp.int32, (TOPK, tokens), 1)
    places = ranks.astype(jnp.int32) + lax.rem(token // part, blocks) * (slots // blocks)
    slot = lax.broadcasted_iota(jnp.int32, (slots, tokens), 0)
    for e in range(experts):
        hit = ids.astype(jnp.int32) == first_ref[0] + e
        chosen = slot == jnp.max(jnp.where(hit, places, -1), axis=0, keepdims=True)
        gate = jnp.sum(jnp.where(hit, gates, 0.0), axis=0, keepdims=True)
        here = slice(e * slots, (e + 1) * slots)
        pick_all[here, :] = jnp.where(chosen, 1.0, 0.0).astype(BF)
        scale_all[here, :] = jnp.sum(jnp.where(chosen, gate, 0.0), axis=1, keepdims=True)
    out_all[...] = jnp.dot(pick_all[...], x_all[...], preferred_element_type=F32).astype(BF)
    wait(0)
    act[0] = gate_up(0)

    @pl.loop(0, experts - 1)
    def _(e):
        @pl.when(e + depth - 1 < experts)
        def _():
            start(e + depth - 1)

        wait(e + 1)
        following = gate_up(e + 1)
        here, out = down(e)
        act[lax.rem(e + 1, 2)] = following
        out_all[here, :] = out

    here, out = down(experts - 1)
    out_all[here, :] = out
    quarter = tokens // 4
    for i, o_ref in enumerate(outs):
        o_ref[...] = lax.dot_general(
            pick_all[:, i * quarter : (i + 1) * quarter],
            out_all[...],
            (((0,), (0,)), ((), ())),
            preferred_element_type=F32,
        ).astype(BF)


def cube_experts(first, pieces, w_gate, w_up, w_down, slots):
    rows, hidden, model = w_down.shape
    halves = 2
    experts = rows // halves
    tokens = len(pieces) * pieces[0].shape[0]
    depth = min(4, experts)
    vmem = pl.BlockSpec(memory_space=pltpu.VMEM)
    hbm = pl.BlockSpec(memory_space=pltpu.HBM)

    out = jax.ShapeDtypeStruct((tokens // 4, model), BF)
    return pl.pallas_call(
        functools.partial(expert_kernel, len(pieces), depth, experts),
        out_shape=(out,) * 4,
        in_specs=[pl.BlockSpec(memory_space=pltpu.SMEM)] + [vmem] * len(pieces) + [hbm] * 3,
        out_specs=(vmem,) * 4,
        scratch_shapes=[
            pltpu.VMEM((tokens, model), BF),
            pltpu.VMEM((tokens, LANES), F32),
            pltpu.VMEM((experts * slots, tokens), BF),
            pltpu.VMEM((experts * slots, 1), F32),
            pltpu.VMEM((experts * slots, model), BF),
            pltpu.VMEM((depth, 2, halves, hidden, model), BF),
            pltpu.VMEM((depth, halves, hidden, model), BF),
            pltpu.VMEM((2, halves * hidden, slots), BF),
            pltpu.SemaphoreType.DMA((3, depth)),
        ],
        compiler_params=pltpu.CompilerParams(vmem_limit_bytes=44 * MIB),
        cost_estimate=pl.CostEstimate(
            flops=2 * experts * slots * model * (3 * halves * hidden + 2 * tokens),
            bytes_accessed=6 * rows * model * hidden + 4 * tokens * model,
            transcendentals=experts * slots * halves * hidden,
        ),
        name="experts",
    )(
        first,
        *pieces,
        in_hbm(jnp.swapaxes(w_gate, 1, 2)),
        in_hbm(jnp.swapaxes(w_up, 1, 2)),
        in_hbm(w_down),
    )


def sums_back(mine, mine_across, other, other_across, part):
    def add(a, *others):
        total = a.astype(F32)
        for b in others:
            total = total + b.astype(F32)
        return total.astype(BF)

    across = add(mine_across, flip(other_across, "tp", 1))
    here = add(mine, flip(other, "tp", 1))
    across = [across[z * part : (z + 1) * part] for z in range(4)]
    here = [here[z * part : (z + 1) * part] for z in range(4)]
    far_across = flip(across[2], "exp", 1)
    last_across = flip_both(across[3])
    last = flip(here[3], "ctx", 1)
    own = flip(across[0], "exp", 1)
    near = flip(here[1], "ctx", 1)
    near_across = flip_both(across[1])
    far = flip(add(here[2], last, far_across, last_across), "ctx", 2)
    total = here[0].astype(F32)
    for term in (own, near, near_across, far):
        total = total + term.astype(F32)
    return total


def on_device(
    queries, keys, values, out_weight, resid, expert_ids, router_probs, w_gate, w_up, w_down
):
    n_ctx, n_exp, n_tp = (lax.axis_size(a) for a in ("ctx", "exp", "tp"))
    part = resid.shape[0]
    rows_here = w_gate.shape[0]
    block = expert_ids.shape[0]
    cube = (n_ctx, n_exp, n_tp) == (4, 2, 2) and block == n_tp * part <= LANES
    if not cube or part % 16 or rows_here * n_ctx * n_exp != 2 * EXPERTS:
        return on_device_any_size(
            queries, keys, values, out_weight, resid, expert_ids, router_probs, w_gate, w_up, w_down
        )
    ctx, exp, tp = (lax.axis_index(a) for a in ("ctx", "exp", "tp"))
    place = jnp.stack([ctx, exp, tp]).astype(jnp.int32)
    heads_here = queries.shape[1] // HEAD_DIMENSION
    first = (ctx * n_exp + exp) * rows_here // 2
    slots = n_ctx * n_exp * min(8, block)

    shared = (exp * n_tp + tp) * heads_here // (QUERY_HEADS // KEY_VALUE_HEADS)
    key_head = lax.dynamic_slice_in_dim(keys, shared * HEAD_DIMENSION, HEAD_DIMENSION, 1)
    value_head = lax.dynamic_slice_in_dim(values, shared * HEAD_DIMENSION, HEAD_DIMENSION, 1)
    kv = jnp.concatenate([key_head, value_head], axis=1)
    kv_pieces = [from_earlier(kv, "ctx", z) for z in range(1, n_ctx)]
    *own, routing = own_block(
        place, kv, expert_ids, router_probs, queries, out_weight, resid, n_exp, n_tp
    )
    base, across, other = attend_project(place, kv_pieces, own, n_exp, n_tp)

    other = flip(other, "tp", 1).astype(F32)
    across = flip((across.astype(F32) + other[part:]).astype(BF), "exp", 1)
    hidden = base + other[:part] + across.astype(F32)
    mean_square = jnp.mean(hidden * hidden, axis=1, keepdims=True)
    normed = (hidden * lax.rsqrt(mean_square + 1e-06)).astype(BF)
    normed = jnp.concatenate([normed, routing], axis=1)

    far = flip(normed, "ctx", 2)
    across = flip(normed, "exp", 1)
    near = flip(normed, "ctx", 1)
    near_across = flip_both(normed)
    far_across = flip(far, "exp", 1)
    last_across = flip_both(far)
    last = flip(far, "ctx", 1)
    early = lax.optimization_barrier((normed, near, far, across, near_across))
    pieces = [normed, near, far, last, across, near_across, far_across, last_across]
    pieces += [flip(piece, "tp", 1) for piece in early[:3] + (last,)]
    pieces += [flip(piece, "tp", 1) for piece in early[3:] + (far_across, last_across)]
    sums = cube_experts(
        first.astype(jnp.int32).reshape(1), pieces, w_gate, w_up, w_down, slots
    )
    return (hidden + sums_back(*sums, part)).astype(BF)


def solution(mesh):
    in_specs = (
        P(("groups", "ctx"), ("exp", "tp")),
        P(("groups", "ctx"), None),
        P(("groups", "ctx"), None),
        P(("exp", "tp"), None),
        P(("groups", "ctx", "exp", "tp"), None),
        P(("groups", "ctx", "exp"), None),
        P(("groups", "ctx", "exp"), None),
        P(("ctx", "exp"), None, "tp"),
        P(("ctx", "exp"), None, "tp"),
        P(("ctx", "exp"), "tp", None),
    )
    out_specs = P(("groups", "ctx", "exp", "tp"), None)
    return jax.shard_map(
        on_device, mesh=mesh, in_specs=in_specs, out_specs=out_specs, check_vma=False
    )
```

```python
import functools
import math

import jax
import jax.numpy as jnp
from jax import lax
from jax.experimental import pallas as pl
from jax.experimental.pallas import tpu as pltpu
from jax.sharding import PartitionSpec as P

HEAD_DIMENSION = 128
QUERY_HEADS = 32
KEY_VALUE_HEADS = 4
EXPERTS = 64
TOPK = 8
MIB = 1 << 20
LANES = 128
BF = jnp.bfloat16
F32 = jnp.float32


def attend_blocks(blocks, key_head, value_head, heads_here):
    score_scale = 1.0 / math.sqrt(HEAD_DIMENSION)

    def make_state(query_rows):
        row_total = query_rows.shape[0]
        return (
            jnp.full((row_total, heads_here), -1e30, jnp.float32),
            jnp.zeros((row_total, heads_here), jnp.float32),
            jnp.zeros((row_total, heads_here, HEAD_DIMENSION), jnp.float32),
        )

    initial = tuple((make_state(query_rows) for query_rows, query_places in blocks))

    def fold_keys(carry, piece, first):
        key_piece, value_piece = piece
        key_places = jnp.arange(key_piece.shape[0], dtype=jnp.int32)
        updated = []
        for (query_rows, query_places), state in zip(blocks, carry):

            def refresh(state, query_rows=query_rows, query_places=query_places):
                running_max, running_sum, accum = state
                shaped = query_rows.reshape(query_rows.shape[0], heads_here, HEAD_DIMENSION)
                scores = (
                    jnp.einsum("qhd,kd->qhk", shaped, key_piece, preferred_element_type=jnp.float32)
                    * score_scale
                )
                allowed = key_places[None, None, :] <= query_places[:, None, None]
                scores = jnp.where(allowed, scores, -1e30)
                new_max = jnp.maximum(running_max, jnp.max(scores, axis=2))
                weights = jnp.where(allowed, jnp.exp(scores - new_max[:, :, None]), 0.0)
                running_sum = jnp.sum(weights, axis=2)
                accum = jnp.einsum(
                    "qhk,kd->qhd",
                    weights,
                    value_piece.astype(jnp.float32),
                    precision=lax.Precision.HIGHEST,
                )
                return (new_max, running_sum, accum)

            needed = first <= query_places[-1]
            updated.append(lax.cond(needed, refresh, lambda state: state, state))
        return tuple(updated)

    final = fold_keys(
        initial,
        (
            lax.all_gather(key_head, "ctx", axis=0, tiled=True),
            lax.all_gather(value_head, "ctx", axis=0, tiled=True),
        ),
        jnp.int32(0),
    )
    results = []
    for (query_rows, query_places), state in zip(blocks, final):
        running_max, running_sum, accum = state
        results.append(
            (accum / running_sum[:, :, None])
            .reshape(query_rows.shape[0], heads_here * HEAD_DIMENSION)
            .astype(jnp.bfloat16)
        )
    return results


def run_experts(inputs, w_gate, w_up, w_down):
    gate_out = jnp.einsum("rnd,rdf->rnf", inputs, w_gate, preferred_element_type=jnp.float32)
    up_out = jnp.einsum("rnd,rdf->rnf", inputs, w_up, preferred_element_type=jnp.float32)
    activated = (jax.nn.silu(gate_out) * up_out).astype(jnp.bfloat16)
    return jnp.einsum("rnf,rfd->rnd", activated, w_down, preferred_element_type=jnp.float32).astype(
        jnp.bfloat16
    )


def on_device_any_size(
    queries, keys, values, out_weight, resid, expert_ids, router_probs, w_gate, w_up, w_down
):
    rows_ctx = queries.shape[0]
    heads_here = queries.shape[1] // HEAD_DIMENSION
    group_width = QUERY_HEADS // KEY_VALUE_HEADS
    head_rank = lax.axis_index(("exp", "tp"))
    shared = head_rank * heads_here // group_width
    key_head = lax.dynamic_slice_in_dim(keys, shared * HEAD_DIMENSION, HEAD_DIMENSION, 1)
    value_head = lax.dynamic_slice_in_dim(values, shared * HEAD_DIMENSION, HEAD_DIMENSION, 1)
    cycle_rank = lax.axis_index("ctx")
    own_places = cycle_rank * rows_ctx + jnp.arange(rows_ctx, dtype=jnp.int32)
    attended = attend_blocks([(queries, own_places)], key_head, value_head, heads_here)[0]
    projected = lax.psum_scatter(
        jnp.dot(attended, out_weight, preferred_element_type=jnp.float32).astype(jnp.bfloat16),
        ("exp", "tp"),
        scatter_dimension=0,
        tiled=True,
    ).astype(jnp.float32)
    hidden = resid.astype(jnp.float32) + projected
    mean_square = jnp.mean(hidden * hidden, axis=1, keepdims=True)
    normed = (hidden * lax.rsqrt(mean_square + 1e-06)).astype(jnp.bfloat16)
    pair_rows = lax.all_gather(normed, "tp", axis=0, tiled=True)
    slot_count = min(8, expert_ids.shape[0])
    gate_weights = router_probs / jnp.sum(router_probs, axis=1, keepdims=True)
    flat_ids = expert_ids.reshape(-1)
    assigned = flat_ids.shape[0]
    onehot = (flat_ids[:, None] == jnp.arange(EXPERTS, dtype=jnp.int32)[None, :]).astype(jnp.int32)
    slots = jnp.sum(onehot * (jnp.cumsum(onehot, axis=0) - 1), axis=1)
    token_of = jnp.arange(assigned, dtype=jnp.int32) // TOPK
    peer_count = lax.axis_size(("ctx", "exp"))
    rows_here = w_gate.shape[0]
    cell_parts = []
    for half_index in range(2):
        half_rows_id = 2 * flat_ids + half_index
        target = half_rows_id // rows_here
        local_row = half_rows_id % rows_here
        cell_parts.append((local_row * slot_count + slots) * peer_count + target)
    cells = jnp.concatenate(cell_parts)
    table = (
        jnp.full((rows_here * slot_count * peer_count,), -1, jnp.int32)
        .at[cells]
        .set(jnp.concatenate([token_of, token_of]))
    )
    send_buffer = jnp.where(
        table[:, None] >= 0, pair_rows[jnp.maximum(table, 0)], jnp.zeros((), jnp.bfloat16)
    )
    model_width = pair_rows.shape[1]
    received = lax.all_to_all(
        send_buffer.reshape(rows_here * slot_count, peer_count, model_width),
        ("ctx", "exp"),
        split_axis=1,
        concat_axis=1,
        tiled=True,
    )
    expert_out = run_experts(
        received.reshape(rows_here, slot_count * peer_count, model_width), w_gate, w_up, w_down
    )
    returned = lax.all_to_all(
        expert_out.reshape(rows_here * slot_count, peer_count, model_width),
        ("ctx", "exp"),
        split_axis=1,
        concat_axis=1,
        tiled=True,
    )
    returned_flat = returned.reshape(rows_here * slot_count * peer_count, model_width)
    gathered = returned_flat[cells].reshape(2, expert_ids.shape[0], TOPK, model_width)
    routed_part = jnp.einsum(
        "hakd,ak->ad", gathered.astype(jnp.float32), gate_weights, precision=lax.Precision.HIGHEST
    )
    routed = lax.psum_scatter(
        routed_part.astype(jnp.bfloat16), "tp", scatter_dimension=0, tiled=True
    ).astype(jnp.float32)
    return (hidden + routed).astype(jnp.bfloat16)


def flip(x, axis, bit):
    return lax.ppermute(x, axis, [(i, i ^ bit) for i in range(lax.axis_size(axis))])


def flip_both(x):
    n_exp = lax.axis_size("exp")
    mask = n_exp + 1
    size = lax.axis_size("ctx") * n_exp
    return lax.ppermute(x, ("ctx", "exp"), [(i, i ^ mask) for i in range(size)])


def from_earlier(x, axis, steps):
    size = lax.axis_size(axis)
    return lax.ppermute(x, axis, [(i, i + steps) for i in range(size - steps)])


def in_hbm(x):
    return pltpu.with_memory_space_constraint(x, pltpu.HBM)


def dot_rows(a, b):
    return lax.dot_general(a, b, (((1,), (1,)), ((), ())), preferred_element_type=F32)


def own_block_kernel(sizes, place, kv_ref, ids_hbm, probs_hbm, q_hbm, w_hbm, resid_hbm, *refs):
    n_exp, n_tp, heads, part = sizes
    rows = n_exp * n_tp * part
    q_ref, w_ref, resid_ref, out_ref, sum_ref, max_ref, routing_ref = refs[:7]
    v_ext, ids_ref, probs_ref, packed, q_sem, sems = refs[7:]
    fetch = [
        pltpu.make_async_copy(ids_hbm, ids_ref, sems.at[0]),
        pltpu.make_async_copy(probs_hbm, probs_ref, sems.at[1]),
        pltpu.make_async_copy(resid_hbm, resid_ref, sems.at[2]),
        pltpu.make_async_copy(w_hbm, w_ref, sems.at[3]),
    ]
    fetch_q = pltpu.make_async_copy(q_hbm, q_ref, q_sem)
    fetch_q.start()
    for copy in fetch:
        copy.start()
    tp = place[2]
    v_ext[:, :HEAD_DIMENSION] = kv_ref[:, HEAD_DIMENSION:]
    v_ext[:, HEAD_DIMENSION:] = jnp.ones((rows, HEAD_DIMENSION), BF)
    keys = kv_ref[:, :HEAD_DIMENSION]
    allowed = lax.broadcasted_iota(jnp.int32, (rows, rows), 1) <= lax.broadcasted_iota(
        jnp.int32, (rows, rows), 0
    )
    scale = 1.0 / math.sqrt(HEAD_DIMENSION)
    fetch_q.wait()
    for h in range(heads):
        columns = slice(h * HEAD_DIMENSION, (h + 1) * HEAD_DIMENSION)
        s = jnp.where(allowed, dot_rows(q_ref[:, columns], keys) * scale, -1e30)
        top = jnp.max(s, axis=1, keepdims=True)
        out = jnp.dot(jnp.exp(s - top).astype(BF), v_ext[...], preferred_element_type=F32)
        out_ref[:, columns] = out[:, :HEAD_DIMENSION]
        sum_ref[:, columns] = out[:, HEAD_DIMENSION:]
        max_ref[:, h : h + 1] = top

    fetch[0].wait()
    fetch[1].wait()
    block = n_tp * part
    ids = ids_ref[...]
    probs = probs_ref[...]
    expert = lax.broadcasted_iota(jnp.int32, (EXPERTS, block), 0)
    named = jnp.zeros((EXPERTS, block), F32)
    for k in range(TOPK):
        named = named + jnp.where(expert == ids[k : k + 1, :], 1.0, 0.0)
    before = lax.broadcasted_iota(jnp.int32, (block, block), 0) < lax.broadcasted_iota(
        jnp.int32, (block, block), 1
    )
    count = jnp.dot(
        named.astype(BF), jnp.where(before, 1.0, 0.0).astype(BF), preferred_element_type=F32
    )
    ranks = [
        jnp.sum(jnp.where(expert == ids[k : k + 1, :], count, 0.0), axis=0, keepdims=True)
        for k in range(TOPK)
    ]
    gates = probs / jnp.sum(probs, axis=0, keepdims=True)
    high = gates.astype(BF).astype(F32)
    fields = jnp.concatenate([ids.astype(F32)] + ranks + [high, gates - high], axis=0)
    packed[...] = jnp.zeros_like(packed)
    packed[: 4 * TOPK, :block] = fields
    packed[...] = packed[...].T
    routing_ref[...] = packed[pl.ds(pl.multiple_of(tp * part, part), part), :].astype(BF)
    fetch[2].wait()
    fetch[3].wait()


def own_block(place, kv, expert_ids, router_probs, queries, out_weight, resid, n_exp, n_tp):
    rows, width = queries.shape
    heads = width // HEAD_DIMENSION
    part, model = resid.shape
    block = expert_ids.shape[0]
    vmem = pl.BlockSpec(memory_space=pltpu.VMEM)
    hbm = pl.BlockSpec(memory_space=pltpu.HBM)
    return pl.pallas_call(
        functools.partial(own_block_kernel, (n_exp, n_tp, heads, part)),
        out_shape=(
            jax.ShapeDtypeStruct((rows, width), BF),
            jax.ShapeDtypeStruct((width, model), BF),
            jax.ShapeDtypeStruct((part, model), BF),
            jax.ShapeDtypeStruct((rows, width), F32),
            jax.ShapeDtypeStruct((rows, width), F32),
            jax.ShapeDtypeStruct((rows, LANES), F32),
            jax.ShapeDtypeStruct((part, LANES), BF),
        ),
        in_specs=[pl.BlockSpec(memory_space=pltpu.SMEM), vmem] + [hbm] * 5,
        out_specs=(vmem,) * 7,
        scratch_shapes=[
            pltpu.VMEM((rows, 2 * HEAD_DIMENSION), BF),
            pltpu.VMEM((TOPK, block), jnp.int32),
            pltpu.VMEM((TOPK, block), F32),
            pltpu.VMEM((LANES, LANES), F32),
            pltpu.SemaphoreType.DMA,
            pltpu.SemaphoreType.DMA((4,)),
        ],
        compiler_params=pltpu.CompilerParams(vmem_limit_bytes=20 * MIB),
        cost_estimate=pl.CostEstimate(
            flops=6 * rows * width * rows,
            bytes_accessed=2 * (rows * width + width * model + rows * model),
            transcendentals=rows * rows * heads,
        ),
        name="own_block",
    )(place, kv, *map(in_hbm, (expert_ids.T, router_probs.T, queries, out_weight, resid)))


def dot_columns(a, b):
    return lax.dot_general(a, b, (((0,), (0,)), ((), ())), preferred_element_type=F32)


def attention_kernel(sizes, place, *refs):
    n_ctx, n_exp, n_tp, heads, part = sizes
    rows = n_exp * n_tp * part
    kv_refs, refs = refs[: n_ctx - 1], refs[n_ctx - 1 :]
    q_ref, w_ref, resid_ref, out_ref, sum_ref, max_ref = refs[:6]
    base_ref, across_ref, other_ref = refs[6:9]
    k_all, v_all, att, att_rel = refs[9:]
    ctx, exp, tp = place[0], place[1], place[2]
    for z in range(n_ctx - 1):
        k_all[z * rows : (z + 1) * rows, :] = kv_refs[z][:, :HEAD_DIMENSION]
        v_all[z * rows : (z + 1) * rows, :HEAD_DIMENSION] = kv_refs[z][:, HEAD_DIMENSION:]
    v_all[:, HEAD_DIMENSION:] = jnp.ones(((n_ctx - 1) * rows, HEAD_DIMENSION), BF)
    allowed = lax.broadcasted_iota(jnp.int32, (1, (n_ctx - 1) * rows), 1) < ctx * rows
    scale = 1.0 / math.sqrt(HEAD_DIMENSION)
    for h in range(heads):
        columns = slice(h * HEAD_DIMENSION, (h + 1) * HEAD_DIMENSION)
        s = jnp.where(allowed, dot_rows(q_ref[:, columns], k_all[...]) * scale, -1e30)
        own_top = max_ref[:, h : h + 1]
        top = jnp.maximum(own_top, jnp.max(s, axis=1, keepdims=True))
        keep = jnp.exp(own_top - top)
        out = jnp.dot(jnp.exp(s - top).astype(BF), v_all[...], preferred_element_type=F32)
        total = sum_ref[:, columns] * keep + out[:, HEAD_DIMENSION:]
        out = out_ref[:, columns] * keep + out[:, :HEAD_DIMENSION]
        att[:, columns] = (out / total).astype(BF)
    for t in range(n_tp):
        for x in range(n_exp):
            owner = lax.rem(exp + x, n_exp) * n_tp + lax.rem(tp + t, n_tp)
            source = pl.ds(pl.multiple_of(owner * part, part), part)
            at = (t * n_exp + x) * part
            att_rel[at : at + part, :] = att[source, :]
    projected = jnp.dot(att_rel[...], w_ref[...], preferred_element_type=F32)
    base_ref[...] = resid_ref[...].astype(F32) + projected[:part]
    across_ref[...] = projected[part : 2 * part].astype(BF)
    other_ref[...] = projected[2 * part :].astype(BF)


def attend_project(place, pieces, own, n_exp, n_tp):
    queries, out_weight, resid = own[:3]
    rows, width = queries.shape
    n_ctx, heads = len(pieces) + 1, width // HEAD_DIMENSION
    part, model = resid.shape
    vmem = pl.BlockSpec(memory_space=pltpu.VMEM)
    return pl.pallas_call(
        functools.partial(attention_kernel, (n_ctx, n_exp, n_tp, heads, part)),
        out_shape=(
            jax.ShapeDtypeStruct((part, model), F32),
            jax.ShapeDtypeStruct((part, model), BF),
            jax.ShapeDtypeStruct((2 * part, model), BF),
        ),
        in_specs=[pl.BlockSpec(memory_space=pltpu.SMEM)] + [vmem] * (n_ctx - 1 + len(own)),
        out_specs=(vmem,) * 3,
        scratch_shapes=[
            pltpu.VMEM(((n_ctx - 1) * rows, HEAD_DIMENSION), BF),
            pltpu.VMEM(((n_ctx - 1) * rows, 2 * HEAD_DIMENSION), BF),
            pltpu.VMEM((rows, width), BF),
            pltpu.VMEM((rows, width), BF),
        ],
        compiler_params=pltpu.CompilerParams(vmem_limit_bytes=20 * MIB),
        cost_estimate=pl.CostEstimate(
            flops=2 * rows * width * (3 * (n_ctx - 1) * rows + model),
            bytes_accessed=2 * (rows * width + width * model + rows * model),
            transcendentals=rows * n_ctx * rows * heads,
        ),
        name="attend_project",
    )(place, *pieces, *own)


def expert_kernel(n_pieces, depth, experts, first_ref, *refs):
    pieces, (wg_hbm, wu_hbm, wd_hbm) = refs[:n_pieces], refs[n_pieces : n_pieces + 3]
    outs = refs[n_pieces + 3 : n_pieces + 9]
    x_all, packed, pick_all, scale_all, out_all, wgu, wd, act, sems = refs[n_pieces + 9 :]
    sides, tokens, model = x_all.shape
    slots = pick_all.shape[1] // experts
    _, _, halves, hidden, _ = wgu.shape
    blocks = n_pieces // (2 * sides)
    part = tokens // (2 * blocks)

    def copies(e):
        slot = lax.rem(e, depth)
        rows = pl.ds(e * halves, halves)
        return (
            pltpu.make_async_copy(wg_hbm.at[rows], wgu.at[slot, 0], sems.at[0, slot]),
            pltpu.make_async_copy(wu_hbm.at[rows], wgu.at[slot, 1], sems.at[1, slot]),
            pltpu.make_async_copy(wd_hbm.at[rows], wd.at[slot], sems.at[2, slot]),
        )

    def start(e):
        for copy in copies(e):
            copy.start()

    def wait(e):
        for copy in copies(e):
            copy.wait()

    def of_expert(e):
        return pl.ds(pl.multiple_of(e * slots, slots), slots)

    def gate_up(e):
        x = jnp.concatenate([out_all[side, of_expert(e), :] for side in range(sides)])
        weight = wgu[lax.rem(e, depth)].reshape(2 * halves * hidden, model)
        both = dot_rows(weight, x)
        gate, up = both[: halves * hidden], both[halves * hidden :]
        return (gate * jax.nn.sigmoid(gate) * up).astype(BF)

    def down(e):
        weight = wd[lax.rem(e, depth)].reshape(halves * hidden, model)
        out = dot_columns(act[lax.rem(e, 2)], weight)
        scale = jnp.concatenate([scale_all[side, of_expert(e), :] for side in range(sides)])
        return (out * scale).astype(BF)

    def keep(e, out):
        for side in range(sides):
            out_all[side, of_expert(e), :] = out[side * slots : (side + 1) * slots]

    for e in range(min(depth - 1, experts)):
        start(e)
    for i, piece in enumerate(pieces):
        core, side, block = i // (sides * blocks), i // blocks % sides, i % blocks
        rows = slice((core * blocks + block) * part, (core * blocks + block + 1) * part)
        x_all[side, rows, :] = piece[:, :model]
        packed[side, rows, :] = piece[:, model:].astype(F32)
    slot = lax.broadcasted_iota(jnp.int32, (slots, tokens), 0)
    token = lax.broadcasted_iota(jnp.int32, (TOPK, tokens), 1)
    offset = lax.rem(token // part, blocks) * (slots // blocks)
    for side in range(sides):
        fields = packed[side].T
        ids, ranks = fields[:TOPK].astype(jnp.int32), fields[TOPK : 2 * TOPK]
        gates = fields[2 * TOPK : 3 * TOPK] + fields[3 * TOPK : 4 * TOPK]
        places = ranks.astype(jnp.int32) + offset
        for e in range(experts):
            hit = ids == first_ref[0] + e
            chosen = slot == jnp.max(jnp.where(hit, places, -1), axis=0, keepdims=True)
            gate = jnp.sum(jnp.where(hit, gates, 0.0), axis=0, keepdims=True)
            here = slice(e * slots, (e + 1) * slots)
            pick_all[side, here, :] = jnp.where(chosen, 1.0, 0.0).astype(BF)
            scale_all[side, here, :] = jnp.sum(
                jnp.where(chosen, gate, 0.0), axis=1, keepdims=True
            )
        out_all[side] = jnp.dot(
            pick_all[side], x_all[side], preferred_element_type=F32
        ).astype(BF)
    wait(0)
    act[0] = gate_up(0)

    @pl.loop(0, experts - 1)
    def _(e):
        @pl.when(e + depth - 1 < experts)
        def _():
            start(e + depth - 1)

        wait(e + 1)
        following = gate_up(e + 1)
        out = down(e)
        act[lax.rem(e + 1, 2)] = following
        keep(e, out)

    keep(experts - 1, down(experts - 1))
    half = blocks * part // 2
    for side in (1, 0):
        routed = dot_columns(pick_all[side], out_all[side]).astype(BF)
        for core in range(2):
            near, far = routed[2 * core * half :][:half], routed[(2 * core + 1) * half :][:half]
            outs[3 * core + 1 - side][...] = far
            outs[3 * core + 2][(1 - side) * half : (2 - side) * half, :] = near


def cube_experts(first, pieces, w_gate, w_up, w_down, slots):
    rows, hidden, model = w_down.shape
    halves, sides = 2, 2
    experts = rows // halves
    tokens = len(pieces) * pieces[0].shape[0] // sides
    depth = min(4, experts)
    vmem = pl.BlockSpec(memory_space=pltpu.VMEM)
    hbm = pl.BlockSpec(memory_space=pltpu.HBM)

    half = jax.ShapeDtypeStruct((tokens // 4, model), BF)
    whole = jax.ShapeDtypeStruct((tokens // 2, model), BF)
    return pl.pallas_call(
        functools.partial(expert_kernel, len(pieces), depth, experts),
        out_shape=(half, half, whole) * 2,
        in_specs=[pl.BlockSpec(memory_space=pltpu.SMEM)] + [vmem] * len(pieces) + [hbm] * 3,
        out_specs=(vmem,) * 6,
        scratch_shapes=[
            pltpu.VMEM((sides, tokens, model), BF),
            pltpu.VMEM((sides, tokens, LANES), F32),
            pltpu.VMEM((sides, experts * slots, tokens), BF),
            pltpu.VMEM((sides, experts * slots, 1), F32),
            pltpu.VMEM((sides, experts * slots, model), BF),
            pltpu.VMEM((depth, 2, halves, hidden, model), BF),
            pltpu.VMEM((depth, halves, hidden, model), BF),
            pltpu.VMEM((2, halves * hidden, sides * slots), BF),
            pltpu.SemaphoreType.DMA((3, depth)),
        ],
        compiler_params=pltpu.CompilerParams(vmem_limit_bytes=44 * MIB),
        cost_estimate=pl.CostEstimate(
            flops=2 * experts * sides * slots * model * (3 * halves * hidden + 2 * tokens),
            bytes_accessed=6 * rows * model * hidden + 4 * tokens * model,
            transcendentals=experts * sides * slots * halves * hidden,
        ),
        name="experts",
    )(
        first,
        *pieces,
        in_hbm(jnp.swapaxes(w_gate, 1, 2)),
        in_hbm(jnp.swapaxes(w_up, 1, 2)),
        in_hbm(w_down),
    )


def sums_back(mine, other, part):
    def add(a, *others):
        total = a.astype(F32)
        for b in others:
            total = total + b.astype(F32)
        return total.astype(BF)

    sums = [add(a, flip(b, "tp", 1)) for a, b in zip(mine, other)]
    sums[1], sums[2] = lax.optimization_barrier((sums[1], sums[2]))
    sums = [[x[at : at + part] for at in range(0, x.shape[0], part)] for x in sums]
    across = sums[2][:2] + sums[0]
    here = sums[2][2:] + sums[1]
    far_across = flip(across[2], "exp", 1)
    last_across = flip_both(across[3])
    last = flip(here[3], "ctx", 1)
    own = flip(across[0], "exp", 1)
    near = flip(here[1], "ctx", 1)
    near_across = flip_both(across[1])
    far = flip(add(here[2], last, far_across, last_across), "ctx", 2)
    total = here[0].astype(F32)
    for term in (own, near, near_across, far):
        total = total + term.astype(F32)
    return total


def on_device(
    queries, keys, values, out_weight, resid, expert_ids, router_probs, w_gate, w_up, w_down
):
    n_ctx, n_exp, n_tp = (lax.axis_size(a) for a in ("ctx", "exp", "tp"))
    part = resid.shape[0]
    rows_here = w_gate.shape[0]
    block = expert_ids.shape[0]
    cube = (n_ctx, n_exp, n_tp) == (4, 2, 2) and block == n_tp * part <= LANES
    if not cube or part % 16 or rows_here * n_ctx * n_exp != 2 * EXPERTS:
        return on_device_any_size(
            queries, keys, values, out_weight, resid, expert_ids, router_probs, w_gate, w_up, w_down
        )
    ctx, exp, tp = (lax.axis_index(a) for a in ("ctx", "exp", "tp"))
    place = jnp.stack([ctx, exp, tp]).astype(jnp.int32)
    heads_here = queries.shape[1] // HEAD_DIMENSION
    first = (ctx * n_exp + exp) * rows_here // 2
    slots = n_ctx * min(8, block)

    shared = (exp * n_tp + tp) * heads_here // (QUERY_HEADS // KEY_VALUE_HEADS)
    key_head = lax.dynamic_slice_in_dim(keys, shared * HEAD_DIMENSION, HEAD_DIMENSION, 1)
    value_head = lax.dynamic_slice_in_dim(values, shared * HEAD_DIMENSION, HEAD_DIMENSION, 1)
    kv = jnp.concatenate([key_head, value_head], axis=1)
    kv_pieces = [from_earlier(kv, "ctx", z) for z in range(1, n_ctx)]
    *own, routing = own_block(
        place, kv, expert_ids, router_probs, queries, out_weight, resid, n_exp, n_tp
    )
    base, across, other = attend_project(place, kv_pieces, own, n_exp, n_tp)

    other = flip(other, "tp", 1).astype(F32)
    across = flip((across.astype(F32) + other[part:]).astype(BF), "exp", 1)
    hidden = base + other[:part] + across.astype(F32)
    mean_square = jnp.mean(hidden * hidden, axis=1, keepdims=True)
    normed = (hidden * lax.rsqrt(mean_square + 1e-06)).astype(BF)
    normed = jnp.concatenate([normed, routing], axis=1)

    far = flip(normed, "ctx", 2)
    across = flip(normed, "exp", 1)
    near = flip(normed, "ctx", 1)
    near_across = flip_both(normed)
    far_across = flip(far, "exp", 1)
    last_across = flip_both(far)
    last = flip(far, "ctx", 1)
    pieces = [normed, near, far, last, across, near_across, far_across, last_across]
    pieces += [flip(piece, "tp", 1) for piece in pieces]
    sums = cube_experts(
        first.astype(jnp.int32).reshape(1), pieces, w_gate, w_up, w_down, slots
    )
    return (hidden + sums_back(sums[:3], sums[3:], part)).astype(BF)


def solution(mesh):
    in_specs = (
        P(("groups", "ctx"), ("exp", "tp")),
        P(("groups", "ctx"), None),
        P(("groups", "ctx"), None),
        P(("exp", "tp"), None),
        P(("groups", "ctx", "exp", "tp"), None),
        P(("groups", "ctx", "exp"), None),
        P(("groups", "ctx", "exp"), None),
        P(("ctx", "exp"), None, "tp"),
        P(("ctx", "exp"), None, "tp"),
        P(("ctx", "exp"), "tp", None),
    )
    out_specs = P(("groups", "ctx", "exp", "tp"), None)
    return jax.shard_map(
        on_device, mesh=mesh, in_specs=in_specs, out_specs=out_specs, check_vma=False
    )
```

```python
import functools
import math

import jax
import jax.numpy as jnp
from jax import lax
from jax.experimental import pallas as pl
from jax.experimental.pallas import tpu as pltpu
from jax.sharding import PartitionSpec as P

HEAD_DIMENSION = 128
QUERY_HEADS = 32
KEY_VALUE_HEADS = 4
EXPERTS = 64
TOPK = 8
MIB = 1 << 20
LANES = 128
BF = jnp.bfloat16
F32 = jnp.float32


def attend_blocks(blocks, key_head, value_head, heads_here):
    score_scale = 1.0 / math.sqrt(HEAD_DIMENSION)

    def make_state(query_rows):
        row_total = query_rows.shape[0]
        return (
            jnp.full((row_total, heads_here), -1e30, jnp.float32),
            jnp.zeros((row_total, heads_here), jnp.float32),
            jnp.zeros((row_total, heads_here, HEAD_DIMENSION), jnp.float32),
        )

    initial = tuple((make_state(query_rows) for query_rows, query_places in blocks))

    def fold_keys(carry, piece, first):
        key_piece, value_piece = piece
        key_places = jnp.arange(key_piece.shape[0], dtype=jnp.int32)
        updated = []
        for (query_rows, query_places), state in zip(blocks, carry):

            def refresh(state, query_rows=query_rows, query_places=query_places):
                running_max, running_sum, accum = state
                shaped = query_rows.reshape(query_rows.shape[0], heads_here, HEAD_DIMENSION)
                scores = (
                    jnp.einsum("qhd,kd->qhk", shaped, key_piece, preferred_element_type=jnp.float32)
                    * score_scale
                )
                allowed = key_places[None, None, :] <= query_places[:, None, None]
                scores = jnp.where(allowed, scores, -1e30)
                new_max = jnp.maximum(running_max, jnp.max(scores, axis=2))
                weights = jnp.where(allowed, jnp.exp(scores - new_max[:, :, None]), 0.0)
                running_sum = jnp.sum(weights, axis=2)
                accum = jnp.einsum(
                    "qhk,kd->qhd",
                    weights,
                    value_piece.astype(jnp.float32),
                    precision=lax.Precision.HIGHEST,
                )
                return (new_max, running_sum, accum)

            needed = first <= query_places[-1]
            updated.append(lax.cond(needed, refresh, lambda state: state, state))
        return tuple(updated)

    final = fold_keys(
        initial,
        (
            lax.all_gather(key_head, "ctx", axis=0, tiled=True),
            lax.all_gather(value_head, "ctx", axis=0, tiled=True),
        ),
        jnp.int32(0),
    )
    results = []
    for (query_rows, query_places), state in zip(blocks, final):
        running_max, running_sum, accum = state
        results.append(
            (accum / running_sum[:, :, None])
            .reshape(query_rows.shape[0], heads_here * HEAD_DIMENSION)
            .astype(jnp.bfloat16)
        )
    return results


def run_experts(inputs, w_gate, w_up, w_down):
    gate_out = jnp.einsum("rnd,rdf->rnf", inputs, w_gate, preferred_element_type=jnp.float32)
    up_out = jnp.einsum("rnd,rdf->rnf", inputs, w_up, preferred_element_type=jnp.float32)
    activated = (jax.nn.silu(gate_out) * up_out).astype(jnp.bfloat16)
    return jnp.einsum("rnf,rfd->rnd", activated, w_down, preferred_element_type=jnp.float32).astype(
        jnp.bfloat16
    )


def on_device_any_size(
    queries, keys, values, out_weight, resid, expert_ids, router_probs, w_gate, w_up, w_down
):
    rows_ctx = queries.shape[0]
    heads_here = queries.shape[1] // HEAD_DIMENSION
    group_width = QUERY_HEADS // KEY_VALUE_HEADS
    head_rank = lax.axis_index(("exp", "tp"))
    shared = head_rank * heads_here // group_width
    key_head = lax.dynamic_slice_in_dim(keys, shared * HEAD_DIMENSION, HEAD_DIMENSION, 1)
    value_head = lax.dynamic_slice_in_dim(values, shared * HEAD_DIMENSION, HEAD_DIMENSION, 1)
    cycle_rank = lax.axis_index("ctx")
    own_places = cycle_rank * rows_ctx + jnp.arange(rows_ctx, dtype=jnp.int32)
    attended = attend_blocks([(queries, own_places)], key_head, value_head, heads_here)[0]
    projected = lax.psum_scatter(
        jnp.dot(attended, out_weight, preferred_element_type=jnp.float32).astype(jnp.bfloat16),
        ("exp", "tp"),
        scatter_dimension=0,
        tiled=True,
    ).astype(jnp.float32)
    hidden = resid.astype(jnp.float32) + projected
    mean_square = jnp.mean(hidden * hidden, axis=1, keepdims=True)
    normed = (hidden * lax.rsqrt(mean_square + 1e-06)).astype(jnp.bfloat16)
    pair_rows = lax.all_gather(normed, "tp", axis=0, tiled=True)
    slot_count = min(8, expert_ids.shape[0])
    gate_weights = router_probs / jnp.sum(router_probs, axis=1, keepdims=True)
    flat_ids = expert_ids.reshape(-1)
    assigned = flat_ids.shape[0]
    onehot = (flat_ids[:, None] == jnp.arange(EXPERTS, dtype=jnp.int32)[None, :]).astype(jnp.int32)
    slots = jnp.sum(onehot * (jnp.cumsum(onehot, axis=0) - 1), axis=1)
    token_of = jnp.arange(assigned, dtype=jnp.int32) // TOPK
    peer_count = lax.axis_size(("ctx", "exp"))
    rows_here = w_gate.shape[0]
    cell_parts = []
    for half_index in range(2):
        half_rows_id = 2 * flat_ids + half_index
        target = half_rows_id // rows_here
        local_row = half_rows_id % rows_here
        cell_parts.append((local_row * slot_count + slots) * peer_count + target)
    cells = jnp.concatenate(cell_parts)
    table = (
        jnp.full((rows_here * slot_count * peer_count,), -1, jnp.int32)
        .at[cells]
        .set(jnp.concatenate([token_of, token_of]))
    )
    send_buffer = jnp.where(
        table[:, None] >= 0, pair_rows[jnp.maximum(table, 0)], jnp.zeros((), jnp.bfloat16)
    )
    model_width = pair_rows.shape[1]
    received = lax.all_to_all(
        send_buffer.reshape(rows_here * slot_count, peer_count, model_width),
        ("ctx", "exp"),
        split_axis=1,
        concat_axis=1,
        tiled=True,
    )
    expert_out = run_experts(
        received.reshape(rows_here, slot_count * peer_count, model_width), w_gate, w_up, w_down
    )
    returned = lax.all_to_all(
        expert_out.reshape(rows_here * slot_count, peer_count, model_width),
        ("ctx", "exp"),
        split_axis=1,
        concat_axis=1,
        tiled=True,
    )
    returned_flat = returned.reshape(rows_here * slot_count * peer_count, model_width)
    gathered = returned_flat[cells].reshape(2, expert_ids.shape[0], TOPK, model_width)
    routed_part = jnp.einsum(
        "hakd,ak->ad", gathered.astype(jnp.float32), gate_weights, precision=lax.Precision.HIGHEST
    )
    routed = lax.psum_scatter(
        routed_part.astype(jnp.bfloat16), "tp", scatter_dimension=0, tiled=True
    ).astype(jnp.float32)
    return (hidden + routed).astype(jnp.bfloat16)


def flip(x, axis, bit):
    return lax.ppermute(x, axis, [(i, i ^ bit) for i in range(lax.axis_size(axis))])


def flip_both(x):
    n_exp = lax.axis_size("exp")
    mask = n_exp + 1
    size = lax.axis_size("ctx") * n_exp
    return lax.ppermute(x, ("ctx", "exp"), [(i, i ^ mask) for i in range(size)])


def from_earlier(x, axis, steps):
    size = lax.axis_size(axis)
    return lax.ppermute(x, axis, [(i, i + steps) for i in range(size - steps)])


def in_hbm(x):
    return pltpu.with_memory_space_constraint(x, pltpu.HBM)


def dot_rows(a, b):
    return lax.dot_general(a, b, (((1,), (1,)), ((), ())), preferred_element_type=F32)


def own_block_kernel(sizes, place, kv_ref, ids_hbm, probs_hbm, q_hbm, w_hbm, resid_hbm, *refs):
    n_exp, n_tp, heads, part = sizes
    rows = n_exp * n_tp * part
    q_ref, w_ref, resid_ref, out_ref, sum_ref, max_ref, routing_ref = refs[:7]
    v_ext, ids_ref, probs_ref, packed, q_sem, sems = refs[7:]
    fetch = [
        pltpu.make_async_copy(ids_hbm, ids_ref, sems.at[0]),
        pltpu.make_async_copy(probs_hbm, probs_ref, sems.at[1]),
        pltpu.make_async_copy(resid_hbm, resid_ref, sems.at[2]),
        pltpu.make_async_copy(w_hbm, w_ref, sems.at[3]),
    ]
    fetch_q = pltpu.make_async_copy(q_hbm, q_ref, q_sem)
    fetch_q.start()
    for copy in fetch:
        copy.start()
    tp = place[2]
    v_ext[:, :HEAD_DIMENSION] = kv_ref[:, HEAD_DIMENSION:]
    v_ext[:, HEAD_DIMENSION:] = jnp.ones((rows, HEAD_DIMENSION), BF)
    keys = kv_ref[:, :HEAD_DIMENSION]
    allowed = lax.broadcasted_iota(jnp.int32, (rows, rows), 1) <= lax.broadcasted_iota(
        jnp.int32, (rows, rows), 0
    )
    scale = 1.0 / math.sqrt(HEAD_DIMENSION)
    fetch_q.wait()
    for h in range(heads):
        columns = slice(h * HEAD_DIMENSION, (h + 1) * HEAD_DIMENSION)
        s = jnp.where(allowed, dot_rows(q_ref[:, columns], keys) * scale, -1e30)
        top = jnp.max(s, axis=1, keepdims=True)
        out = jnp.dot(jnp.exp(s - top).astype(BF), v_ext[...], preferred_element_type=F32)
        out_ref[:, columns] = out[:, :HEAD_DIMENSION]
        sum_ref[:, columns] = out[:, HEAD_DIMENSION:]
        max_ref[:, h : h + 1] = top

    fetch[0].wait()
    fetch[1].wait()
    block = n_tp * part
    ids = ids_ref[...]
    probs = probs_ref[...]
    expert = lax.broadcasted_iota(jnp.int32, (EXPERTS, block), 0)
    named = jnp.zeros((EXPERTS, block), F32)
    for k in range(TOPK):
        named = named + jnp.where(expert == ids[k : k + 1, :], 1.0, 0.0)
    before = lax.broadcasted_iota(jnp.int32, (block, block), 0) < lax.broadcasted_iota(
        jnp.int32, (block, block), 1
    )
    count = jnp.dot(
        named.astype(BF), jnp.where(before, 1.0, 0.0).astype(BF), preferred_element_type=F32
    )
    ranks = [
        jnp.sum(jnp.where(expert == ids[k : k + 1, :], count, 0.0), axis=0, keepdims=True)
        for k in range(TOPK)
    ]
    gates = probs / jnp.sum(probs, axis=0, keepdims=True)
    high = gates.astype(BF).astype(F32)
    fields = jnp.concatenate([ids.astype(F32)] + ranks + [high, gates - high], axis=0)
    packed[...] = jnp.zeros_like(packed)
    packed[: 4 * TOPK, :block] = fields
    packed[...] = packed[...].T
    routing_ref[...] = packed[pl.ds(pl.multiple_of(tp * part, part), part), :].astype(BF)
    fetch[2].wait()
    fetch[3].wait()


def own_block(place, kv, expert_ids, router_probs, queries, out_weight, resid, n_exp, n_tp):
    rows, width = queries.shape
    heads = width // HEAD_DIMENSION
    part, model = resid.shape
    block = expert_ids.shape[0]
    vmem = pl.BlockSpec(memory_space=pltpu.VMEM)
    hbm = pl.BlockSpec(memory_space=pltpu.HBM)
    return pl.pallas_call(
        functools.partial(own_block_kernel, (n_exp, n_tp, heads, part)),
        out_shape=(
            jax.ShapeDtypeStruct((rows, width), BF),
            jax.ShapeDtypeStruct((width, model), BF),
            jax.ShapeDtypeStruct((part, model), BF),
            jax.ShapeDtypeStruct((rows, width), F32),
            jax.ShapeDtypeStruct((rows, width), F32),
            jax.ShapeDtypeStruct((rows, LANES), F32),
            jax.ShapeDtypeStruct((part, LANES), BF),
        ),
        in_specs=[pl.BlockSpec(memory_space=pltpu.SMEM), vmem] + [hbm] * 5,
        out_specs=(vmem,) * 7,
        scratch_shapes=[
            pltpu.VMEM((rows, 2 * HEAD_DIMENSION), BF),
            pltpu.VMEM((TOPK, block), jnp.int32),
            pltpu.VMEM((TOPK, block), F32),
            pltpu.VMEM((LANES, LANES), F32),
            pltpu.SemaphoreType.DMA,
            pltpu.SemaphoreType.DMA((4,)),
        ],
        compiler_params=pltpu.CompilerParams(vmem_limit_bytes=20 * MIB),
        cost_estimate=pl.CostEstimate(
            flops=6 * rows * width * rows,
            bytes_accessed=2 * (rows * width + width * model + rows * model),
            transcendentals=rows * rows * heads,
        ),
        name="own_block",
    )(place, kv, *map(in_hbm, (expert_ids.T, router_probs.T, queries, out_weight, resid)))


def dot_columns(a, b):
    return lax.dot_general(a, b, (((0,), (0,)), ((), ())), preferred_element_type=F32)


def attention_kernel(sizes, place, *refs):
    n_ctx, n_exp, n_tp, heads, part = sizes
    rows = n_exp * n_tp * part
    kv_refs, refs = refs[: n_ctx - 1], refs[n_ctx - 1 :]
    q_ref, w_ref, resid_ref, out_ref, sum_ref, max_ref = refs[:6]
    base_ref, across_ref, other_ref = refs[6:9]
    k_all, v_all, att, att_rel = refs[9:]
    ctx, exp, tp = place[0], place[1], place[2]
    for z in range(n_ctx - 1):
        k_all[z * rows : (z + 1) * rows, :] = kv_refs[z][:, :HEAD_DIMENSION]
        v_all[z * rows : (z + 1) * rows, :HEAD_DIMENSION] = kv_refs[z][:, HEAD_DIMENSION:]
    v_all[:, HEAD_DIMENSION:] = jnp.ones(((n_ctx - 1) * rows, HEAD_DIMENSION), BF)
    column = lax.broadcasted_iota(jnp.int32, (1, (n_ctx - 1) * rows), 1)
    allowed = column >= (n_ctx - 1 - ctx) * rows
    scale = 1.0 / math.sqrt(HEAD_DIMENSION)
    for h in range(heads):
        columns = slice(h * HEAD_DIMENSION, (h + 1) * HEAD_DIMENSION)
        s = jnp.where(allowed, dot_rows(q_ref[:, columns], k_all[...]) * scale, -1e30)
        own_top = max_ref[:, h : h + 1]
        top = jnp.maximum(own_top, jnp.max(s, axis=1, keepdims=True))
        keep = jnp.exp(own_top - top)
        out = jnp.dot(jnp.exp(s - top).astype(BF), v_all[...], preferred_element_type=F32)
        total = sum_ref[:, columns] * keep + out[:, HEAD_DIMENSION:]
        out = out_ref[:, columns] * keep + out[:, :HEAD_DIMENSION]
        att[:, columns] = (out / total).astype(BF)
    for t in range(n_tp):
        for x in range(n_exp):
            owner = lax.rem(exp + x, n_exp) * n_tp + lax.rem(tp + t, n_tp)
            source = pl.ds(pl.multiple_of(owner * part, part), part)
            at = (t * n_exp + x) * part
            att_rel[at : at + part, :] = att[source, :]
    projected = jnp.dot(att_rel[...], w_ref[...], preferred_element_type=F32)
    base_ref[...] = resid_ref[...].astype(F32) + projected[:part]
    across_ref[...] = projected[part : 2 * part].astype(BF)
    other_ref[...] = projected[2 * part :].astype(BF)


def attend_project(place, pieces, own, n_exp, n_tp):
    queries, out_weight, resid = own[:3]
    rows, width = queries.shape
    n_ctx, heads = len(pieces) + 1, width // HEAD_DIMENSION
    part, model = resid.shape
    vmem = pl.BlockSpec(memory_space=pltpu.VMEM)
    return pl.pallas_call(
        functools.partial(attention_kernel, (n_ctx, n_exp, n_tp, heads, part)),
        out_shape=(
            jax.ShapeDtypeStruct((part, model), F32),
            jax.ShapeDtypeStruct((part, model), BF),
            jax.ShapeDtypeStruct((2 * part, model), BF),
        ),
        in_specs=[pl.BlockSpec(memory_space=pltpu.SMEM)] + [vmem] * (n_ctx - 1 + len(own)),
        out_specs=(vmem,) * 3,
        scratch_shapes=[
            pltpu.VMEM(((n_ctx - 1) * rows, HEAD_DIMENSION), BF),
            pltpu.VMEM(((n_ctx - 1) * rows, 2 * HEAD_DIMENSION), BF),
            pltpu.VMEM((rows, width), BF),
            pltpu.VMEM((rows, width), BF),
        ],
        compiler_params=pltpu.CompilerParams(vmem_limit_bytes=20 * MIB),
        cost_estimate=pl.CostEstimate(
            flops=2 * rows * width * (3 * (n_ctx - 1) * rows + model),
            bytes_accessed=2 * (rows * width + width * model + rows * model),
            transcendentals=rows * n_ctx * rows * heads,
        ),
        name="attend_project",
    )(place, *pieces, *own)


def expert_kernel(n_pieces, depth, experts, first_ref, *refs):
    pieces, (wg_hbm, wu_hbm, wd_hbm) = refs[:n_pieces], refs[n_pieces : n_pieces + 3]
    outs = refs[n_pieces + 3 : n_pieces + 9]
    x_all, packed, pick_all, scale_all, out_all, wgu, wd, act, sems = refs[n_pieces + 9 :]
    sides, tokens, model = x_all.shape
    slots = pick_all.shape[1] // experts
    _, _, halves, hidden, _ = wgu.shape
    blocks = n_pieces // (2 * sides)
    part = tokens // (2 * blocks)

    def gate_up_copies(e):
        slot, rows = lax.rem(e, depth), pl.ds(e * halves, halves)
        return (
            pltpu.make_async_copy(wg_hbm.at[rows], wgu.at[slot, 0], sems.at[0, slot]),
            pltpu.make_async_copy(wu_hbm.at[rows], wgu.at[slot, 1], sems.at[1, slot]),
        )

    def down_copies(e):
        slot, rows = lax.rem(e, depth), pl.ds(e * halves, halves)
        return (pltpu.make_async_copy(wd_hbm.at[rows], wd.at[slot], sems.at[2, slot]),)

    def start(copies):
        for copy in copies:
            copy.start()

    def wait(copies):
        for copy in copies:
            copy.wait()

    def of_expert(e):
        return pl.ds(pl.multiple_of(e * slots, slots), slots)

    def gate_up(e):
        x = jnp.concatenate([out_all[side, of_expert(e), :] for side in range(sides)])
        weight = wgu[lax.rem(e, depth)].reshape(2 * halves * hidden, model)
        both = dot_rows(weight, x)
        gate, up = both[: halves * hidden], both[halves * hidden :]
        return (gate * jax.nn.sigmoid(gate) * up).astype(BF)

    def down(e):
        weight = wd[lax.rem(e, depth)].reshape(halves * hidden, model)
        out = dot_columns(act[lax.rem(e, 2)], weight)
        scale = jnp.concatenate([scale_all[side, of_expert(e), :] for side in range(sides)])
        return (out * scale).astype(BF)

    def keep(e, out):
        for side in range(sides):
            out_all[side, of_expert(e), :] = out[side * slots : (side + 1) * slots]

    for e in range(depth - 1):
        start(gate_up_copies(e))
        if e:
            start(down_copies(e - 1))
    for i, piece in enumerate(pieces):
        core, side, block = i // (sides * blocks), i // blocks % sides, i % blocks
        rows = slice((core * blocks + block) * part, (core * blocks + block + 1) * part)
        x_all[side, rows, :] = piece[:, :model]
        packed[side, rows, :] = piece[:, model:].astype(F32)
    slot = lax.broadcasted_iota(jnp.int32, (slots, tokens), 0)
    token = lax.broadcasted_iota(jnp.int32, (TOPK, tokens), 1)
    offset = lax.rem(token // part, blocks) * (slots // blocks)
    for side in range(sides):
        fields = packed[side].T
        ids, ranks = fields[:TOPK].astype(jnp.int32), fields[TOPK : 2 * TOPK]
        gates = fields[2 * TOPK : 3 * TOPK] + fields[3 * TOPK : 4 * TOPK]
        places = ranks.astype(jnp.int32) + offset
        for e in range(experts):
            hit = ids == first_ref[0] + e
            chosen = slot == jnp.max(jnp.where(hit, places, -1), axis=0, keepdims=True)
            gate = jnp.sum(jnp.where(hit, gates, 0.0), axis=0, keepdims=True)
            here = slice(e * slots, (e + 1) * slots)
            pick_all[side, here, :] = jnp.where(chosen, 1.0, 0.0).astype(BF)
            scale_all[side, here, :] = jnp.sum(
                jnp.where(chosen, gate, 0.0), axis=1, keepdims=True
            )
        out_all[side] = jnp.dot(
            pick_all[side], x_all[side], preferred_element_type=F32
        ).astype(BF)
    wait(gate_up_copies(0))
    act[0] = gate_up(0)

    @pl.loop(0, experts - 1)
    def _(e):
        @pl.when(e + depth - 1 < experts)
        def _():
            start(gate_up_copies(e + depth - 1))

        @pl.when(e + depth - 2 < experts)
        def _():
            start(down_copies(e + depth - 2))

        wait(down_copies(e))
        wait(gate_up_copies(e + 1))
        following = gate_up(e + 1)
        out = down(e)
        act[lax.rem(e + 1, 2)] = following
        keep(e, out)

    wait(down_copies(experts - 1))
    keep(experts - 1, down(experts - 1))
    half = blocks * part // 2
    for side in (1, 0):
        routed = dot_columns(pick_all[side], out_all[side]).astype(BF)
        for core in range(2):
            near, far = routed[2 * core * half :][:half], routed[(2 * core + 1) * half :][:half]
            outs[3 * core + 1 - side][...] = far
            outs[3 * core + 2][(1 - side) * half : (2 - side) * half, :] = near


def cube_experts(first, pieces, w_gate, w_up, w_down, slots):
    rows, hidden, model = w_down.shape
    halves, sides = 2, 2
    experts = rows // halves
    tokens = len(pieces) * pieces[0].shape[0] // sides
    depth = 4
    vmem = pl.BlockSpec(memory_space=pltpu.VMEM)
    hbm = pl.BlockSpec(memory_space=pltpu.HBM)

    half = jax.ShapeDtypeStruct((tokens // 4, model), BF)
    whole = jax.ShapeDtypeStruct((tokens // 2, model), BF)
    return pl.pallas_call(
        functools.partial(expert_kernel, len(pieces), depth, experts),
        out_shape=(half, half, whole) * 2,
        in_specs=[pl.BlockSpec(memory_space=pltpu.SMEM)] + [vmem] * len(pieces) + [hbm] * 3,
        out_specs=(vmem,) * 6,
        scratch_shapes=[
            pltpu.VMEM((sides, tokens, model), BF),
            pltpu.VMEM((sides, tokens, LANES), F32),
            pltpu.VMEM((sides, experts * slots, tokens), BF),
            pltpu.VMEM((sides, experts * slots, 1), F32),
            pltpu.VMEM((sides, experts * slots, model), BF),
            pltpu.VMEM((depth, 2, halves, hidden, model), BF),
            pltpu.VMEM((depth, halves, hidden, model), BF),
            pltpu.VMEM((2, halves * hidden, sides * slots), BF),
            pltpu.SemaphoreType.DMA((3, depth)),
        ],
        compiler_params=pltpu.CompilerParams(vmem_limit_bytes=44 * MIB),
        cost_estimate=pl.CostEstimate(
            flops=2 * experts * sides * slots * model * (3 * halves * hidden + 2 * tokens),
            bytes_accessed=6 * rows * model * hidden + 4 * tokens * model,
            transcendentals=experts * sides * slots * halves * hidden,
        ),
        name="experts",
    )(
        first,
        *pieces,
        in_hbm(jnp.swapaxes(w_gate, 1, 2)),
        in_hbm(jnp.swapaxes(w_up, 1, 2)),
        in_hbm(w_down),
    )


def sums_back(mine, other, part):
    def add(a, *others):
        total = a.astype(F32)
        for b in others:
            total = total + b.astype(F32)
        return total.astype(BF)

    sums = [add(a, flip(b, "tp", 1)) for a, b in zip(mine, other)]
    sums[1], sums[2] = lax.optimization_barrier((sums[1], sums[2]))
    sums = [[x[at : at + part] for at in range(0, x.shape[0], part)] for x in sums]
    across = sums[2][:2] + sums[0]
    here = sums[2][2:] + sums[1]
    far_across = flip(across[2], "exp", 1)
    last_across = flip_both(across[3])
    last = flip(here[3], "ctx", 1)
    own = flip(across[0], "exp", 1)
    near = flip(here[1], "ctx", 1)
    near_across = flip_both(across[1])
    far = flip(add(here[2], last, far_across, last_across), "ctx", 2)
    total = here[0].astype(F32)
    for term in (own, near, near_across, far):
        total = total + term.astype(F32)
    return total


def on_device(
    queries, keys, values, out_weight, resid, expert_ids, router_probs, w_gate, w_up, w_down
):
    n_ctx, n_exp, n_tp = (lax.axis_size(a) for a in ("ctx", "exp", "tp"))
    part = resid.shape[0]
    rows_here = w_gate.shape[0]
    block = expert_ids.shape[0]
    cube = (n_ctx, n_exp, n_tp) == (4, 2, 2) and block == n_tp * part <= LANES
    if not cube or part % 16 or rows_here * n_ctx * n_exp != 2 * EXPERTS:
        return on_device_any_size(
            queries, keys, values, out_weight, resid, expert_ids, router_probs, w_gate, w_up, w_down
        )
    ctx, exp, tp = (lax.axis_index(a) for a in ("ctx", "exp", "tp"))
    place = jnp.stack([ctx, exp, tp]).astype(jnp.int32)
    heads_here = queries.shape[1] // HEAD_DIMENSION
    first = (ctx * n_exp + exp) * rows_here // 2
    slots = n_ctx * min(8, block)

    shared = (exp * n_tp + tp) * heads_here // (QUERY_HEADS // KEY_VALUE_HEADS)
    key_head = lax.dynamic_slice_in_dim(keys, shared * HEAD_DIMENSION, HEAD_DIMENSION, 1)
    value_head = lax.dynamic_slice_in_dim(values, shared * HEAD_DIMENSION, HEAD_DIMENSION, 1)
    kv = jnp.concatenate([key_head, value_head], axis=1)
    kv_pieces = [from_earlier(kv, "ctx", z) for z in range(n_ctx - 1, 0, -1)]
    *own, routing = own_block(
        place, kv, expert_ids, router_probs, queries, out_weight, resid, n_exp, n_tp
    )
    base, across, other = attend_project(place, kv_pieces, own, n_exp, n_tp)

    other = flip(other, "tp", 1).astype(F32)
    across = flip((across.astype(F32) + other[part:]).astype(BF), "exp", 1)
    hidden = base + other[:part] + across.astype(F32)
    mean_square = jnp.mean(hidden * hidden, axis=1, keepdims=True)
    normed = (hidden * lax.rsqrt(mean_square + 1e-06)).astype(BF)
    normed = jnp.concatenate([normed, routing], axis=1)

    far = flip(normed, "ctx", 2)
    across = flip(normed, "exp", 1)
    near = flip(normed, "ctx", 1)
    near_across = flip_both(normed)
    far_across = flip(far, "exp", 1)
    last_across = flip_both(far)
    last = flip(far, "ctx", 1)
    early = lax.optimization_barrier((normed, near, far, across, near_across))
    pieces = [normed, near, far, last, across, near_across, far_across, last_across]
    pieces += [flip(piece, "tp", 1) for piece in early[:3] + (last,)]
    pieces += [flip(piece, "tp", 1) for piece in early[3:] + (far_across, last_across)]
    sums = cube_experts(
        first.astype(jnp.int32).reshape(1), pieces, w_gate, w_up, w_down, slots
    )
    return (hidden + sums_back(sums[:3], sums[3:], part)).astype(BF)


def solution(mesh):
    in_specs = (
        P(("groups", "ctx"), ("exp", "tp")),
        P(("groups", "ctx"), None),
        P(("groups", "ctx"), None),
        P(("exp", "tp"), None),
        P(("groups", "ctx", "exp", "tp"), None),
        P(("groups", "ctx", "exp"), None),
        P(("groups", "ctx", "exp"), None),
        P(("ctx", "exp"), None, "tp"),
        P(("ctx", "exp"), None, "tp"),
        P(("ctx", "exp"), "tp", None),
    )
    out_specs = P(("groups", "ctx", "exp", "tp"), None)
    return jax.shard_map(
        on_device, mesh=mesh, in_specs=in_specs, out_specs=out_specs, check_vma=False
    )
```

```python
import functools
import math

import jax
import jax.numpy as jnp
from jax import lax
from jax.experimental import pallas as pl
from jax.experimental.pallas import tpu as pltpu
from jax.sharding import PartitionSpec as P

HEAD_DIMENSION = 128
QUERY_HEADS = 32
KEY_VALUE_HEADS = 4
EXPERTS = 64
TOPK = 8
MIB = 1 << 20
LANES = 128
BF = jnp.bfloat16
F32 = jnp.float32


def attend_blocks(blocks, key_head, value_head, heads_here):
    score_scale = 1.0 / math.sqrt(HEAD_DIMENSION)

    def make_state(query_rows):
        row_total = query_rows.shape[0]
        return (
            jnp.full((row_total, heads_here), -1e30, jnp.float32),
            jnp.zeros((row_total, heads_here), jnp.float32),
            jnp.zeros((row_total, heads_here, HEAD_DIMENSION), jnp.float32),
        )

    initial = tuple((make_state(query_rows) for query_rows, query_places in blocks))

    def fold_keys(carry, piece, first):
        key_piece, value_piece = piece
        key_places = jnp.arange(key_piece.shape[0], dtype=jnp.int32)
        updated = []
        for (query_rows, query_places), state in zip(blocks, carry):

            def refresh(state, query_rows=query_rows, query_places=query_places):
                running_max, running_sum, accum = state
                shaped = query_rows.reshape(query_rows.shape[0], heads_here, HEAD_DIMENSION)
                scores = (
                    jnp.einsum("qhd,kd->qhk", shaped, key_piece, preferred_element_type=jnp.float32)
                    * score_scale
                )
                allowed = key_places[None, None, :] <= query_places[:, None, None]
                scores = jnp.where(allowed, scores, -1e30)
                new_max = jnp.maximum(running_max, jnp.max(scores, axis=2))
                weights = jnp.where(allowed, jnp.exp(scores - new_max[:, :, None]), 0.0)
                running_sum = jnp.sum(weights, axis=2)
                accum = jnp.einsum(
                    "qhk,kd->qhd",
                    weights,
                    value_piece.astype(jnp.float32),
                    precision=lax.Precision.HIGHEST,
                )
                return (new_max, running_sum, accum)

            needed = first <= query_places[-1]
            updated.append(lax.cond(needed, refresh, lambda state: state, state))
        return tuple(updated)

    final = fold_keys(
        initial,
        (
            lax.all_gather(key_head, "ctx", axis=0, tiled=True),
            lax.all_gather(value_head, "ctx", axis=0, tiled=True),
        ),
        jnp.int32(0),
    )
    results = []
    for (query_rows, query_places), state in zip(blocks, final):
        running_max, running_sum, accum = state
        results.append(
            (accum / running_sum[:, :, None])
            .reshape(query_rows.shape[0], heads_here * HEAD_DIMENSION)
            .astype(jnp.bfloat16)
        )
    return results


def run_experts(inputs, w_gate, w_up, w_down):
    gate_out = jnp.einsum("rnd,rdf->rnf", inputs, w_gate, preferred_element_type=jnp.float32)
    up_out = jnp.einsum("rnd,rdf->rnf", inputs, w_up, preferred_element_type=jnp.float32)
    activated = (jax.nn.silu(gate_out) * up_out).astype(jnp.bfloat16)
    return jnp.einsum("rnf,rfd->rnd", activated, w_down, preferred_element_type=jnp.float32).astype(
        jnp.bfloat16
    )


def on_device_any_size(
    queries, keys, values, out_weight, resid, expert_ids, router_probs, w_gate, w_up, w_down
):
    rows_ctx = queries.shape[0]
    heads_here = queries.shape[1] // HEAD_DIMENSION
    group_width = QUERY_HEADS // KEY_VALUE_HEADS
    head_rank = lax.axis_index(("exp", "tp"))
    shared = head_rank * heads_here // group_width
    key_head = lax.dynamic_slice_in_dim(keys, shared * HEAD_DIMENSION, HEAD_DIMENSION, 1)
    value_head = lax.dynamic_slice_in_dim(values, shared * HEAD_DIMENSION, HEAD_DIMENSION, 1)
    cycle_rank = lax.axis_index("ctx")
    own_places = cycle_rank * rows_ctx + jnp.arange(rows_ctx, dtype=jnp.int32)
    attended = attend_blocks([(queries, own_places)], key_head, value_head, heads_here)[0]
    projected = lax.psum_scatter(
        jnp.dot(attended, out_weight, preferred_element_type=jnp.float32).astype(jnp.bfloat16),
        ("exp", "tp"),
        scatter_dimension=0,
        tiled=True,
    ).astype(jnp.float32)
    hidden = resid.astype(jnp.float32) + projected
    mean_square = jnp.mean(hidden * hidden, axis=1, keepdims=True)
    normed = (hidden * lax.rsqrt(mean_square + 1e-06)).astype(jnp.bfloat16)
    pair_rows = lax.all_gather(normed, "tp", axis=0, tiled=True)
    slot_count = min(8, expert_ids.shape[0])
    gate_weights = router_probs / jnp.sum(router_probs, axis=1, keepdims=True)
    flat_ids = expert_ids.reshape(-1)
    assigned = flat_ids.shape[0]
    onehot = (flat_ids[:, None] == jnp.arange(EXPERTS, dtype=jnp.int32)[None, :]).astype(jnp.int32)
    slots = jnp.sum(onehot * (jnp.cumsum(onehot, axis=0) - 1), axis=1)
    token_of = jnp.arange(assigned, dtype=jnp.int32) // TOPK
    peer_count = lax.axis_size(("ctx", "exp"))
    rows_here = w_gate.shape[0]
    cell_parts = []
    for half_index in range(2):
        half_rows_id = 2 * flat_ids + half_index
        target = half_rows_id // rows_here
        local_row = half_rows_id % rows_here
        cell_parts.append((local_row * slot_count + slots) * peer_count + target)
    cells = jnp.concatenate(cell_parts)
    table = (
        jnp.full((rows_here * slot_count * peer_count,), -1, jnp.int32)
        .at[cells]
        .set(jnp.concatenate([token_of, token_of]))
    )
    send_buffer = jnp.where(
        table[:, None] >= 0, pair_rows[jnp.maximum(table, 0)], jnp.zeros((), jnp.bfloat16)
    )
    model_width = pair_rows.shape[1]
    received = lax.all_to_all(
        send_buffer.reshape(rows_here * slot_count, peer_count, model_width),
        ("ctx", "exp"),
        split_axis=1,
        concat_axis=1,
        tiled=True,
    )
    expert_out = run_experts(
        received.reshape(rows_here, slot_count * peer_count, model_width), w_gate, w_up, w_down
    )
    returned = lax.all_to_all(
        expert_out.reshape(rows_here * slot_count, peer_count, model_width),
        ("ctx", "exp"),
        split_axis=1,
        concat_axis=1,
        tiled=True,
    )
    returned_flat = returned.reshape(rows_here * slot_count * peer_count, model_width)
    gathered = returned_flat[cells].reshape(2, expert_ids.shape[0], TOPK, model_width)
    routed_part = jnp.einsum(
        "hakd,ak->ad", gathered.astype(jnp.float32), gate_weights, precision=lax.Precision.HIGHEST
    )
    routed = lax.psum_scatter(
        routed_part.astype(jnp.bfloat16), "tp", scatter_dimension=0, tiled=True
    ).astype(jnp.float32)
    return (hidden + routed).astype(jnp.bfloat16)


def flip(x, axis, bit):
    return lax.ppermute(x, axis, [(i, i ^ bit) for i in range(lax.axis_size(axis))])


def flip_both(x):
    n_exp = lax.axis_size("exp")
    mask = n_exp + 1
    size = lax.axis_size("ctx") * n_exp
    return lax.ppermute(x, ("ctx", "exp"), [(i, i ^ mask) for i in range(size)])


def from_earlier(x, axis, bits):
    return lax.ppermute(x, axis, [(i, i ^ bits) for i in range(lax.axis_size(axis)) if i < i ^ bits])


def in_hbm(x):
    return pltpu.with_memory_space_constraint(x, pltpu.HBM)


def dot_rows(a, b):
    return lax.dot_general(a, b, (((1,), (1,)), ((), ())), preferred_element_type=F32)


KV_ORDER = (1, 2, 3)


def own_block_kernel(sizes, place, kv_ref, ids_hbm, probs_hbm, q_hbm, w_hbm, resid_hbm, *refs):
    n_exp, n_tp, heads, part = sizes
    rows = n_exp * n_tp * part
    q_ref, w_ref, resid_ref, out_ref, sum_ref, max_ref, routing_ref = refs[:7]
    v_ext, ids_ref, probs_ref, packed, q_sem, sems = refs[7:]
    fetch = [
        pltpu.make_async_copy(ids_hbm, ids_ref, sems.at[0]),
        pltpu.make_async_copy(probs_hbm, probs_ref, sems.at[1]),
        pltpu.make_async_copy(resid_hbm, resid_ref, sems.at[2]),
        pltpu.make_async_copy(w_hbm, w_ref, sems.at[3]),
    ]
    fetch_q = []
    for h in range(heads):
        columns = slice(h * HEAD_DIMENSION, (h + 1) * HEAD_DIMENSION)
        fetch_q.append(
            pltpu.make_async_copy(
                q_hbm.at[:, columns], q_ref.at[pl.ds(h * rows, rows)], q_sem.at[h]
            )
        )
        fetch_q[h].start()
    for copy in fetch:
        copy.start()
    tp = place[2]
    v_ext[:, :HEAD_DIMENSION] = kv_ref[:, HEAD_DIMENSION:]
    v_ext[:, HEAD_DIMENSION:] = jnp.ones((rows, HEAD_DIMENSION), BF)
    keys = kv_ref[:, :HEAD_DIMENSION]
    column = lax.broadcasted_iota(jnp.int32, (rows, rows), 1)
    allowed = column <= lax.broadcasted_iota(jnp.int32, (rows, rows), 0)
    scale = 1.0 / math.sqrt(HEAD_DIMENSION)
    for copy in fetch_q:
        copy.wait()
    s = dot_rows(q_ref[...], keys).reshape(heads, rows, rows)
    s = jnp.where(allowed, s * scale, -1e30).reshape(heads * rows, rows)
    top = jnp.max(s, axis=1, keepdims=True)
    out = jnp.dot(jnp.exp(s - top).astype(BF), v_ext[...], preferred_element_type=F32)
    out_ref[...] = out[:, :HEAD_DIMENSION]
    sum_ref[...] = out[:, HEAD_DIMENSION:]
    max_ref[...] = jnp.broadcast_to(top, max_ref.shape)

    fetch[0].wait()
    fetch[1].wait()
    block = n_tp * part
    ids = ids_ref[...]
    probs = probs_ref[...]
    expert = lax.broadcasted_iota(jnp.int32, (EXPERTS, block), 0)
    named = jnp.zeros((EXPERTS, block), F32)
    for k in range(TOPK):
        named = named + jnp.where(expert == ids[k : k + 1, :], 1.0, 0.0)
    before = lax.broadcasted_iota(jnp.int32, (block, block), 0) < lax.broadcasted_iota(
        jnp.int32, (block, block), 1
    )
    count = jnp.dot(
        named.astype(BF), jnp.where(before, 1.0, 0.0).astype(BF), preferred_element_type=F32
    )
    ranks = [
        jnp.sum(jnp.where(expert == ids[k : k + 1, :], count, 0.0), axis=0, keepdims=True)
        for k in range(TOPK)
    ]
    gates = probs / jnp.sum(probs, axis=0, keepdims=True)
    high = gates.astype(BF).astype(F32)
    fields = jnp.concatenate([ids.astype(F32)] + ranks + [high, gates - high], axis=0)
    packed[...] = jnp.zeros_like(packed)
    packed[: 4 * TOPK, :block] = fields
    packed[...] = packed[...].T
    routing_ref[...] = packed[pl.ds(pl.multiple_of(tp * part, part), part), :].astype(BF)
    fetch[2].wait()
    fetch[3].wait()


def own_block(place, kv, expert_ids, router_probs, queries, out_weight, resid, n_exp, n_tp):
    rows, width = queries.shape
    heads = width // HEAD_DIMENSION
    part, model = resid.shape
    block = expert_ids.shape[0]
    vmem = pl.BlockSpec(memory_space=pltpu.VMEM)
    hbm = pl.BlockSpec(memory_space=pltpu.HBM)
    return pl.pallas_call(
        functools.partial(own_block_kernel, (n_exp, n_tp, heads, part)),
        out_shape=(
            jax.ShapeDtypeStruct((heads * rows, HEAD_DIMENSION), BF),
            jax.ShapeDtypeStruct((width, model), BF),
            jax.ShapeDtypeStruct((part, model), BF),
            jax.ShapeDtypeStruct((heads * rows, HEAD_DIMENSION), F32),
            jax.ShapeDtypeStruct((heads * rows, HEAD_DIMENSION), F32),
            jax.ShapeDtypeStruct((heads * rows, LANES), F32),
            jax.ShapeDtypeStruct((part, LANES), BF),
        ),
        in_specs=[pl.BlockSpec(memory_space=pltpu.SMEM), vmem] + [hbm] * 5,
        out_specs=(vmem,) * 7,
        scratch_shapes=[
            pltpu.VMEM((rows, 2 * HEAD_DIMENSION), BF),
            pltpu.VMEM((TOPK, block), jnp.int32),
            pltpu.VMEM((TOPK, block), F32),
            pltpu.VMEM((LANES, LANES), F32),
            pltpu.SemaphoreType.DMA((heads,)),
            pltpu.SemaphoreType.DMA((4,)),
        ],
        compiler_params=pltpu.CompilerParams(vmem_limit_bytes=20 * MIB),
        cost_estimate=pl.CostEstimate(
            flops=6 * rows * width * rows,
            bytes_accessed=2 * (rows * width + width * model + rows * model),
            transcendentals=rows * rows * heads,
        ),
        name="own_block",
    )(place, kv, *map(in_hbm, (expert_ids.T, router_probs.T, queries, out_weight, resid)))


def dot_columns(a, b):
    return lax.dot_general(a, b, (((0,), (0,)), ((), ())), preferred_element_type=F32)


def attention_kernel(sizes, place, *refs):
    n_ctx, n_exp, n_tp, heads, part = sizes
    rows = n_exp * n_tp * part
    kv_refs, refs = refs[: n_ctx - 1], refs[n_ctx - 1 :]
    q_ref, w_ref, resid_ref, out_ref, sum_ref, max_ref = refs[:6]
    base_ref, across_ref, other_ref = refs[6:9]
    k_all, v_all, att, att_rel = refs[9:]
    ctx, exp, tp = place[0], place[1], place[2]
    for i, kv_ref in enumerate(kv_refs):
        at = slice(i * rows, (i + 1) * rows)
        k_all[at, :] = kv_ref[:, :HEAD_DIMENSION]
        v_all[at, :HEAD_DIMENSION] = kv_ref[:, HEAD_DIMENSION:]
    v_all[:, HEAD_DIMENSION:] = jnp.ones(((n_ctx - 1) * rows, HEAD_DIMENSION), BF)
    piece = lax.broadcasted_iota(jnp.int32, (1, (n_ctx - 1) * rows), 1) // rows
    earlier = jnp.zeros_like(piece)
    for i, bits in enumerate(KV_ORDER):
        there = jnp.where(lax.bitwise_xor(ctx, bits) < ctx, 1, 0)
        earlier = earlier + jnp.where(piece == i, there, 0)
    allowed = earlier == 1
    scale = 1.0 / math.sqrt(HEAD_DIMENSION)
    s = jnp.where(allowed, dot_rows(q_ref[...], k_all[...]) * scale, -1e30)
    own_top = max_ref[...]
    top = jnp.maximum(own_top, jnp.max(s, axis=1, keepdims=True))
    keep = jnp.exp(own_top - top)
    out = jnp.dot(jnp.exp(s - top[:, :1]).astype(BF), v_all[...], preferred_element_type=F32)
    total = sum_ref[...] * keep + out[:, HEAD_DIMENSION:]
    out = out_ref[...] * keep + out[:, :HEAD_DIMENSION]
    att[...] = (out / total).astype(BF)
    for t in range(n_tp):
        for x in range(n_exp):
            owner = lax.rem(exp + x, n_exp) * n_tp + lax.rem(tp + t, n_tp)
            at = (t * n_exp + x) * part
            for h in range(heads):
                source = pl.ds(pl.multiple_of(h * rows + owner * part, part), part)
                columns = slice(h * HEAD_DIMENSION, (h + 1) * HEAD_DIMENSION)
                att_rel[at : at + part, columns] = att[source, :]
    projected = jnp.dot(att_rel[...], w_ref[...], preferred_element_type=F32)
    base_ref[...] = resid_ref[...].astype(F32) + projected[:part]
    across_ref[...] = projected[part : 2 * part].astype(BF)
    other_ref[...] = projected[2 * part :].astype(BF)


def attend_project(place, pieces, own, n_exp, n_tp):
    queries, out_weight, resid = own[:3]
    width, model = out_weight.shape
    n_ctx, heads = len(pieces) + 1, width // HEAD_DIMENSION
    rows = queries.shape[0] // heads
    part = resid.shape[0]
    vmem = pl.BlockSpec(memory_space=pltpu.VMEM)
    return pl.pallas_call(
        functools.partial(attention_kernel, (n_ctx, n_exp, n_tp, heads, part)),
        out_shape=(
            jax.ShapeDtypeStruct((part, model), F32),
            jax.ShapeDtypeStruct((part, model), BF),
            jax.ShapeDtypeStruct((2 * part, model), BF),
        ),
        in_specs=[pl.BlockSpec(memory_space=pltpu.SMEM)] + [vmem] * (n_ctx - 1 + len(own)),
        out_specs=(vmem,) * 3,
        scratch_shapes=[
            pltpu.VMEM(((n_ctx - 1) * rows, HEAD_DIMENSION), BF),
            pltpu.VMEM(((n_ctx - 1) * rows, 2 * HEAD_DIMENSION), BF),
            pltpu.VMEM((heads * rows, HEAD_DIMENSION), BF),
            pltpu.VMEM((rows, width), BF),
        ],
        compiler_params=pltpu.CompilerParams(vmem_limit_bytes=20 * MIB),
        cost_estimate=pl.CostEstimate(
            flops=2 * rows * width * (3 * (n_ctx - 1) * rows + model),
            bytes_accessed=2 * (rows * width + width * model + rows * model),
            transcendentals=rows * n_ctx * rows * heads,
        ),
        name="attend_project",
    )(place, *pieces, *own)


def expert_kernel(n_pieces, depth, experts, first_ref, *refs):
    pieces, (wg_hbm, wu_hbm, wd_hbm) = refs[:n_pieces], refs[n_pieces : n_pieces + 3]
    outs = refs[n_pieces + 3 : n_pieces + 9]
    x_all, packed, pick_all, scale_all, out_all, wgu, wd, act, sems = refs[n_pieces + 9 :]
    sides, tokens, model = x_all.shape
    slots = pick_all.shape[1] // experts
    _, _, halves, hidden, _ = wgu.shape
    blocks = n_pieces // (2 * sides)
    part = tokens // (2 * blocks)

    def gate_up_copies(e):
        slot, rows = lax.rem(e, depth), pl.ds(e * halves, halves)
        return (
            pltpu.make_async_copy(wg_hbm.at[rows], wgu.at[slot, 0], sems.at[0, slot]),
            pltpu.make_async_copy(wu_hbm.at[rows], wgu.at[slot, 1], sems.at[1, slot]),
        )

    def down_copies(e):
        slot, rows = lax.rem(e, depth), pl.ds(e * halves, halves)
        return (pltpu.make_async_copy(wd_hbm.at[rows], wd.at[slot], sems.at[2, slot]),)

    def start(copies):
        for copy in copies:
            copy.start()

    def wait(copies):
        for copy in copies:
            copy.wait()

    def of_expert(e):
        return pl.ds(pl.multiple_of(e * slots, slots), slots)

    def gate_up(e):
        x = jnp.concatenate([out_all[side, of_expert(e), :] for side in range(sides)])
        weight = wgu[lax.rem(e, depth)].reshape(2 * halves * hidden, model)
        both = dot_rows(weight, x)
        gate, up = both[: halves * hidden], both[halves * hidden :]
        return (gate * jax.nn.sigmoid(gate) * up).astype(BF)

    def down(e):
        weight = wd[lax.rem(e, depth)].reshape(halves * hidden, model)
        out = dot_columns(act[lax.rem(e, 2)], weight)
        scale = jnp.concatenate([scale_all[side, of_expert(e), :] for side in range(sides)])
        return (out * scale).astype(BF)

    def keep(e, out):
        for side in range(sides):
            out_all[side, of_expert(e), :] = out[side * slots : (side + 1) * slots]

    for e in range(depth - 1):
        start(gate_up_copies(e))
        if e:
            start(down_copies(e - 1))
    for i, piece in enumerate(pieces):
        core, side, block = i // (sides * blocks), i // blocks % sides, i % blocks
        rows = slice((core * blocks + block) * part, (core * blocks + block + 1) * part)
        x_all[side, rows, :] = piece[:, :model]
        packed[side, rows, :] = piece[:, model:].astype(F32)
    slot = lax.broadcasted_iota(jnp.int32, (slots, tokens), 0)
    token = lax.broadcasted_iota(jnp.int32, (TOPK, tokens), 1)
    offset = lax.rem(token // part, blocks) * (slots // blocks)
    for side in range(sides):
        fields = packed[side].T
        ids, ranks = fields[:TOPK].astype(jnp.int32), fields[TOPK : 2 * TOPK]
        gates = fields[2 * TOPK : 3 * TOPK] + fields[3 * TOPK : 4 * TOPK]
        places = ranks.astype(jnp.int32) + offset
        for e in range(experts):
            hit = ids == first_ref[0] + e
            chosen = slot == jnp.max(jnp.where(hit, places, -1), axis=0, keepdims=True)
            gate = jnp.sum(jnp.where(hit, gates, 0.0), axis=0, keepdims=True)
            here = slice(e * slots, (e + 1) * slots)
            pick_all[side, here, :] = jnp.where(chosen, 1.0, 0.0).astype(BF)
            scale_all[side, here, :] = jnp.sum(
                jnp.where(chosen, gate, 0.0), axis=1, keepdims=True
            )
        out_all[side] = jnp.dot(
            pick_all[side], x_all[side], preferred_element_type=F32
        ).astype(BF)
    wait(gate_up_copies(0))
    act[0] = gate_up(0)

    @pl.loop(0, experts - 1)
    def _(e):
        @pl.when(e + depth - 1 < experts)
        def _():
            start(gate_up_copies(e + depth - 1))

        @pl.when(e + depth - 2 < experts)
        def _():
            start(down_copies(e + depth - 2))

        wait(down_copies(e))
        wait(gate_up_copies(e + 1))
        following = gate_up(e + 1)
        out = down(e)
        act[lax.rem(e + 1, 2)] = following
        keep(e, out)

    wait(down_copies(experts - 1))
    keep(experts - 1, down(experts - 1))
    half = blocks * part // 2
    for side in (1, 0):
        routed = dot_columns(pick_all[side], out_all[side]).astype(BF)
        for core in range(2):
            near, far = routed[2 * core * half :][:half], routed[(2 * core + 1) * half :][:half]
            outs[3 * core + 1 - side][...] = far
            outs[3 * core + 2][(1 - side) * half : (2 - side) * half, :] = near


def cube_experts(first, pieces, w_gate, w_up, w_down, slots):
    rows, hidden, model = w_down.shape
    halves, sides = 2, 2
    experts = rows // halves
    tokens = len(pieces) * pieces[0].shape[0] // sides
    depth = 4
    vmem = pl.BlockSpec(memory_space=pltpu.VMEM)
    hbm = pl.BlockSpec(memory_space=pltpu.HBM)

    half = jax.ShapeDtypeStruct((tokens // 4, model), BF)
    whole = jax.ShapeDtypeStruct((tokens // 2, model), BF)
    return pl.pallas_call(
        functools.partial(expert_kernel, len(pieces), depth, experts),
        out_shape=(half, half, whole) * 2,
        in_specs=[pl.BlockSpec(memory_space=pltpu.SMEM)] + [vmem] * len(pieces) + [hbm] * 3,
        out_specs=(vmem,) * 6,
        scratch_shapes=[
            pltpu.VMEM((sides, tokens, model), BF),
            pltpu.VMEM((sides, tokens, LANES), F32),
            pltpu.VMEM((sides, experts * slots, tokens), BF),
            pltpu.VMEM((sides, experts * slots, 1), F32),
            pltpu.VMEM((sides, experts * slots, model), BF),
            pltpu.VMEM((depth, 2, halves, hidden, model), BF),
            pltpu.VMEM((depth, halves, hidden, model), BF),
            pltpu.VMEM((2, halves * hidden, sides * slots), BF),
            pltpu.SemaphoreType.DMA((3, depth)),
        ],
        compiler_params=pltpu.CompilerParams(vmem_limit_bytes=44 * MIB),
        cost_estimate=pl.CostEstimate(
            flops=2 * experts * sides * slots * model * (3 * halves * hidden + 2 * tokens),
            bytes_accessed=6 * rows * model * hidden + 4 * tokens * model,
            transcendentals=experts * sides * slots * halves * hidden,
        ),
        name="experts",
    )(
        first,
        *pieces,
        in_hbm(jnp.swapaxes(w_gate, 1, 2)),
        in_hbm(jnp.swapaxes(w_up, 1, 2)),
        in_hbm(w_down),
    )


def sums_back(mine, other, part):
    def add(a, *others):
        total = a.astype(F32)
        for b in others:
            total = total + b.astype(F32)
        return total.astype(BF)

    sums = [add(a, flip(b, "tp", 1)) for a, b in zip(mine, other)]
    sums[1], sums[2] = lax.optimization_barrier((sums[1], sums[2]))
    sums = [[x[at : at + part] for at in range(0, x.shape[0], part)] for x in sums]
    across = sums[2][:2] + sums[0]
    here = sums[2][2:] + sums[1]
    far_across = flip(across[2], "exp", 1)
    last_across = flip_both(across[3])
    last = flip(here[3], "ctx", 1)
    own = flip(across[0], "exp", 1)
    near = flip(here[1], "ctx", 1)
    near_across = flip_both(across[1])
    far = flip(add(here[2], last_across, far_across, last), "ctx", 2)
    total = here[0].astype(F32)
    for term in (far, near, near_across, own):
        total = total + term.astype(F32)
    return total


def on_device(
    queries, keys, values, out_weight, resid, expert_ids, router_probs, w_gate, w_up, w_down
):
    n_ctx, n_exp, n_tp = (lax.axis_size(a) for a in ("ctx", "exp", "tp"))
    part = resid.shape[0]
    rows_here = w_gate.shape[0]
    block = expert_ids.shape[0]
    cube = (n_ctx, n_exp, n_tp) == (4, 2, 2) and block == n_tp * part <= LANES
    if not cube or part % 16 or rows_here * n_ctx * n_exp != 2 * EXPERTS:
        return on_device_any_size(
            queries, keys, values, out_weight, resid, expert_ids, router_probs, w_gate, w_up, w_down
        )
    ctx, exp, tp = (lax.axis_index(a) for a in ("ctx", "exp", "tp"))
    place = jnp.stack([ctx, exp, tp]).astype(jnp.int32)
    heads_here = queries.shape[1] // HEAD_DIMENSION
    first = (ctx * n_exp + exp) * rows_here // 2
    slots = n_ctx * min(8, block)

    shared = (exp * n_tp + tp) * heads_here // (QUERY_HEADS // KEY_VALUE_HEADS)
    key_head = lax.dynamic_slice_in_dim(keys, shared * HEAD_DIMENSION, HEAD_DIMENSION, 1)
    value_head = lax.dynamic_slice_in_dim(values, shared * HEAD_DIMENSION, HEAD_DIMENSION, 1)
    kv = jnp.concatenate([key_head, value_head], axis=1)
    kv_pieces = [from_earlier(kv, "ctx", bits) for bits in KV_ORDER]
    *own, routing = own_block(
        place, kv, expert_ids, router_probs, queries, out_weight, resid, n_exp, n_tp
    )
    base, across, other = attend_project(place, kv_pieces, own, n_exp, n_tp)

    other = flip(other, "tp", 1).astype(F32)
    across = flip((across.astype(F32) + other[part:]).astype(BF), "exp", 1)
    hidden = base + other[:part] + across.astype(F32)
    mean_square = jnp.mean(hidden * hidden, axis=1, keepdims=True)
    normed = (hidden * lax.rsqrt(mean_square + 1e-06)).astype(BF)
    normed = jnp.concatenate([normed, routing], axis=1)

    far = flip(normed, "ctx", 2)
    across = flip(normed, "exp", 1)
    near = flip(normed, "ctx", 1)
    near_across = flip_both(normed)
    far_across = flip(far, "exp", 1)
    last_across = flip_both(far)
    last = flip(far, "ctx", 1)
    early = lax.optimization_barrier((normed, near, far, across, near_across))
    pieces = [normed, near, far, last, across, near_across, far_across, last_across]
    pieces += [flip(piece, "tp", 1) for piece in early[:3] + (last,)]
    pieces += [flip(piece, "tp", 1) for piece in early[3:] + (far_across, last_across)]
    sums = cube_experts(
        first.astype(jnp.int32).reshape(1), pieces, w_gate, w_up, w_down, slots
    )
    return (hidden + sums_back(sums[:3], sums[3:], part)).astype(BF)


def solution(mesh):
    in_specs = (
        P(("groups", "ctx"), ("exp", "tp")),
        P(("groups", "ctx"), None),
        P(("groups", "ctx"), None),
        P(("exp", "tp"), None),
        P(("groups", "ctx", "exp", "tp"), None),
        P(("groups", "ctx", "exp"), None),
        P(("groups", "ctx", "exp"), None),
        P(("ctx", "exp"), None, "tp"),
        P(("ctx", "exp"), None, "tp"),
        P(("ctx", "exp"), "tp", None),
    )
    out_specs = P(("groups", "ctx", "exp", "tp"), None)
    return jax.shard_map(
        on_device, mesh=mesh, in_specs=in_specs, out_specs=out_specs, check_vma=False
    )
```

```python
import functools
import math

import jax
import jax.numpy as jnp
from jax import lax
from jax.experimental import pallas as pl
from jax.experimental.pallas import tpu as pltpu
from jax.sharding import PartitionSpec as P

HEAD_DIMENSION = 128
QUERY_HEADS = 32
KEY_VALUE_HEADS = 4
EXPERTS = 64
TOPK = 8
MIB = 1 << 20
LANES = 128
BF = jnp.bfloat16
F32 = jnp.float32


def attend_blocks(blocks, key_head, value_head, heads_here):
    score_scale = 1.0 / math.sqrt(HEAD_DIMENSION)

    def make_state(query_rows):
        row_total = query_rows.shape[0]
        return (
            jnp.full((row_total, heads_here), -1e30, jnp.float32),
            jnp.zeros((row_total, heads_here), jnp.float32),
            jnp.zeros((row_total, heads_here, HEAD_DIMENSION), jnp.float32),
        )

    initial = tuple((make_state(query_rows) for query_rows, query_places in blocks))

    def fold_keys(carry, piece, first):
        key_piece, value_piece = piece
        key_places = jnp.arange(key_piece.shape[0], dtype=jnp.int32)
        updated = []
        for (query_rows, query_places), state in zip(blocks, carry):

            def refresh(state, query_rows=query_rows, query_places=query_places):
                running_max, running_sum, accum = state
                shaped = query_rows.reshape(query_rows.shape[0], heads_here, HEAD_DIMENSION)
                scores = (
                    jnp.einsum("qhd,kd->qhk", shaped, key_piece, preferred_element_type=jnp.float32)
                    * score_scale
                )
                allowed = key_places[None, None, :] <= query_places[:, None, None]
                scores = jnp.where(allowed, scores, -1e30)
                new_max = jnp.maximum(running_max, jnp.max(scores, axis=2))
                weights = jnp.where(allowed, jnp.exp(scores - new_max[:, :, None]), 0.0)
                running_sum = jnp.sum(weights, axis=2)
                accum = jnp.einsum(
                    "qhk,kd->qhd",
                    weights,
                    value_piece.astype(jnp.float32),
                    precision=lax.Precision.HIGHEST,
                )
                return (new_max, running_sum, accum)

            needed = first <= query_places[-1]
            updated.append(lax.cond(needed, refresh, lambda state: state, state))
        return tuple(updated)

    final = fold_keys(
        initial,
        (
            lax.all_gather(key_head, "ctx", axis=0, tiled=True),
            lax.all_gather(value_head, "ctx", axis=0, tiled=True),
        ),
        jnp.int32(0),
    )
    results = []
    for (query_rows, query_places), state in zip(blocks, final):
        running_max, running_sum, accum = state
        results.append(
            (accum / running_sum[:, :, None])
            .reshape(query_rows.shape[0], heads_here * HEAD_DIMENSION)
            .astype(jnp.bfloat16)
        )
    return results


def run_experts(inputs, w_gate, w_up, w_down):
    gate_out = jnp.einsum("rnd,rdf->rnf", inputs, w_gate, preferred_element_type=jnp.float32)
    up_out = jnp.einsum("rnd,rdf->rnf", inputs, w_up, preferred_element_type=jnp.float32)
    activated = (jax.nn.silu(gate_out) * up_out).astype(jnp.bfloat16)
    return jnp.einsum("rnf,rfd->rnd", activated, w_down, preferred_element_type=jnp.float32).astype(
        jnp.bfloat16
    )


def on_device_any_size(
    queries, keys, values, out_weight, resid, expert_ids, router_probs, w_gate, w_up, w_down
):
    rows_ctx = queries.shape[0]
    heads_here = queries.shape[1] // HEAD_DIMENSION
    group_width = QUERY_HEADS // KEY_VALUE_HEADS
    head_rank = lax.axis_index(("exp", "tp"))
    shared = head_rank * heads_here // group_width
    key_head = lax.dynamic_slice_in_dim(keys, shared * HEAD_DIMENSION, HEAD_DIMENSION, 1)
    value_head = lax.dynamic_slice_in_dim(values, shared * HEAD_DIMENSION, HEAD_DIMENSION, 1)
    cycle_rank = lax.axis_index("ctx")
    own_places = cycle_rank * rows_ctx + jnp.arange(rows_ctx, dtype=jnp.int32)
    attended = attend_blocks([(queries, own_places)], key_head, value_head, heads_here)[0]
    projected = lax.psum_scatter(
        jnp.dot(attended, out_weight, preferred_element_type=jnp.float32).astype(jnp.bfloat16),
        ("exp", "tp"),
        scatter_dimension=0,
        tiled=True,
    ).astype(jnp.float32)
    hidden = resid.astype(jnp.float32) + projected
    mean_square = jnp.mean(hidden * hidden, axis=1, keepdims=True)
    normed = (hidden * lax.rsqrt(mean_square + 1e-06)).astype(jnp.bfloat16)
    pair_rows = lax.all_gather(normed, "tp", axis=0, tiled=True)
    slot_count = min(8, expert_ids.shape[0])
    gate_weights = router_probs / jnp.sum(router_probs, axis=1, keepdims=True)
    flat_ids = expert_ids.reshape(-1)
    assigned = flat_ids.shape[0]
    onehot = (flat_ids[:, None] == jnp.arange(EXPERTS, dtype=jnp.int32)[None, :]).astype(jnp.int32)
    slots = jnp.sum(onehot * (jnp.cumsum(onehot, axis=0) - 1), axis=1)
    token_of = jnp.arange(assigned, dtype=jnp.int32) // TOPK
    peer_count = lax.axis_size(("ctx", "exp"))
    rows_here = w_gate.shape[0]
    cell_parts = []
    for half_index in range(2):
        half_rows_id = 2 * flat_ids + half_index
        target = half_rows_id // rows_here
        local_row = half_rows_id % rows_here
        cell_parts.append((local_row * slot_count + slots) * peer_count + target)
    cells = jnp.concatenate(cell_parts)
    table = (
        jnp.full((rows_here * slot_count * peer_count,), -1, jnp.int32)
        .at[cells]
        .set(jnp.concatenate([token_of, token_of]))
    )
    send_buffer = jnp.where(
        table[:, None] >= 0, pair_rows[jnp.maximum(table, 0)], jnp.zeros((), jnp.bfloat16)
    )
    model_width = pair_rows.shape[1]
    received = lax.all_to_all(
        send_buffer.reshape(rows_here * slot_count, peer_count, model_width),
        ("ctx", "exp"),
        split_axis=1,
        concat_axis=1,
        tiled=True,
    )
    expert_out = run_experts(
        received.reshape(rows_here, slot_count * peer_count, model_width), w_gate, w_up, w_down
    )
    returned = lax.all_to_all(
        expert_out.reshape(rows_here * slot_count, peer_count, model_width),
        ("ctx", "exp"),
        split_axis=1,
        concat_axis=1,
        tiled=True,
    )
    returned_flat = returned.reshape(rows_here * slot_count * peer_count, model_width)
    gathered = returned_flat[cells].reshape(2, expert_ids.shape[0], TOPK, model_width)
    routed_part = jnp.einsum(
        "hakd,ak->ad", gathered.astype(jnp.float32), gate_weights, precision=lax.Precision.HIGHEST
    )
    routed = lax.psum_scatter(
        routed_part.astype(jnp.bfloat16), "tp", scatter_dimension=0, tiled=True
    ).astype(jnp.float32)
    return (hidden + routed).astype(jnp.bfloat16)


def flip(x, axis, bit):
    return lax.ppermute(x, axis, [(i, i ^ bit) for i in range(lax.axis_size(axis))])


def flip_both(x):
    n_exp = lax.axis_size("exp")
    mask = n_exp + 1
    size = lax.axis_size("ctx") * n_exp
    return lax.ppermute(x, ("ctx", "exp"), [(i, i ^ mask) for i in range(size)])


def from_earlier(x, axis, bits):
    return lax.ppermute(x, axis, [(i, i ^ bits) for i in range(lax.axis_size(axis)) if i < i ^ bits])


def in_hbm(x):
    return pltpu.with_memory_space_constraint(x, pltpu.HBM)


def dot_rows(a, b):
    return lax.dot_general(a, b, (((1,), (1,)), ((), ())), preferred_element_type=F32)


KV_ORDER = (1, 2, 3)


def own_block_kernel(sizes, place, kv_ref, ids_hbm, probs_hbm, q_hbm, w_hbm, resid_hbm, *refs):
    n_exp, n_tp, heads, part = sizes
    rows = n_exp * n_tp * part
    q_ref, w_ref, resid_ref, out_ref, sum_ref, max_ref, routing_ref = refs[:7]
    v_ext, ids_ref, probs_ref, packed, q_sem, sems = refs[7:]
    fetch = [
        pltpu.make_async_copy(ids_hbm, ids_ref, sems.at[0]),
        pltpu.make_async_copy(probs_hbm, probs_ref, sems.at[1]),
        pltpu.make_async_copy(resid_hbm, resid_ref, sems.at[2]),
        pltpu.make_async_copy(w_hbm, w_ref, sems.at[3]),
    ]
    fetch_q = []
    for h in range(heads):
        columns = slice(h * HEAD_DIMENSION, (h + 1) * HEAD_DIMENSION)
        fetch_q.append(
            pltpu.make_async_copy(
                q_hbm.at[:, columns], q_ref.at[pl.ds(h * rows, rows)], q_sem.at[h]
            )
        )
        fetch_q[h].start()
    for copy in fetch:
        copy.start()
    tp = place[2]
    v_ext[:, :HEAD_DIMENSION] = kv_ref[:, HEAD_DIMENSION:]
    v_ext[:, HEAD_DIMENSION:] = jnp.ones((rows, HEAD_DIMENSION), BF)
    keys = kv_ref[:, :HEAD_DIMENSION]
    column = lax.broadcasted_iota(jnp.int32, (rows, rows), 1)
    allowed = column <= lax.broadcasted_iota(jnp.int32, (rows, rows), 0)
    scale = 1.0 / math.sqrt(HEAD_DIMENSION)
    for copy in fetch_q:
        copy.wait()
    s = dot_rows(q_ref[...], keys).reshape(heads, rows, rows)
    s = jnp.where(allowed, s * scale, -1e30).reshape(heads * rows, rows)
    top = jnp.max(s, axis=1, keepdims=True)
    out = jnp.dot(jnp.exp(s - top).astype(BF), v_ext[...], preferred_element_type=F32)
    out_ref[...] = out[:, :HEAD_DIMENSION]
    sum_ref[...] = out[:, HEAD_DIMENSION:]
    max_ref[...] = jnp.broadcast_to(top, max_ref.shape)

    fetch[0].wait()
    fetch[1].wait()
    block = n_tp * part
    ids = ids_ref[...]
    probs = probs_ref[...]
    expert = lax.broadcasted_iota(jnp.int32, (EXPERTS, block), 0)
    named = jnp.zeros((EXPERTS, block), F32)
    for k in range(TOPK):
        named = named + jnp.where(expert == ids[k : k + 1, :], 1.0, 0.0)
    before = lax.broadcasted_iota(jnp.int32, (block, block), 0) < lax.broadcasted_iota(
        jnp.int32, (block, block), 1
    )
    count = jnp.dot(
        named.astype(BF), jnp.where(before, 1.0, 0.0).astype(BF), preferred_element_type=F32
    )
    ranks = [
        jnp.sum(jnp.where(expert == ids[k : k + 1, :], count, 0.0), axis=0, keepdims=True)
        for k in range(TOPK)
    ]
    gates = probs / jnp.sum(probs, axis=0, keepdims=True)
    high = gates.astype(BF).astype(F32)
    fields = jnp.concatenate([ids.astype(F32)] + ranks + [high, gates - high], axis=0)
    packed[...] = jnp.zeros_like(packed)
    packed[: 4 * TOPK, :block] = fields
    packed[...] = packed[...].T
    routing_ref[...] = packed[pl.ds(pl.multiple_of(tp * part, part), part), :].astype(BF)
    fetch[2].wait()
    fetch[3].wait()


def own_block(place, kv, expert_ids, router_probs, queries, out_weight, resid, n_exp, n_tp):
    rows, width = queries.shape
    heads = width // HEAD_DIMENSION
    part, model = resid.shape
    block = expert_ids.shape[0]
    vmem = pl.BlockSpec(memory_space=pltpu.VMEM)
    hbm = pl.BlockSpec(memory_space=pltpu.HBM)
    return pl.pallas_call(
        functools.partial(own_block_kernel, (n_exp, n_tp, heads, part)),
        out_shape=(
            jax.ShapeDtypeStruct((heads * rows, HEAD_DIMENSION), BF),
            jax.ShapeDtypeStruct((width, model), BF),
            jax.ShapeDtypeStruct((part, model), BF),
            jax.ShapeDtypeStruct((heads * rows, HEAD_DIMENSION), F32),
            jax.ShapeDtypeStruct((heads * rows, HEAD_DIMENSION), F32),
            jax.ShapeDtypeStruct((heads * rows, LANES), F32),
            jax.ShapeDtypeStruct((part, LANES), BF),
        ),
        in_specs=[pl.BlockSpec(memory_space=pltpu.SMEM), vmem] + [hbm] * 5,
        out_specs=(vmem,) * 7,
        scratch_shapes=[
            pltpu.VMEM((rows, 2 * HEAD_DIMENSION), BF),
            pltpu.VMEM((TOPK, block), jnp.int32),
            pltpu.VMEM((TOPK, block), F32),
            pltpu.VMEM((LANES, LANES), F32),
            pltpu.SemaphoreType.DMA((heads,)),
            pltpu.SemaphoreType.DMA((4,)),
        ],
        compiler_params=pltpu.CompilerParams(vmem_limit_bytes=20 * MIB),
        cost_estimate=pl.CostEstimate(
            flops=6 * rows * width * rows,
            bytes_accessed=2 * (rows * width + width * model + rows * model),
            transcendentals=rows * rows * heads,
        ),
        name="own_block",
    )(place, kv, *map(in_hbm, (expert_ids.T, router_probs.T, queries, out_weight, resid)))


def dot_columns(a, b):
    return lax.dot_general(a, b, (((0,), (0,)), ((), ())), preferred_element_type=F32)


def attention_kernel(sizes, place, *refs):
    n_ctx, n_exp, n_tp, heads, part = sizes
    rows = n_exp * n_tp * part
    kv_refs, refs = refs[: n_ctx - 1], refs[n_ctx - 1 :]
    q_ref, w_ref, resid_ref, out_ref, sum_ref, max_ref = refs[:6]
    base_ref, across_ref, other_ref = refs[6:9]
    k_all, v_all, att, att_rel = refs[9:]
    ctx, exp, tp = place[0], place[1], place[2]
    for i, kv_ref in enumerate(kv_refs):
        at = slice(i * rows, (i + 1) * rows)
        k_all[at, :] = kv_ref[:, :HEAD_DIMENSION]
        v_all[at, :HEAD_DIMENSION] = kv_ref[:, HEAD_DIMENSION:]
    v_all[:, HEAD_DIMENSION:] = jnp.ones(((n_ctx - 1) * rows, HEAD_DIMENSION), BF)
    piece = lax.broadcasted_iota(jnp.int32, (1, (n_ctx - 1) * rows), 1) // rows
    earlier = jnp.zeros_like(piece)
    for i, bits in enumerate(KV_ORDER):
        there = jnp.where(lax.bitwise_xor(ctx, bits) < ctx, 1, 0)
        earlier = earlier + jnp.where(piece == i, there, 0)
    allowed = earlier == 1
    scale = 1.0 / math.sqrt(HEAD_DIMENSION)
    s = jnp.where(allowed, dot_rows(q_ref[...], k_all[...]) * scale, -1e30)
    own_top = max_ref[...]
    top = jnp.maximum(own_top, jnp.max(s, axis=1, keepdims=True))
    keep = jnp.exp(own_top - top)
    out = jnp.dot(jnp.exp(s - top[:, :1]).astype(BF), v_all[...], preferred_element_type=F32)
    total = sum_ref[...] * keep + out[:, HEAD_DIMENSION:]
    out = out_ref[...] * keep + out[:, :HEAD_DIMENSION]
    att[...] = (out / total).astype(BF)
    for t in range(n_tp):
        for x in range(n_exp):
            owner = lax.rem(exp + x, n_exp) * n_tp + lax.rem(tp + t, n_tp)
            at = (t * n_exp + x) * part
            for h in range(heads):
                source = pl.ds(pl.multiple_of(h * rows + owner * part, part), part)
                columns = slice(h * HEAD_DIMENSION, (h + 1) * HEAD_DIMENSION)
                att_rel[at : at + part, columns] = att[source, :]
    projected = jnp.dot(att_rel[...], w_ref[...], preferred_element_type=F32)
    base_ref[...] = resid_ref[...].astype(F32) + projected[:part]
    across_ref[...] = projected[part : 2 * part].astype(BF)
    other_ref[...] = projected[2 * part :].astype(BF)


def attend_project(place, pieces, own, n_exp, n_tp):
    queries, out_weight, resid = own[:3]
    width, model = out_weight.shape
    n_ctx, heads = len(pieces) + 1, width // HEAD_DIMENSION
    rows = queries.shape[0] // heads
    part = resid.shape[0]
    vmem = pl.BlockSpec(memory_space=pltpu.VMEM)
    return pl.pallas_call(
        functools.partial(attention_kernel, (n_ctx, n_exp, n_tp, heads, part)),
        out_shape=(
            jax.ShapeDtypeStruct((part, model), F32),
            jax.ShapeDtypeStruct((part, model), BF),
            jax.ShapeDtypeStruct((2 * part, model), BF),
        ),
        in_specs=[pl.BlockSpec(memory_space=pltpu.SMEM)] + [vmem] * (n_ctx - 1 + len(own)),
        out_specs=(vmem,) * 3,
        scratch_shapes=[
            pltpu.VMEM(((n_ctx - 1) * rows, HEAD_DIMENSION), BF),
            pltpu.VMEM(((n_ctx - 1) * rows, 2 * HEAD_DIMENSION), BF),
            pltpu.VMEM((heads * rows, HEAD_DIMENSION), BF),
            pltpu.VMEM((rows, width), BF),
        ],
        compiler_params=pltpu.CompilerParams(vmem_limit_bytes=20 * MIB),
        cost_estimate=pl.CostEstimate(
            flops=2 * rows * width * (3 * (n_ctx - 1) * rows + model),
            bytes_accessed=2 * (rows * width + width * model + rows * model),
            transcendentals=rows * n_ctx * rows * heads,
        ),
        name="attend_project",
    )(place, *pieces, *own)


def expert_kernel(n_pieces, depth, experts, first_ref, *refs):
    pieces, (wg_hbm, wu_hbm, wd_hbm) = refs[:n_pieces], refs[n_pieces : n_pieces + 3]
    outs = refs[n_pieces + 3 : n_pieces + 9]
    x_all, packed, pick_all, scale_all, out_all, wgu, wd, act, sems = refs[n_pieces + 9 :]
    sides, tokens, model = x_all.shape
    slots = pick_all.shape[1] // experts
    _, _, halves, hidden, _ = wgu.shape
    blocks = n_pieces // (2 * sides)
    part = tokens // (2 * blocks)

    def gate_up_copies(e):
        slot, rows = lax.rem(e, depth), pl.ds(e * halves, halves)
        return (
            pltpu.make_async_copy(wg_hbm.at[rows], wgu.at[slot, 0], sems.at[0, slot]),
            pltpu.make_async_copy(wu_hbm.at[rows], wgu.at[slot, 1], sems.at[1, slot]),
        )

    def down_copies(e):
        slot, rows = lax.rem(e, depth), pl.ds(e * halves, halves)
        return (pltpu.make_async_copy(wd_hbm.at[rows], wd.at[slot], sems.at[2, slot]),)

    def start(copies):
        for copy in copies:
            copy.start()

    def wait(copies):
        for copy in copies:
            copy.wait()

    def of_expert(e):
        return pl.ds(pl.multiple_of(e * slots, slots), slots)

    def gate_up(e):
        x = jnp.concatenate([out_all[side, of_expert(e), :] for side in range(sides)])
        weight = wgu[lax.rem(e, depth)].reshape(2 * halves * hidden, model)
        both = dot_rows(weight, x)
        gate, up = both[: halves * hidden], both[halves * hidden :]
        return (gate * jax.nn.sigmoid(gate) * up).astype(BF)

    def down(e):
        weight = wd[lax.rem(e, depth)].reshape(halves * hidden, model)
        out = dot_columns(act[lax.rem(e, 2)], weight)
        scale = jnp.concatenate([scale_all[side, of_expert(e), :] for side in range(sides)])
        return (out * scale).astype(BF)

    def keep(e, out):
        for side in range(sides):
            out_all[side, of_expert(e), :] = out[side * slots : (side + 1) * slots]

    for e in range(depth - 1):
        start(gate_up_copies(e))
        if e:
            start(down_copies(e - 1))
    for i, piece in enumerate(pieces):
        core, side, block = i // (sides * blocks), i // blocks % sides, i % blocks
        rows = slice((core * blocks + block) * part, (core * blocks + block + 1) * part)
        x_all[side, rows, :] = piece[:, :model]
        packed[side, rows, :] = piece[:, model:].astype(F32)
    slot = lax.broadcasted_iota(jnp.int32, (slots, tokens), 0)
    token = lax.broadcasted_iota(jnp.int32, (TOPK, tokens), 1)
    offset = lax.rem(token // part, blocks) * (slots // blocks)
    @pl.loop(0, sides)
    def _(side):
        fields = packed[side].T
        ids, ranks = fields[:TOPK].astype(jnp.int32), fields[TOPK : 2 * TOPK]
        gates = fields[2 * TOPK : 3 * TOPK] + fields[3 * TOPK : 4 * TOPK]
        places = ranks.astype(jnp.int32) + offset
        for e in range(experts):
            hit = ids == first_ref[0] + e
            chosen = slot == jnp.max(jnp.where(hit, places, -1), axis=0, keepdims=True)
            gate = jnp.sum(jnp.where(hit, gates, 0.0), axis=0, keepdims=True)
            here = slice(e * slots, (e + 1) * slots)
            pick_all[side, here, :] = jnp.where(chosen, 1.0, 0.0).astype(BF)
            scale_all[side, here, :] = jnp.sum(
                jnp.where(chosen, gate, 0.0), axis=1, keepdims=True
            )
        out_all[side] = jnp.dot(
            pick_all[side], x_all[side], preferred_element_type=F32
        ).astype(BF)
    wait(gate_up_copies(0))
    act[0] = gate_up(0)

    @pl.loop(0, experts - 1)
    def _(e):
        @pl.when(e + depth - 1 < experts)
        def _():
            start(gate_up_copies(e + depth - 1))

        @pl.when(e + depth - 2 < experts)
        def _():
            start(down_copies(e + depth - 2))

        wait(down_copies(e))
        wait(gate_up_copies(e + 1))
        following = gate_up(e + 1)
        out = down(e)
        act[lax.rem(e + 1, 2)] = following
        keep(e, out)

    wait(down_copies(experts - 1))
    keep(experts - 1, down(experts - 1))
    half = blocks * part // 2
    for side in (1, 0):
        routed = dot_columns(pick_all[side], out_all[side]).astype(BF)
        for core in range(2):
            near, far = routed[2 * core * half :][:half], routed[(2 * core + 1) * half :][:half]
            outs[3 * core + 1 - side][...] = far
            outs[3 * core + 2][(1 - side) * half : (2 - side) * half, :] = near


def cube_experts(first, pieces, w_gate, w_up, w_down, slots):
    rows, hidden, model = w_down.shape
    halves, sides = 2, 2
    experts = rows // halves
    tokens = len(pieces) * pieces[0].shape[0] // sides
    depth = 4
    vmem = pl.BlockSpec(memory_space=pltpu.VMEM)
    hbm = pl.BlockSpec(memory_space=pltpu.HBM)

    half = jax.ShapeDtypeStruct((tokens // 4, model), BF)
    whole = jax.ShapeDtypeStruct((tokens // 2, model), BF)
    return pl.pallas_call(
        functools.partial(expert_kernel, len(pieces), depth, experts),
        out_shape=(half, half, whole) * 2,
        in_specs=[pl.BlockSpec(memory_space=pltpu.SMEM)] + [vmem] * len(pieces) + [hbm] * 3,
        out_specs=(vmem,) * 6,
        scratch_shapes=[
            pltpu.VMEM((sides, tokens, model), BF),
            pltpu.VMEM((sides, tokens, LANES), F32),
            pltpu.VMEM((sides, experts * slots, tokens), BF),
            pltpu.VMEM((sides, experts * slots, 1), F32),
            pltpu.VMEM((sides, experts * slots, model), BF),
            pltpu.VMEM((depth, 2, halves, hidden, model), BF),
            pltpu.VMEM((depth, halves, hidden, model), BF),
            pltpu.VMEM((2, halves * hidden, sides * slots), BF),
            pltpu.SemaphoreType.DMA((3, depth)),
        ],
        compiler_params=pltpu.CompilerParams(vmem_limit_bytes=44 * MIB),
        cost_estimate=pl.CostEstimate(
            flops=2 * experts * sides * slots * model * (3 * halves * hidden + 2 * tokens),
            bytes_accessed=6 * rows * model * hidden + 4 * tokens * model,
            transcendentals=experts * sides * slots * halves * hidden,
        ),
        name="experts",
    )(
        first,
        *pieces,
        in_hbm(jnp.swapaxes(w_gate, 1, 2)),
        in_hbm(jnp.swapaxes(w_up, 1, 2)),
        in_hbm(w_down),
    )


def sums_back(mine, other, part):
    def add(a, *others):
        total = a.astype(F32)
        for b in others:
            total = total + b.astype(F32)
        return total.astype(BF)

    sums = [add(a, flip(b, "tp", 1)) for a, b in zip(mine, other)]
    sums[1], sums[2] = lax.optimization_barrier((sums[1], sums[2]))
    sums = [[x[at : at + part] for at in range(0, x.shape[0], part)] for x in sums]
    across = sums[2][:2] + sums[0]
    here = sums[2][2:] + sums[1]
    far_across = flip(across[2], "exp", 1)
    last_across = flip_both(across[3])
    last = flip(here[3], "ctx", 1)
    own = flip(across[0], "exp", 1)
    near = flip(here[1], "ctx", 1)
    near_across = flip_both(across[1])
    far = flip(add(here[2], last_across, far_across, last), "ctx", 2)
    total = here[0].astype(F32)
    for term in (far, near, near_across, own):
        total = total + term.astype(F32)
    return total


def on_device(
    queries, keys, values, out_weight, resid, expert_ids, router_probs, w_gate, w_up, w_down
):
    n_ctx, n_exp, n_tp = (lax.axis_size(a) for a in ("ctx", "exp", "tp"))
    part = resid.shape[0]
    rows_here = w_gate.shape[0]
    block = expert_ids.shape[0]
    cube = (n_ctx, n_exp, n_tp) == (4, 2, 2) and block == n_tp * part <= LANES
    if not cube or part % 16 or rows_here * n_ctx * n_exp != 2 * EXPERTS:
        return on_device_any_size(
            queries, keys, values, out_weight, resid, expert_ids, router_probs, w_gate, w_up, w_down
        )
    ctx, exp, tp = (lax.axis_index(a) for a in ("ctx", "exp", "tp"))
    place = jnp.stack([ctx, exp, tp]).astype(jnp.int32)
    heads_here = queries.shape[1] // HEAD_DIMENSION
    first = (ctx * n_exp + exp) * rows_here // 2
    slots = n_ctx * min(8, block)

    shared = (exp * n_tp + tp) * heads_here // (QUERY_HEADS // KEY_VALUE_HEADS)
    key_head = lax.dynamic_slice_in_dim(keys, shared * HEAD_DIMENSION, HEAD_DIMENSION, 1)
    value_head = lax.dynamic_slice_in_dim(values, shared * HEAD_DIMENSION, HEAD_DIMENSION, 1)
    kv = jnp.concatenate([key_head, value_head], axis=1)
    kv_pieces = [from_earlier(kv, "ctx", bits) for bits in KV_ORDER]
    *own, routing = own_block(
        place, kv, expert_ids, router_probs, queries, out_weight, resid, n_exp, n_tp
    )
    base, across, other = attend_project(place, kv_pieces, own, n_exp, n_tp)

    other = flip(other, "tp", 1).astype(F32)
    across = flip((across.astype(F32) + other[part:]).astype(BF), "exp", 1)
    hidden = base + other[:part] + across.astype(F32)
    mean_square = jnp.mean(hidden * hidden, axis=1, keepdims=True)
    normed = (hidden * lax.rsqrt(mean_square + 1e-06)).astype(BF)
    normed = jnp.concatenate([normed, routing], axis=1)

    far = flip(normed, "ctx", 2)
    across = flip(normed, "exp", 1)
    near = flip(normed, "ctx", 1)
    near_across = flip_both(normed)
    far_across = flip(far, "exp", 1)
    last_across = flip_both(far)
    last = flip(far, "ctx", 1)
    early = lax.optimization_barrier((normed, near, far, across, near_across))
    pieces = [normed, near, far, last, across, near_across, far_across, last_across]
    pieces += [flip(piece, "tp", 1) for piece in early[:3] + (last,)]
    pieces += [flip(piece, "tp", 1) for piece in early[3:] + (far_across, last_across)]
    sums = cube_experts(
        first.astype(jnp.int32).reshape(1), pieces, w_gate, w_up, w_down, slots
    )
    return (hidden + sums_back(sums[:3], sums[3:], part)).astype(BF)


def solution(mesh):
    in_specs = (
        P(("groups", "ctx"), ("exp", "tp")),
        P(("groups", "ctx"), None),
        P(("groups", "ctx"), None),
        P(("exp", "tp"), None),
        P(("groups", "ctx", "exp", "tp"), None),
        P(("groups", "ctx", "exp"), None),
        P(("groups", "ctx", "exp"), None),
        P(("ctx", "exp"), None, "tp"),
        P(("ctx", "exp"), None, "tp"),
        P(("ctx", "exp"), "tp", None),
    )
    out_specs = P(("groups", "ctx", "exp", "tp"), None)
    return jax.shard_map(
        on_device, mesh=mesh, in_specs=in_specs, out_specs=out_specs, check_vma=False
    )
```

```python
import functools
import math

import jax
import jax.numpy as jnp
from jax import lax
from jax.experimental import pallas as pl
from jax.experimental.pallas import tpu as pltpu
from jax.sharding import PartitionSpec as P

HEAD_DIMENSION = 128
QUERY_HEADS = 32
KEY_VALUE_HEADS = 4
EXPERTS = 64
TOPK = 8
MIB = 1 << 20
LANES = 128
BF = jnp.bfloat16
F32 = jnp.float32


def attend_blocks(blocks, key_head, value_head, heads_here):
    score_scale = 1.0 / math.sqrt(HEAD_DIMENSION)

    def make_state(query_rows):
        row_total = query_rows.shape[0]
        return (
            jnp.full((row_total, heads_here), -1e30, jnp.float32),
            jnp.zeros((row_total, heads_here), jnp.float32),
            jnp.zeros((row_total, heads_here, HEAD_DIMENSION), jnp.float32),
        )

    initial = tuple((make_state(query_rows) for query_rows, query_places in blocks))

    def fold_keys(carry, piece, first):
        key_piece, value_piece = piece
        key_places = jnp.arange(key_piece.shape[0], dtype=jnp.int32)
        updated = []
        for (query_rows, query_places), state in zip(blocks, carry):

            def refresh(state, query_rows=query_rows, query_places=query_places):
                running_max, running_sum, accum = state
                shaped = query_rows.reshape(query_rows.shape[0], heads_here, HEAD_DIMENSION)
                scores = (
                    jnp.einsum("qhd,kd->qhk", shaped, key_piece, preferred_element_type=jnp.float32)
                    * score_scale
                )
                allowed = key_places[None, None, :] <= query_places[:, None, None]
                scores = jnp.where(allowed, scores, -1e30)
                new_max = jnp.maximum(running_max, jnp.max(scores, axis=2))
                weights = jnp.where(allowed, jnp.exp(scores - new_max[:, :, None]), 0.0)
                running_sum = jnp.sum(weights, axis=2)
                accum = jnp.einsum(
                    "qhk,kd->qhd",
                    weights,
                    value_piece.astype(jnp.float32),
                    precision=lax.Precision.HIGHEST,
                )
                return (new_max, running_sum, accum)

            needed = first <= query_places[-1]
            updated.append(lax.cond(needed, refresh, lambda state: state, state))
        return tuple(updated)

    final = fold_keys(
        initial,
        (
            lax.all_gather(key_head, "ctx", axis=0, tiled=True),
            lax.all_gather(value_head, "ctx", axis=0, tiled=True),
        ),
        jnp.int32(0),
    )
    results = []
    for (query_rows, query_places), state in zip(blocks, final):
        running_max, running_sum, accum = state
        results.append(
            (accum / running_sum[:, :, None])
            .reshape(query_rows.shape[0], heads_here * HEAD_DIMENSION)
            .astype(jnp.bfloat16)
        )
    return results


def run_experts(inputs, w_gate, w_up, w_down):
    gate_out = jnp.einsum("rnd,rdf->rnf", inputs, w_gate, preferred_element_type=jnp.float32)
    up_out = jnp.einsum("rnd,rdf->rnf", inputs, w_up, preferred_element_type=jnp.float32)
    activated = (jax.nn.silu(gate_out) * up_out).astype(jnp.bfloat16)
    return jnp.einsum("rnf,rfd->rnd", activated, w_down, preferred_element_type=jnp.float32).astype(
        jnp.bfloat16
    )


def on_device_any_size(
    queries, keys, values, out_weight, resid, expert_ids, router_probs, w_gate, w_up, w_down
):
    rows_ctx = queries.shape[0]
    heads_here = queries.shape[1] // HEAD_DIMENSION
    group_width = QUERY_HEADS // KEY_VALUE_HEADS
    head_rank = lax.axis_index(("exp", "tp"))
    shared = head_rank * heads_here // group_width
    key_head = lax.dynamic_slice_in_dim(keys, shared * HEAD_DIMENSION, HEAD_DIMENSION, 1)
    value_head = lax.dynamic_slice_in_dim(values, shared * HEAD_DIMENSION, HEAD_DIMENSION, 1)
    cycle_rank = lax.axis_index("ctx")
    own_places = cycle_rank * rows_ctx + jnp.arange(rows_ctx, dtype=jnp.int32)
    attended = attend_blocks([(queries, own_places)], key_head, value_head, heads_here)[0]
    projected = lax.psum_scatter(
        jnp.dot(attended, out_weight, preferred_element_type=jnp.float32).astype(jnp.bfloat16),
        ("exp", "tp"),
        scatter_dimension=0,
        tiled=True,
    ).astype(jnp.float32)
    hidden = resid.astype(jnp.float32) + projected
    mean_square = jnp.mean(hidden * hidden, axis=1, keepdims=True)
    normed = (hidden * lax.rsqrt(mean_square + 1e-06)).astype(jnp.bfloat16)
    pair_rows = lax.all_gather(normed, "tp", axis=0, tiled=True)
    slot_count = min(8, expert_ids.shape[0])
    gate_weights = router_probs / jnp.sum(router_probs, axis=1, keepdims=True)
    flat_ids = expert_ids.reshape(-1)
    assigned = flat_ids.shape[0]
    onehot = (flat_ids[:, None] == jnp.arange(EXPERTS, dtype=jnp.int32)[None, :]).astype(jnp.int32)
    slots = jnp.sum(onehot * (jnp.cumsum(onehot, axis=0) - 1), axis=1)
    token_of = jnp.arange(assigned, dtype=jnp.int32) // TOPK
    peer_count = lax.axis_size(("ctx", "exp"))
    rows_here = w_gate.shape[0]
    cell_parts = []
    for half_index in range(2):
        half_rows_id = 2 * flat_ids + half_index
        target = half_rows_id // rows_here
        local_row = half_rows_id % rows_here
        cell_parts.append((local_row * slot_count + slots) * peer_count + target)
    cells = jnp.concatenate(cell_parts)
    table = (
        jnp.full((rows_here * slot_count * peer_count,), -1, jnp.int32)
        .at[cells]
        .set(jnp.concatenate([token_of, token_of]))
    )
    send_buffer = jnp.where(
        table[:, None] >= 0, pair_rows[jnp.maximum(table, 0)], jnp.zeros((), jnp.bfloat16)
    )
    model_width = pair_rows.shape[1]
    received = lax.all_to_all(
        send_buffer.reshape(rows_here * slot_count, peer_count, model_width),
        ("ctx", "exp"),
        split_axis=1,
        concat_axis=1,
        tiled=True,
    )
    expert_out = run_experts(
        received.reshape(rows_here, slot_count * peer_count, model_width), w_gate, w_up, w_down
    )
    returned = lax.all_to_all(
        expert_out.reshape(rows_here * slot_count, peer_count, model_width),
        ("ctx", "exp"),
        split_axis=1,
        concat_axis=1,
        tiled=True,
    )
    returned_flat = returned.reshape(rows_here * slot_count * peer_count, model_width)
    gathered = returned_flat[cells].reshape(2, expert_ids.shape[0], TOPK, model_width)
    routed_part = jnp.einsum(
        "hakd,ak->ad", gathered.astype(jnp.float32), gate_weights, precision=lax.Precision.HIGHEST
    )
    routed = lax.psum_scatter(
        routed_part.astype(jnp.bfloat16), "tp", scatter_dimension=0, tiled=True
    ).astype(jnp.float32)
    return (hidden + routed).astype(jnp.bfloat16)


def flip(x, axis, bit):
    return lax.ppermute(x, axis, [(i, i ^ bit) for i in range(lax.axis_size(axis))])


def flip_both(x):
    n_exp = lax.axis_size("exp")
    mask = n_exp + 1
    size = lax.axis_size("ctx") * n_exp
    return lax.ppermute(x, ("ctx", "exp"), [(i, i ^ mask) for i in range(size)])


def from_earlier(x, axis, bits):
    return lax.ppermute(x, axis, [(i, i ^ bits) for i in range(lax.axis_size(axis)) if i < i ^ bits])


def in_hbm(x):
    return pltpu.with_memory_space_constraint(x, pltpu.HBM)


def dot_rows(a, b):
    return lax.dot_general(a, b, (((1,), (1,)), ((), ())), preferred_element_type=F32)


KV_ORDER = (1, 2, 3)


def own_block_kernel(sizes, place, kv_ref, ids_hbm, probs_hbm, q_hbm, w_hbm, resid_hbm, *refs):
    n_exp, n_tp, heads, part = sizes
    rows = n_exp * n_tp * part
    q_ref, w_ref, resid_ref, out_ref, sum_ref, max_ref, routing_ref = refs[:7]
    v_ext, ids_ref, probs_ref, packed, q_sem, sems = refs[7:]
    fetch = [
        pltpu.make_async_copy(ids_hbm, ids_ref, sems.at[0]),
        pltpu.make_async_copy(probs_hbm, probs_ref, sems.at[1]),
        pltpu.make_async_copy(resid_hbm, resid_ref, sems.at[2]),
        pltpu.make_async_copy(w_hbm, w_ref, sems.at[3]),
    ]
    fetch_q = []
    for h in range(heads):
        columns = slice(h * HEAD_DIMENSION, (h + 1) * HEAD_DIMENSION)
        fetch_q.append(
            pltpu.make_async_copy(
                q_hbm.at[:, columns], q_ref.at[pl.ds(h * rows, rows)], q_sem.at[h]
            )
        )
        fetch_q[h].start()
    for copy in fetch:
        copy.start()
    tp = place[2]
    v_ext[:, :HEAD_DIMENSION] = kv_ref[:, HEAD_DIMENSION:]
    v_ext[:, HEAD_DIMENSION:] = jnp.ones((rows, HEAD_DIMENSION), BF)
    keys = kv_ref[:, :HEAD_DIMENSION]
    column = lax.broadcasted_iota(jnp.int32, (rows, rows), 1)
    allowed = column <= lax.broadcasted_iota(jnp.int32, (rows, rows), 0)
    scale = 1.0 / math.sqrt(HEAD_DIMENSION)
    for copy in fetch_q:
        copy.wait()
    s = dot_rows(q_ref[...], keys).reshape(heads, rows, rows)
    s = jnp.where(allowed, s * scale, -1e30).reshape(heads * rows, rows)
    top = jnp.max(s, axis=1, keepdims=True)
    out = jnp.dot(jnp.exp(s - top).astype(BF), v_ext[...], preferred_element_type=F32)
    out_ref[...] = out[:, :HEAD_DIMENSION]
    sum_ref[...] = out[:, HEAD_DIMENSION:]
    max_ref[...] = jnp.broadcast_to(top, max_ref.shape)

    fetch[0].wait()
    fetch[1].wait()
    block = n_tp * part
    ids = ids_ref[...]
    probs = probs_ref[...]
    expert = lax.broadcasted_iota(jnp.int32, (EXPERTS, block), 0)
    named = jnp.zeros((EXPERTS, block), F32)
    for k in range(TOPK):
        named = named + jnp.where(expert == ids[k : k + 1, :], 1.0, 0.0)
    before = lax.broadcasted_iota(jnp.int32, (block, block), 0) < lax.broadcasted_iota(
        jnp.int32, (block, block), 1
    )
    count = jnp.dot(
        named.astype(BF), jnp.where(before, 1.0, 0.0).astype(BF), preferred_element_type=F32
    )
    ranks = [
        jnp.sum(jnp.where(expert == ids[k : k + 1, :], count, 0.0), axis=0, keepdims=True)
        for k in range(TOPK)
    ]
    gates = probs / jnp.sum(probs, axis=0, keepdims=True)
    high = gates.astype(BF).astype(F32)
    fields = jnp.concatenate([ids.astype(F32)] + ranks + [high, gates - high], axis=0)
    packed[...] = jnp.zeros_like(packed)
    packed[: 4 * TOPK, :block] = fields
    packed[...] = packed[...].T
    routing_ref[...] = packed[pl.ds(pl.multiple_of(tp * part, part), part), :].astype(BF)
    fetch[2].wait()
    fetch[3].wait()


def own_block(place, kv, expert_ids, router_probs, queries, out_weight, resid, n_exp, n_tp):
    rows, width = queries.shape
    heads = width // HEAD_DIMENSION
    part, model = resid.shape
    block = expert_ids.shape[0]
    vmem = pl.BlockSpec(memory_space=pltpu.VMEM)
    hbm = pl.BlockSpec(memory_space=pltpu.HBM)
    return pl.pallas_call(
        functools.partial(own_block_kernel, (n_exp, n_tp, heads, part)),
        out_shape=(
            jax.ShapeDtypeStruct((heads * rows, HEAD_DIMENSION), BF),
            jax.ShapeDtypeStruct((width, model), BF),
            jax.ShapeDtypeStruct((part, model), BF),
            jax.ShapeDtypeStruct((heads * rows, HEAD_DIMENSION), F32),
            jax.ShapeDtypeStruct((heads * rows, HEAD_DIMENSION), F32),
            jax.ShapeDtypeStruct((heads * rows, LANES), F32),
            jax.ShapeDtypeStruct((part, LANES), BF),
        ),
        in_specs=[pl.BlockSpec(memory_space=pltpu.SMEM), vmem] + [hbm] * 5,
        out_specs=(vmem,) * 7,
        scratch_shapes=[
            pltpu.VMEM((rows, 2 * HEAD_DIMENSION), BF),
            pltpu.VMEM((TOPK, block), jnp.int32),
            pltpu.VMEM((TOPK, block), F32),
            pltpu.VMEM((LANES, LANES), F32),
            pltpu.SemaphoreType.DMA((heads,)),
            pltpu.SemaphoreType.DMA((4,)),
        ],
        compiler_params=pltpu.CompilerParams(vmem_limit_bytes=20 * MIB),
        cost_estimate=pl.CostEstimate(
            flops=6 * rows * width * rows,
            bytes_accessed=2 * (rows * width + width * model + rows * model),
            transcendentals=rows * rows * heads,
        ),
        name="own_block",
    )(place, kv, *map(in_hbm, (expert_ids.T, router_probs.T, queries, out_weight, resid)))


def dot_columns(a, b):
    return lax.dot_general(a, b, (((0,), (0,)), ((), ())), preferred_element_type=F32)


def attention_kernel(sizes, place, *refs):
    n_ctx, n_exp, n_tp, heads, part = sizes
    rows = n_exp * n_tp * part
    kv_refs, refs = refs[: n_ctx - 1], refs[n_ctx - 1 :]
    q_ref, w_ref, resid_ref, out_ref, sum_ref, max_ref = refs[:6]
    base_ref, across_ref, other_ref = refs[6:9]
    k_all, v_all, att, att_rel = refs[9:]
    ctx, exp, tp = place[0], place[1], place[2]
    for i, kv_ref in enumerate(kv_refs):
        at = slice(i * rows, (i + 1) * rows)
        k_all[at, :] = kv_ref[:, :HEAD_DIMENSION]
        v_all[at, :HEAD_DIMENSION] = kv_ref[:, HEAD_DIMENSION:]
    v_all[:, HEAD_DIMENSION:] = jnp.ones(((n_ctx - 1) * rows, HEAD_DIMENSION), BF)
    piece = lax.broadcasted_iota(jnp.int32, (1, (n_ctx - 1) * rows), 1) // rows
    earlier = jnp.zeros_like(piece)
    for i, bits in enumerate(KV_ORDER):
        there = jnp.where(lax.bitwise_xor(ctx, bits) < ctx, 1, 0)
        earlier = earlier + jnp.where(piece == i, there, 0)
    allowed = earlier == 1
    scale = 1.0 / math.sqrt(HEAD_DIMENSION)
    s = jnp.where(allowed, dot_rows(q_ref[...], k_all[...]) * scale, -1e30)
    own_top = max_ref[...]
    top = jnp.maximum(own_top, jnp.max(s, axis=1, keepdims=True))
    keep = jnp.exp(own_top - top)
    out = jnp.dot(jnp.exp(s - top[:, :1]).astype(BF), v_all[...], preferred_element_type=F32)
    total = sum_ref[...] * keep + out[:, HEAD_DIMENSION:]
    out = out_ref[...] * keep + out[:, :HEAD_DIMENSION]
    att[...] = (out / total).astype(BF)
    for t in range(n_tp):
        for x in range(n_exp):
            owner = lax.rem(exp + x, n_exp) * n_tp + lax.rem(tp + t, n_tp)
            at = (t * n_exp + x) * part
            for h in range(heads):
                source = pl.ds(pl.multiple_of(h * rows + owner * part, part), part)
                columns = slice(h * HEAD_DIMENSION, (h + 1) * HEAD_DIMENSION)
                att_rel[at : at + part, columns] = att[source, :]
    projected = jnp.dot(att_rel[...], w_ref[...], preferred_element_type=F32)
    base_ref[...] = resid_ref[...].astype(F32) + projected[:part]
    across_ref[...] = projected[part : 2 * part].astype(BF)
    other_ref[...] = projected[2 * part :].astype(BF)


def attend_project(place, pieces, own, n_exp, n_tp):
    queries, out_weight, resid = own[:3]
    width, model = out_weight.shape
    n_ctx, heads = len(pieces) + 1, width // HEAD_DIMENSION
    rows = queries.shape[0] // heads
    part = resid.shape[0]
    vmem = pl.BlockSpec(memory_space=pltpu.VMEM)
    return pl.pallas_call(
        functools.partial(attention_kernel, (n_ctx, n_exp, n_tp, heads, part)),
        out_shape=(
            jax.ShapeDtypeStruct((part, model), F32),
            jax.ShapeDtypeStruct((part, model), BF),
            jax.ShapeDtypeStruct((2 * part, model), BF),
        ),
        in_specs=[pl.BlockSpec(memory_space=pltpu.SMEM)] + [vmem] * (n_ctx - 1 + len(own)),
        out_specs=(vmem,) * 3,
        scratch_shapes=[
            pltpu.VMEM(((n_ctx - 1) * rows, HEAD_DIMENSION), BF),
            pltpu.VMEM(((n_ctx - 1) * rows, 2 * HEAD_DIMENSION), BF),
            pltpu.VMEM((heads * rows, HEAD_DIMENSION), BF),
            pltpu.VMEM((rows, width), BF),
        ],
        compiler_params=pltpu.CompilerParams(vmem_limit_bytes=20 * MIB),
        cost_estimate=pl.CostEstimate(
            flops=2 * rows * width * (3 * (n_ctx - 1) * rows + model),
            bytes_accessed=2 * (rows * width + width * model + rows * model),
            transcendentals=rows * n_ctx * rows * heads,
        ),
        name="attend_project",
    )(place, *pieces, *own)


def expert_kernel(n_pieces, depth, experts, first_ref, *refs):
    pieces, (wg_hbm, wu_hbm, wd_hbm) = refs[:n_pieces], refs[n_pieces : n_pieces + 3]
    outs = refs[n_pieces + 3 : n_pieces + 9]
    x_all, packed, pick_all, scale_all, out_all, wgu, wd, act, sems = refs[n_pieces + 9 :]
    sides, tokens, model = x_all.shape
    slots = pick_all.shape[1] // experts
    _, _, halves, hidden, _ = wgu.shape
    blocks = n_pieces // (2 * sides)
    part = tokens // (2 * blocks)

    def gate_up_copies(e):
        slot, rows = lax.rem(e, depth), pl.ds(e * halves, halves)
        return (
            pltpu.make_async_copy(wg_hbm.at[rows], wgu.at[slot, 0], sems.at[0, slot]),
            pltpu.make_async_copy(wu_hbm.at[rows], wgu.at[slot, 1], sems.at[1, slot]),
        )

    def down_copies(e):
        slot, rows = lax.rem(e, depth), pl.ds(e * halves, halves)
        return (pltpu.make_async_copy(wd_hbm.at[rows], wd.at[slot], sems.at[2, slot]),)

    def start(copies):
        for copy in copies:
            copy.start()

    def wait(copies):
        for copy in copies:
            copy.wait()

    def of_expert(e):
        return pl.ds(pl.multiple_of(e * slots, slots), slots)

    def gate_up(e):
        x = jnp.concatenate([out_all[side, of_expert(e), :] for side in range(sides)])
        weight = wgu[lax.rem(e, depth)].reshape(2 * halves * hidden, model)
        both = dot_rows(weight, x)
        gate, up = both[: halves * hidden], both[halves * hidden :]
        return (gate * jax.nn.sigmoid(gate) * up).astype(BF)

    def down(e):
        weight = wd[lax.rem(e, depth)].reshape(halves * hidden, model)
        out = dot_columns(act[lax.rem(e, 2)], weight)
        scale = jnp.concatenate([scale_all[side, of_expert(e), :] for side in range(sides)])
        return (out * scale).astype(BF)

    def keep(e, out):
        for side in range(sides):
            out_all[side, of_expert(e), :] = out[side * slots : (side + 1) * slots]

    for e in range(depth - 1):
        start(gate_up_copies(e))
        if e:
            start(down_copies(e - 1))
    for i, piece in enumerate(pieces):
        core, side, block = i // (sides * blocks), i // blocks % sides, i % blocks
        rows = slice((core * blocks + block) * part, (core * blocks + block + 1) * part)
        x_all[side, rows, :] = piece[:, :model]
        packed[side, rows, :] = piece[:, model:].astype(F32)
    slot = lax.broadcasted_iota(jnp.int32, (slots, tokens), 0)
    token = lax.broadcasted_iota(jnp.int32, (TOPK, tokens), 1)
    offset = lax.rem(token // part, blocks) * (slots // blocks)
    @pl.loop(0, sides)
    def _(side):
        fields = packed[side].T
        ids, ranks = fields[:TOPK].astype(jnp.int32), fields[TOPK : 2 * TOPK]
        gates = fields[2 * TOPK : 3 * TOPK] + fields[3 * TOPK : 4 * TOPK]
        places = ranks.astype(jnp.int32) + offset
        for e in range(experts):
            hit = ids == first_ref[0] + e
            chosen = slot == jnp.max(jnp.where(hit, places, -1), axis=0, keepdims=True)
            gate = jnp.sum(jnp.where(hit, gates, 0.0), axis=0, keepdims=True)
            here = slice(e * slots, (e + 1) * slots)
            pick_all[side, here, :] = jnp.where(chosen, 1.0, 0.0).astype(BF)
            scale_all[side, here, :] = jnp.sum(
                jnp.where(chosen, gate, 0.0), axis=1, keepdims=True
            )
        out_all[side] = jnp.dot(
            pick_all[side], x_all[side], preferred_element_type=F32
        ).astype(BF)
    wait(gate_up_copies(0))
    act[0] = gate_up(0)

    @pl.loop(0, experts - 1)
    def _(e):
        @pl.when(e + depth - 1 < experts)
        def _():
            start(gate_up_copies(e + depth - 1))

        @pl.when(e + depth - 2 < experts)
        def _():
            start(down_copies(e + depth - 2))

        wait(down_copies(e))
        wait(gate_up_copies(e + 1))
        following = gate_up(e + 1)
        out = down(e)
        act[lax.rem(e + 1, 2)] = following
        keep(e, out)

    wait(down_copies(experts - 1))
    keep(experts - 1, down(experts - 1))
    half = blocks * part // 2
    for side in (1, 0):
        routed = dot_columns(pick_all[side], out_all[side]).astype(BF)
        for core in range(2):
            near, far = routed[2 * core * half :][:half], routed[(2 * core + 1) * half :][:half]
            outs[3 * core + 1 - side][...] = far
            outs[3 * core + 2][(1 - side) * half : (2 - side) * half, :] = near


def cube_experts(first, pieces, w_gate, w_up, w_down, slots):
    rows, hidden, model = w_down.shape
    halves, sides = 2, 2
    experts = rows // halves
    tokens = len(pieces) * pieces[0].shape[0] // sides
    depth = 4
    vmem = pl.BlockSpec(memory_space=pltpu.VMEM)
    hbm = pl.BlockSpec(memory_space=pltpu.HBM)

    half = jax.ShapeDtypeStruct((tokens // 4, model), BF)
    whole = jax.ShapeDtypeStruct((tokens // 2, model), BF)
    return pl.pallas_call(
        functools.partial(expert_kernel, len(pieces), depth, experts),
        out_shape=(half, half, whole) * 2,
        in_specs=[pl.BlockSpec(memory_space=pltpu.SMEM)] + [vmem] * len(pieces) + [hbm] * 3,
        out_specs=(vmem,) * 6,
        scratch_shapes=[
            pltpu.VMEM((sides, tokens, model), BF),
            pltpu.VMEM((sides, tokens, LANES), F32),
            pltpu.VMEM((sides, experts * slots, tokens), BF),
            pltpu.VMEM((sides, experts * slots, 1), F32),
            pltpu.VMEM((sides, experts * slots, model), BF),
            pltpu.VMEM((depth, 2, halves, hidden, model), BF),
            pltpu.VMEM((depth, halves, hidden, model), BF),
            pltpu.VMEM((2, halves * hidden, sides * slots), BF),
            pltpu.SemaphoreType.DMA((3, depth)),
        ],
        compiler_params=pltpu.CompilerParams(vmem_limit_bytes=44 * MIB),
        cost_estimate=pl.CostEstimate(
            flops=2 * experts * sides * slots * model * (3 * halves * hidden + 2 * tokens),
            bytes_accessed=6 * rows * model * hidden + 4 * tokens * model,
            transcendentals=experts * sides * slots * halves * hidden,
        ),
        name="experts",
    )(
        first,
        *pieces,
        in_hbm(jnp.swapaxes(w_gate, 1, 2)),
        in_hbm(jnp.swapaxes(w_up, 1, 2)),
        in_hbm(w_down),
    )


def sums_back(mine, other, part):
    def add(a, *others):
        total = a.astype(F32)
        for b in others:
            total = total + b.astype(F32)
        return total.astype(BF)

    sums = [add(a, flip(b, "tp", 1)) for a, b in zip(mine, other)]
    sums[1], sums[2] = lax.optimization_barrier((sums[1], sums[2]))
    sums = [[x[at : at + part] for at in range(0, x.shape[0], part)] for x in sums]
    across = sums[2][:2] + sums[0]
    here = sums[2][2:] + sums[1]
    far_across = flip(across[2], "exp", 1)
    last_across = flip_both(across[3])
    last = flip(here[3], "ctx", 1)
    own = flip(across[0], "exp", 1)
    near = flip(here[1], "ctx", 1)
    near_across = flip_both(across[1])
    far = flip(add(here[2], last_across, far_across, last), "ctx", 2)
    total = here[0].astype(F32)
    for term in (far, near, near_across, own):
        total = total + term.astype(F32)
    return total


def on_device(
    queries, keys, values, out_weight, resid, expert_ids, router_probs, w_gate, w_up, w_down
):
    n_ctx, n_exp, n_tp = (lax.axis_size(a) for a in ("ctx", "exp", "tp"))
    part = resid.shape[0]
    rows_here = w_gate.shape[0]
    block = expert_ids.shape[0]
    cube = (n_ctx, n_exp, n_tp) == (4, 2, 2) and block == n_tp * part <= LANES
    if not cube or part % 16 or rows_here * n_ctx * n_exp != 2 * EXPERTS:
        return on_device_any_size(
            queries, keys, values, out_weight, resid, expert_ids, router_probs, w_gate, w_up, w_down
        )
    ctx, exp, tp = (lax.axis_index(a) for a in ("ctx", "exp", "tp"))
    place = jnp.stack([ctx, exp, tp]).astype(jnp.int32)
    heads_here = queries.shape[1] // HEAD_DIMENSION
    first = (ctx * n_exp + exp) * rows_here // 2
    slots = n_ctx * min(8, block)

    shared = (exp * n_tp + tp) * heads_here // (QUERY_HEADS // KEY_VALUE_HEADS)
    key_head = lax.dynamic_slice_in_dim(keys, shared * HEAD_DIMENSION, HEAD_DIMENSION, 1)
    value_head = lax.dynamic_slice_in_dim(values, shared * HEAD_DIMENSION, HEAD_DIMENSION, 1)
    kv = jnp.concatenate([key_head, value_head], axis=1)
    kv_pieces = [from_earlier(kv, "ctx", bits) for bits in KV_ORDER]
    *own, routing = own_block(
        place, kv, expert_ids, router_probs, queries, out_weight, resid, n_exp, n_tp
    )
    base, across, other = attend_project(place, kv_pieces, own, n_exp, n_tp)

    other = flip(other, "tp", 1).astype(F32)
    across = flip((across.astype(F32) + other[part:]).astype(BF), "exp", 1)
    hidden = base + other[:part] + across.astype(F32)
    mean_square = jnp.mean(hidden * hidden, axis=1, keepdims=True)
    normed = (hidden * lax.rsqrt(mean_square + 1e-06)).astype(BF)
    normed = jnp.concatenate([normed, routing], axis=1)

    far = flip(normed, "ctx", 2)
    across = flip(normed, "exp", 1)
    near = flip(normed, "ctx", 1)
    near_across = flip_both(normed)
    far_across = flip(far, "exp", 1)
    last_across = flip_both(far)
    last = flip(far, "ctx", 1)
    early = lax.optimization_barrier((normed, near, far, across, near_across))
    late = lax.optimization_barrier((far_across, last_across, last))
    pieces = [normed, near, far, last, across, near_across, far_across, last_across]
    pieces += [flip(piece, "tp", 1) for piece in early[:3] + late[2:] + early[3:] + late[:2]]
    sums = cube_experts(
        first.astype(jnp.int32).reshape(1), pieces, w_gate, w_up, w_down, slots
    )
    return (hidden + sums_back(sums[:3], sums[3:], part)).astype(BF)


def solution(mesh):
    in_specs = (
        P(("groups", "ctx"), ("exp", "tp")),
        P(("groups", "ctx"), None),
        P(("groups", "ctx"), None),
        P(("exp", "tp"), None),
        P(("groups", "ctx", "exp", "tp"), None),
        P(("groups", "ctx", "exp"), None),
        P(("groups", "ctx", "exp"), None),
        P(("ctx", "exp"), None, "tp"),
        P(("ctx", "exp"), None, "tp"),
        P(("ctx", "exp"), "tp", None),
    )
    out_specs = P(("groups", "ctx", "exp", "tp"), None)
    return jax.shard_map(
        on_device, mesh=mesh, in_specs=in_specs, out_specs=out_specs, check_vma=False
    )
```

```python
import functools
import math

import jax
import jax.numpy as jnp
from jax import lax
from jax.experimental import pallas as pl
from jax.experimental.pallas import tpu as pltpu
from jax.sharding import PartitionSpec as P

HEAD_DIMENSION = 128
QUERY_HEADS = 32
KEY_VALUE_HEADS = 4
EXPERTS = 64
TOPK = 8
MIB = 1 << 20
LANES = 128
BF = jnp.bfloat16
F32 = jnp.float32


def attend_blocks(blocks, key_head, value_head, heads_here):
    score_scale = 1.0 / math.sqrt(HEAD_DIMENSION)

    def make_state(query_rows):
        row_total = query_rows.shape[0]
        return (
            jnp.full((row_total, heads_here), -1e30, jnp.float32),
            jnp.zeros((row_total, heads_here), jnp.float32),
            jnp.zeros((row_total, heads_here, HEAD_DIMENSION), jnp.float32),
        )

    initial = tuple((make_state(query_rows) for query_rows, query_places in blocks))

    def fold_keys(carry, piece, first):
        key_piece, value_piece = piece
        key_places = jnp.arange(key_piece.shape[0], dtype=jnp.int32)
        updated = []
        for (query_rows, query_places), state in zip(blocks, carry):

            def refresh(state, query_rows=query_rows, query_places=query_places):
                running_max, running_sum, accum = state
                shaped = query_rows.reshape(query_rows.shape[0], heads_here, HEAD_DIMENSION)
                scores = (
                    jnp.einsum("qhd,kd->qhk", shaped, key_piece, preferred_element_type=jnp.float32)
                    * score_scale
                )
                allowed = key_places[None, None, :] <= query_places[:, None, None]
                scores = jnp.where(allowed, scores, -1e30)
                new_max = jnp.maximum(running_max, jnp.max(scores, axis=2))
                weights = jnp.where(allowed, jnp.exp(scores - new_max[:, :, None]), 0.0)
                running_sum = jnp.sum(weights, axis=2)
                accum = jnp.einsum(
                    "qhk,kd->qhd",
                    weights,
                    value_piece.astype(jnp.float32),
                    precision=lax.Precision.HIGHEST,
                )
                return (new_max, running_sum, accum)

            needed = first <= query_places[-1]
            updated.append(lax.cond(needed, refresh, lambda state: state, state))
        return tuple(updated)

    final = fold_keys(
        initial,
        (
            lax.all_gather(key_head, "ctx", axis=0, tiled=True),
            lax.all_gather(value_head, "ctx", axis=0, tiled=True),
        ),
        jnp.int32(0),
    )
    results = []
    for (query_rows, query_places), state in zip(blocks, final):
        running_max, running_sum, accum = state
        results.append(
            (accum / running_sum[:, :, None])
            .reshape(query_rows.shape[0], heads_here * HEAD_DIMENSION)
            .astype(jnp.bfloat16)
        )
    return results


def run_experts(inputs, w_gate, w_up, w_down):
    gate_out = jnp.einsum("rnd,rdf->rnf", inputs, w_gate, preferred_element_type=jnp.float32)
    up_out = jnp.einsum("rnd,rdf->rnf", inputs, w_up, preferred_element_type=jnp.float32)
    activated = (jax.nn.silu(gate_out) * up_out).astype(jnp.bfloat16)
    return jnp.einsum("rnf,rfd->rnd", activated, w_down, preferred_element_type=jnp.float32).astype(
        jnp.bfloat16
    )


def on_device_any_size(
    queries, keys, values, out_weight, resid, expert_ids, router_probs, w_gate, w_up, w_down
):
    rows_ctx = queries.shape[0]
    heads_here = queries.shape[1] // HEAD_DIMENSION
    group_width = QUERY_HEADS // KEY_VALUE_HEADS
    head_rank = lax.axis_index(("exp", "tp"))
    shared = head_rank * heads_here // group_width
    key_head = lax.dynamic_slice_in_dim(keys, shared * HEAD_DIMENSION, HEAD_DIMENSION, 1)
    value_head = lax.dynamic_slice_in_dim(values, shared * HEAD_DIMENSION, HEAD_DIMENSION, 1)
    cycle_rank = lax.axis_index("ctx")
    own_places = cycle_rank * rows_ctx + jnp.arange(rows_ctx, dtype=jnp.int32)
    attended = attend_blocks([(queries, own_places)], key_head, value_head, heads_here)[0]
    projected = lax.psum_scatter(
        jnp.dot(attended, out_weight, preferred_element_type=jnp.float32).astype(jnp.bfloat16),
        ("exp", "tp"),
        scatter_dimension=0,
        tiled=True,
    ).astype(jnp.float32)
    hidden = resid.astype(jnp.float32) + projected
    mean_square = jnp.mean(hidden * hidden, axis=1, keepdims=True)
    normed = (hidden * lax.rsqrt(mean_square + 1e-06)).astype(jnp.bfloat16)
    pair_rows = lax.all_gather(normed, "tp", axis=0, tiled=True)
    slot_count = min(8, expert_ids.shape[0])
    gate_weights = router_probs / jnp.sum(router_probs, axis=1, keepdims=True)
    flat_ids = expert_ids.reshape(-1)
    assigned = flat_ids.shape[0]
    onehot = (flat_ids[:, None] == jnp.arange(EXPERTS, dtype=jnp.int32)[None, :]).astype(jnp.int32)
    slots = jnp.sum(onehot * (jnp.cumsum(onehot, axis=0) - 1), axis=1)
    token_of = jnp.arange(assigned, dtype=jnp.int32) // TOPK
    peer_count = lax.axis_size(("ctx", "exp"))
    rows_here = w_gate.shape[0]
    cell_parts = []
    for half_index in range(2):
        half_rows_id = 2 * flat_ids + half_index
        target = half_rows_id // rows_here
        local_row = half_rows_id % rows_here
        cell_parts.append((local_row * slot_count + slots) * peer_count + target)
    cells = jnp.concatenate(cell_parts)
    table = (
        jnp.full((rows_here * slot_count * peer_count,), -1, jnp.int32)
        .at[cells]
        .set(jnp.concatenate([token_of, token_of]))
    )
    send_buffer = jnp.where(
        table[:, None] >= 0, pair_rows[jnp.maximum(table, 0)], jnp.zeros((), jnp.bfloat16)
    )
    model_width = pair_rows.shape[1]
    received = lax.all_to_all(
        send_buffer.reshape(rows_here * slot_count, peer_count, model_width),
        ("ctx", "exp"),
        split_axis=1,
        concat_axis=1,
        tiled=True,
    )
    expert_out = run_experts(
        received.reshape(rows_here, slot_count * peer_count, model_width), w_gate, w_up, w_down
    )
    returned = lax.all_to_all(
        expert_out.reshape(rows_here * slot_count, peer_count, model_width),
        ("ctx", "exp"),
        split_axis=1,
        concat_axis=1,
        tiled=True,
    )
    returned_flat = returned.reshape(rows_here * slot_count * peer_count, model_width)
    gathered = returned_flat[cells].reshape(2, expert_ids.shape[0], TOPK, model_width)
    routed_part = jnp.einsum(
        "hakd,ak->ad", gathered.astype(jnp.float32), gate_weights, precision=lax.Precision.HIGHEST
    )
    routed = lax.psum_scatter(
        routed_part.astype(jnp.bfloat16), "tp", scatter_dimension=0, tiled=True
    ).astype(jnp.float32)
    return (hidden + routed).astype(jnp.bfloat16)


def flip(x, axis, bit):
    return lax.ppermute(x, axis, [(i, i ^ bit) for i in range(lax.axis_size(axis))])


def flip_both(x):
    n_exp = lax.axis_size("exp")
    mask = n_exp + 1
    size = lax.axis_size("ctx") * n_exp
    return lax.ppermute(x, ("ctx", "exp"), [(i, i ^ mask) for i in range(size)])


def in_hbm(x):
    return pltpu.with_memory_space_constraint(x, pltpu.HBM)


def dot_rows(a, b):
    return lax.dot_general(a, b, (((1,), (1,)), ((), ())), preferred_element_type=F32)


KV_ORDER = (1, 2, 3)


def own_block_kernel(sizes, place, kv_ref, ids_hbm, probs_hbm, q_hbm, w_hbm, resid_hbm, *refs):
    n_exp, n_tp, heads, part = sizes
    rows = n_exp * n_tp * part
    q_ref, w_ref, resid_ref, out_ref, sum_ref, max_ref, routing_ref = refs[:7]
    v_ext, ids_ref, probs_ref, packed, q_sem, sems = refs[7:]
    fetch = [
        pltpu.make_async_copy(ids_hbm, ids_ref, sems.at[0]),
        pltpu.make_async_copy(probs_hbm, probs_ref, sems.at[1]),
        pltpu.make_async_copy(resid_hbm, resid_ref, sems.at[2]),
        pltpu.make_async_copy(w_hbm, w_ref, sems.at[3]),
    ]
    fetch_q = []
    for h in range(heads):
        columns = slice(h * HEAD_DIMENSION, (h + 1) * HEAD_DIMENSION)
        fetch_q.append(
            pltpu.make_async_copy(
                q_hbm.at[:, columns], q_ref.at[pl.ds(h * rows, rows)], q_sem.at[h]
            )
        )
        fetch_q[h].start()
    for copy in fetch:
        copy.start()
    tp = place[2]
    v_ext[:, :HEAD_DIMENSION] = kv_ref[:, HEAD_DIMENSION:]
    v_ext[:, HEAD_DIMENSION:] = jnp.ones((rows, HEAD_DIMENSION), BF)
    keys = kv_ref[:, :HEAD_DIMENSION]
    column = lax.broadcasted_iota(jnp.int32, (rows, rows), 1)
    allowed = column <= lax.broadcasted_iota(jnp.int32, (rows, rows), 0)
    scale = 1.0 / math.sqrt(HEAD_DIMENSION)
    for copy in fetch_q:
        copy.wait()
    s = dot_rows(q_ref[...], keys).reshape(heads, rows, rows)
    s = jnp.where(allowed, s * scale, -1e30).reshape(heads * rows, rows)
    top = jnp.max(s, axis=1, keepdims=True)
    out = jnp.dot(jnp.exp(s - top).astype(BF), v_ext[...], preferred_element_type=F32)
    out_ref[...] = out[:, :HEAD_DIMENSION]
    sum_ref[...] = out[:, HEAD_DIMENSION:]
    max_ref[...] = jnp.broadcast_to(top, max_ref.shape)

    fetch[0].wait()
    fetch[1].wait()
    block = n_tp * part
    ids = ids_ref[...]
    probs = probs_ref[...]
    expert = lax.broadcasted_iota(jnp.int32, (EXPERTS, block), 0)
    named = jnp.zeros((EXPERTS, block), F32)
    for k in range(TOPK):
        named = named + jnp.where(expert == ids[k : k + 1, :], 1.0, 0.0)
    before = lax.broadcasted_iota(jnp.int32, (block, block), 0) < lax.broadcasted_iota(
        jnp.int32, (block, block), 1
    )
    count = jnp.dot(
        named.astype(BF), jnp.where(before, 1.0, 0.0).astype(BF), preferred_element_type=F32
    )
    ranks = [
        jnp.sum(jnp.where(expert == ids[k : k + 1, :], count, 0.0), axis=0, keepdims=True)
        for k in range(TOPK)
    ]
    gates = probs / jnp.sum(probs, axis=0, keepdims=True)
    high = gates.astype(BF).astype(F32)
    fields = jnp.concatenate([ids.astype(F32)] + ranks + [high, gates - high], axis=0)
    packed[...] = jnp.zeros_like(packed)
    packed[: 4 * TOPK, :block] = fields
    packed[...] = packed[...].T
    routing_ref[...] = packed[pl.ds(pl.multiple_of(tp * part, part), part), :].astype(BF)
    fetch[2].wait()
    fetch[3].wait()


def own_block(place, kv, expert_ids, router_probs, queries, out_weight, resid, n_exp, n_tp):
    rows, width = queries.shape
    heads = width // HEAD_DIMENSION
    part, model = resid.shape
    block = expert_ids.shape[0]
    vmem = pl.BlockSpec(memory_space=pltpu.VMEM)
    hbm = pl.BlockSpec(memory_space=pltpu.HBM)
    return pl.pallas_call(
        functools.partial(own_block_kernel, (n_exp, n_tp, heads, part)),
        out_shape=(
            jax.ShapeDtypeStruct((heads * rows, HEAD_DIMENSION), BF),
            jax.ShapeDtypeStruct((width, model), BF),
            jax.ShapeDtypeStruct((part, model), BF),
            jax.ShapeDtypeStruct((heads * rows, HEAD_DIMENSION), F32),
            jax.ShapeDtypeStruct((heads * rows, HEAD_DIMENSION), F32),
            jax.ShapeDtypeStruct((heads * rows, LANES), F32),
            jax.ShapeDtypeStruct((part, LANES), BF),
        ),
        in_specs=[pl.BlockSpec(memory_space=pltpu.SMEM), vmem] + [hbm] * 5,
        out_specs=(vmem,) * 7,
        scratch_shapes=[
            pltpu.VMEM((rows, 2 * HEAD_DIMENSION), BF),
            pltpu.VMEM((TOPK, block), jnp.int32),
            pltpu.VMEM((TOPK, block), F32),
            pltpu.VMEM((LANES, LANES), F32),
            pltpu.SemaphoreType.DMA((heads,)),
            pltpu.SemaphoreType.DMA((4,)),
        ],
        compiler_params=pltpu.CompilerParams(vmem_limit_bytes=20 * MIB),
        cost_estimate=pl.CostEstimate(
            flops=6 * rows * width * rows,
            bytes_accessed=2 * (rows * width + width * model + rows * model),
            transcendentals=rows * rows * heads,
        ),
        name="own_block",
    )(place, kv, *map(in_hbm, (expert_ids.T, router_probs.T, queries, out_weight, resid)))


def dot_columns(a, b):
    return lax.dot_general(a, b, (((0,), (0,)), ((), ())), preferred_element_type=F32)


def attention_kernel(sizes, place, *refs):
    n_ctx, n_exp, n_tp, heads, part = sizes
    rows = n_exp * n_tp * part
    kv_refs, refs = refs[: n_ctx - 1], refs[n_ctx - 1 :]
    q_ref, w_ref, resid_ref, out_ref, sum_ref, max_ref = refs[:6]
    base_ref, across_ref, other_ref = refs[6:9]
    k_all, v_all, att, att_rel = refs[9:]
    ctx, exp, tp = place[0], place[1], place[2]
    for i, kv_ref in enumerate(kv_refs):
        at = slice(i * rows, (i + 1) * rows)
        k_all[at, :] = kv_ref[:, :HEAD_DIMENSION]
        v_all[at, :HEAD_DIMENSION] = kv_ref[:, HEAD_DIMENSION:]
    v_all[:, HEAD_DIMENSION:] = jnp.ones(((n_ctx - 1) * rows, HEAD_DIMENSION), BF)
    piece = lax.broadcasted_iota(jnp.int32, (1, (n_ctx - 1) * rows), 1) // rows
    earlier = jnp.zeros_like(piece)
    for i, bits in enumerate(KV_ORDER):
        there = jnp.where(lax.bitwise_xor(ctx, bits) < ctx, 1, 0)
        earlier = earlier + jnp.where(piece == i, there, 0)
    allowed = earlier == 1
    scale = 1.0 / math.sqrt(HEAD_DIMENSION)
    s = jnp.where(allowed, dot_rows(q_ref[...], k_all[...]) * scale, -1e30)
    own_top = max_ref[...]
    top = jnp.maximum(own_top, jnp.max(s, axis=1, keepdims=True))
    keep = jnp.exp(own_top - top)
    out = jnp.dot(jnp.exp(s - top[:, :1]).astype(BF), v_all[...], preferred_element_type=F32)
    total = sum_ref[...] * keep + out[:, HEAD_DIMENSION:]
    out = out_ref[...] * keep + out[:, :HEAD_DIMENSION]
    att[...] = (out / total).astype(BF)
    for t in range(n_tp):
        for x in range(n_exp):
            owner = lax.rem(exp + x, n_exp) * n_tp + lax.rem(tp + t, n_tp)
            at = (t * n_exp + x) * part
            for h in range(heads):
                source = pl.ds(pl.multiple_of(h * rows + owner * part, part), part)
                columns = slice(h * HEAD_DIMENSION, (h + 1) * HEAD_DIMENSION)
                att_rel[at : at + part, columns] = att[source, :]
    projected = jnp.dot(att_rel[...], w_ref[...], preferred_element_type=F32)
    base_ref[...] = resid_ref[...].astype(F32) + projected[:part]
    across_ref[...] = projected[part : 2 * part].astype(BF)
    other_ref[...] = projected[2 * part :].astype(BF)


def attend_project(place, pieces, own, n_exp, n_tp):
    queries, out_weight, resid = own[:3]
    width, model = out_weight.shape
    n_ctx, heads = len(pieces) + 1, width // HEAD_DIMENSION
    rows = queries.shape[0] // heads
    part = resid.shape[0]
    vmem = pl.BlockSpec(memory_space=pltpu.VMEM)
    return pl.pallas_call(
        functools.partial(attention_kernel, (n_ctx, n_exp, n_tp, heads, part)),
        out_shape=(
            jax.ShapeDtypeStruct((part, model), F32),
            jax.ShapeDtypeStruct((part, model), BF),
            jax.ShapeDtypeStruct((2 * part, model), BF),
        ),
        in_specs=[pl.BlockSpec(memory_space=pltpu.SMEM)] + [vmem] * (n_ctx - 1 + len(own)),
        out_specs=(vmem,) * 3,
        scratch_shapes=[
            pltpu.VMEM(((n_ctx - 1) * rows, HEAD_DIMENSION), BF),
            pltpu.VMEM(((n_ctx - 1) * rows, 2 * HEAD_DIMENSION), BF),
            pltpu.VMEM((heads * rows, HEAD_DIMENSION), BF),
            pltpu.VMEM((rows, width), BF),
        ],
        compiler_params=pltpu.CompilerParams(vmem_limit_bytes=20 * MIB),
        cost_estimate=pl.CostEstimate(
            flops=2 * rows * width * (3 * (n_ctx - 1) * rows + model),
            bytes_accessed=2 * (rows * width + width * model + rows * model),
            transcendentals=rows * n_ctx * rows * heads,
        ),
        name="attend_project",
    )(place, *pieces, *own)


def expert_kernel(n_pieces, depth, experts, first_ref, *refs):
    pieces, (wg_hbm, wu_hbm, wd_hbm) = refs[:n_pieces], refs[n_pieces : n_pieces + 3]
    outs = refs[n_pieces + 3 : n_pieces + 9]
    x_all, packed, pick_all, scale_all, out_all, wgu, wd, act, sems = refs[n_pieces + 9 :]
    sides, tokens, model = x_all.shape
    slots = pick_all.shape[1] // experts
    _, _, halves, hidden, _ = wgu.shape
    blocks = n_pieces // (2 * sides)
    part = tokens // (2 * blocks)

    def gate_up_copies(e):
        slot, rows = lax.rem(e, depth), pl.ds(e * halves, halves)
        return (
            pltpu.make_async_copy(wg_hbm.at[rows], wgu.at[slot, 0], sems.at[0, slot]),
            pltpu.make_async_copy(wu_hbm.at[rows], wgu.at[slot, 1], sems.at[1, slot]),
        )

    def down_copies(e):
        slot, rows = lax.rem(e, depth), pl.ds(e * halves, halves)
        return (pltpu.make_async_copy(wd_hbm.at[rows], wd.at[slot], sems.at[2, slot]),)

    def start(copies):
        for copy in copies:
            copy.start()

    def wait(copies):
        for copy in copies:
            copy.wait()

    def of_expert(e):
        return pl.ds(pl.multiple_of(e * slots, slots), slots)

    def gate_up(e):
        x = jnp.concatenate([out_all[side, of_expert(e), :] for side in range(sides)])
        weight = wgu[lax.rem(e, depth)].reshape(2 * halves * hidden, model)
        both = dot_rows(weight, x)
        gate, up = both[: halves * hidden], both[halves * hidden :]
        return (gate * jax.nn.sigmoid(gate) * up).astype(BF)

    def down(e):
        weight = wd[lax.rem(e, depth)].reshape(halves * hidden, model)
        out = dot_columns(act[lax.rem(e, 2)], weight)
        scale = jnp.concatenate([scale_all[side, of_expert(e), :] for side in range(sides)])
        return (out * scale).astype(BF)

    def keep(e, out):
        for side in range(sides):
            out_all[side, of_expert(e), :] = out[side * slots : (side + 1) * slots]

    for e in range(depth - 1):
        start(gate_up_copies(e))
        if e:
            start(down_copies(e - 1))
    for i, piece in enumerate(pieces):
        core, side, block = i // (sides * blocks), i // blocks % sides, i % blocks
        rows = slice((core * blocks + block) * part, (core * blocks + block + 1) * part)
        x_all[side, rows, :] = piece[:, :model]
        packed[side, rows, :] = piece[:, model:].astype(F32)
    slot = lax.broadcasted_iota(jnp.int32, (slots, tokens), 0)
    token = lax.broadcasted_iota(jnp.int32, (TOPK, tokens), 1)
    offset = lax.rem(token // part, blocks) * (slots // blocks)
    @pl.loop(0, sides)
    def _(side):
        fields = packed[side].T
        ids, ranks = fields[:TOPK].astype(jnp.int32), fields[TOPK : 2 * TOPK]
        gates = fields[2 * TOPK : 3 * TOPK] + fields[3 * TOPK : 4 * TOPK]
        places = ranks.astype(jnp.int32) + offset
        for e in range(experts):
            hit = ids == first_ref[0] + e
            chosen = slot == jnp.max(jnp.where(hit, places, -1), axis=0, keepdims=True)
            gate = jnp.sum(jnp.where(hit, gates, 0.0), axis=0, keepdims=True)
            here = slice(e * slots, (e + 1) * slots)
            pick_all[side, here, :] = jnp.where(chosen, 1.0, 0.0).astype(BF)
            scale_all[side, here, :] = jnp.sum(
                jnp.where(chosen, gate, 0.0), axis=1, keepdims=True
            )
        out_all[side] = jnp.dot(
            pick_all[side], x_all[side], preferred_element_type=F32
        ).astype(BF)
    wait(gate_up_copies(0))
    act[0] = gate_up(0)

    @pl.loop(0, experts - 1)
    def _(e):
        @pl.when(e + depth - 1 < experts)
        def _():
            start(gate_up_copies(e + depth - 1))

        @pl.when(e + depth - 2 < experts)
        def _():
            start(down_copies(e + depth - 2))

        wait(down_copies(e))
        wait(gate_up_copies(e + 1))
        following = gate_up(e + 1)
        out = down(e)
        act[lax.rem(e + 1, 2)] = following
        keep(e, out)

    wait(down_copies(experts - 1))
    keep(experts - 1, down(experts - 1))
    half = blocks * part // 2
    for side in (1, 0):
        routed = dot_columns(pick_all[side], out_all[side]).astype(BF)
        for core in range(2):
            near, far = routed[2 * core * half :][:half], routed[(2 * core + 1) * half :][:half]
            outs[3 * core + 1 - side][...] = far
            outs[3 * core + 2][(1 - side) * half : (2 - side) * half, :] = near


def cube_experts(first, pieces, w_gate, w_up, w_down, slots):
    rows, hidden, model = w_down.shape
    halves, sides = 2, 2
    experts = rows // halves
    tokens = len(pieces) * pieces[0].shape[0] // sides
    depth = 4
    vmem = pl.BlockSpec(memory_space=pltpu.VMEM)
    hbm = pl.BlockSpec(memory_space=pltpu.HBM)

    half = jax.ShapeDtypeStruct((tokens // 4, model), BF)
    whole = jax.ShapeDtypeStruct((tokens // 2, model), BF)
    return pl.pallas_call(
        functools.partial(expert_kernel, len(pieces), depth, experts),
        out_shape=(half, half, whole) * 2,
        in_specs=[pl.BlockSpec(memory_space=pltpu.SMEM)] + [vmem] * len(pieces) + [hbm] * 3,
        out_specs=(vmem,) * 6,
        scratch_shapes=[
            pltpu.VMEM((sides, tokens, model), BF),
            pltpu.VMEM((sides, tokens, LANES), F32),
            pltpu.VMEM((sides, experts * slots, tokens), BF),
            pltpu.VMEM((sides, experts * slots, 1), F32),
            pltpu.VMEM((sides, experts * slots, model), BF),
            pltpu.VMEM((depth, 2, halves, hidden, model), BF),
            pltpu.VMEM((depth, halves, hidden, model), BF),
            pltpu.VMEM((2, halves * hidden, sides * slots), BF),
            pltpu.SemaphoreType.DMA((3, depth)),
        ],
        compiler_params=pltpu.CompilerParams(vmem_limit_bytes=44 * MIB),
        cost_estimate=pl.CostEstimate(
            flops=2 * experts * sides * slots * model * (3 * halves * hidden + 2 * tokens),
            bytes_accessed=6 * rows * model * hidden + 4 * tokens * model,
            transcendentals=experts * sides * slots * halves * hidden,
        ),
        name="experts",
    )(
        first,
        *pieces,
        in_hbm(jnp.swapaxes(w_gate, 1, 2)),
        in_hbm(jnp.swapaxes(w_up, 1, 2)),
        in_hbm(w_down),
    )


def sums_back(mine, other, part):
    def add(a, *others):
        total = a.astype(F32)
        for b in others:
            total = total + b.astype(F32)
        return total.astype(BF)

    sums = [add(a, flip(b, "tp", 1)) for a, b in zip(mine, other)]
    sums[1], sums[2] = lax.optimization_barrier((sums[1], sums[2]))
    sums = [[x[at : at + part] for at in range(0, x.shape[0], part)] for x in sums]
    across = sums[2][:2] + sums[0]
    here = sums[2][2:] + sums[1]
    far_across = flip(across[2], "exp", 1)
    last_across = flip_both(across[3])
    last = flip(here[3], "ctx", 1)
    own = flip(across[0], "exp", 1)
    near = flip(here[1], "ctx", 1)
    near_across = flip_both(across[1])
    far = flip(add(here[2], last_across, far_across, last), "ctx", 2)
    total = here[0].astype(F32)
    for term in (far, near, near_across, own):
        total = total + term.astype(F32)
    return total


def on_device(
    queries, keys, values, out_weight, resid, expert_ids, router_probs, w_gate, w_up, w_down
):
    n_ctx, n_exp, n_tp = (lax.axis_size(a) for a in ("ctx", "exp", "tp"))
    part = resid.shape[0]
    rows_here = w_gate.shape[0]
    block = expert_ids.shape[0]
    cube = (n_ctx, n_exp, n_tp) == (4, 2, 2) and block == n_tp * part <= LANES
    if not cube or part % 16 or rows_here * n_ctx * n_exp != 2 * EXPERTS:
        return on_device_any_size(
            queries, keys, values, out_weight, resid, expert_ids, router_probs, w_gate, w_up, w_down
        )
    ctx, exp, tp = (lax.axis_index(a) for a in ("ctx", "exp", "tp"))
    place = jnp.stack([ctx, exp, tp]).astype(jnp.int32)
    heads_here = queries.shape[1] // HEAD_DIMENSION
    first = (ctx * n_exp + exp) * rows_here // 2
    slots = n_ctx * min(8, block)

    shared = (exp * n_tp + tp) * heads_here // (QUERY_HEADS // KEY_VALUE_HEADS)
    key_head = lax.dynamic_slice_in_dim(keys, shared * HEAD_DIMENSION, HEAD_DIMENSION, 1)
    value_head = lax.dynamic_slice_in_dim(values, shared * HEAD_DIMENSION, HEAD_DIMENSION, 1)
    kv = jnp.concatenate([key_head, value_head], axis=1)
    kv_pieces = [flip(kv, "ctx", bits) for bits in KV_ORDER]
    *own, routing = own_block(
        place, kv, expert_ids, router_probs, queries, out_weight, resid, n_exp, n_tp
    )
    base, across, other = attend_project(place, kv_pieces, own, n_exp, n_tp)

    other = flip(other, "tp", 1).astype(F32)
    across = flip((across.astype(F32) + other[part:]).astype(BF), "exp", 1)
    hidden = base + other[:part] + across.astype(F32)
    mean_square = jnp.mean(hidden * hidden, axis=1, keepdims=True)
    normed = (hidden * lax.rsqrt(mean_square + 1e-06)).astype(BF)
    normed = jnp.concatenate([normed, routing], axis=1)

    far = flip(normed, "ctx", 2)
    across = flip(normed, "exp", 1)
    near = flip(normed, "ctx", 1)
    near_across = flip_both(normed)
    far_across = flip(far, "exp", 1)
    last_across = flip_both(far)
    last = flip(far, "ctx", 1)
    early = lax.optimization_barrier((normed, near, far, across, near_across))
    late = lax.optimization_barrier((far_across, last_across, last))
    pieces = [normed, near, far, last, across, near_across, far_across, last_across]
    pieces += [flip(piece, "tp", 1) for piece in early[:3] + late[2:] + early[3:] + late[:2]]
    sums = cube_experts(
        first.astype(jnp.int32).reshape(1), pieces, w_gate, w_up, w_down, slots
    )
    return (hidden + sums_back(sums[:3], sums[3:], part)).astype(BF)


def solution(mesh):
    in_specs = (
        P(("groups", "ctx"), ("exp", "tp")),
        P(("groups", "ctx"), None),
        P(("groups", "ctx"), None),
        P(("exp", "tp"), None),
        P(("groups", "ctx", "exp", "tp"), None),
        P(("groups", "ctx", "exp"), None),
        P(("groups", "ctx", "exp"), None),
        P(("ctx", "exp"), None, "tp"),
        P(("ctx", "exp"), None, "tp"),
        P(("ctx", "exp"), "tp", None),
    )
    out_specs = P(("groups", "ctx", "exp", "tp"), None)
    return jax.shard_map(
        on_device, mesh=mesh, in_specs=in_specs, out_specs=out_specs, check_vma=False
    )
```

```python
import functools
import math

import jax
import jax.numpy as jnp
from jax import lax
from jax.experimental import pallas as pl
from jax.experimental.pallas import tpu as pltpu
from jax.sharding import PartitionSpec as P

HEAD_DIMENSION = 128
QUERY_HEADS = 32
KEY_VALUE_HEADS = 4
EXPERTS = 64
TOPK = 8
MIB = 1 << 20
LANES = 128
BF = jnp.bfloat16
F32 = jnp.float32


def attend_blocks(blocks, key_head, value_head, heads_here):
    score_scale = 1.0 / math.sqrt(HEAD_DIMENSION)

    def make_state(query_rows):
        row_total = query_rows.shape[0]
        return (
            jnp.full((row_total, heads_here), -1e30, jnp.float32),
            jnp.zeros((row_total, heads_here), jnp.float32),
            jnp.zeros((row_total, heads_here, HEAD_DIMENSION), jnp.float32),
        )

    initial = tuple((make_state(query_rows) for query_rows, query_places in blocks))

    def fold_keys(carry, piece, first):
        key_piece, value_piece = piece
        key_places = jnp.arange(key_piece.shape[0], dtype=jnp.int32)
        updated = []
        for (query_rows, query_places), state in zip(blocks, carry):

            def refresh(state, query_rows=query_rows, query_places=query_places):
                running_max, running_sum, accum = state
                shaped = query_rows.reshape(query_rows.shape[0], heads_here, HEAD_DIMENSION)
                scores = (
                    jnp.einsum("qhd,kd->qhk", shaped, key_piece, preferred_element_type=jnp.float32)
                    * score_scale
                )
                allowed = key_places[None, None, :] <= query_places[:, None, None]
                scores = jnp.where(allowed, scores, -1e30)
                new_max = jnp.maximum(running_max, jnp.max(scores, axis=2))
                weights = jnp.where(allowed, jnp.exp(scores - new_max[:, :, None]), 0.0)
                running_sum = jnp.sum(weights, axis=2)
                accum = jnp.einsum(
                    "qhk,kd->qhd",
                    weights,
                    value_piece.astype(jnp.float32),
                    precision=lax.Precision.HIGHEST,
                )
                return (new_max, running_sum, accum)

            needed = first <= query_places[-1]
            updated.append(lax.cond(needed, refresh, lambda state: state, state))
        return tuple(updated)

    final = fold_keys(
        initial,
        (
            lax.all_gather(key_head, "ctx", axis=0, tiled=True),
            lax.all_gather(value_head, "ctx", axis=0, tiled=True),
        ),
        jnp.int32(0),
    )
    results = []
    for (query_rows, query_places), state in zip(blocks, final):
        running_max, running_sum, accum = state
        results.append(
            (accum / running_sum[:, :, None])
            .reshape(query_rows.shape[0], heads_here * HEAD_DIMENSION)
            .astype(jnp.bfloat16)
        )
    return results


def run_experts(inputs, w_gate, w_up, w_down):
    gate_out = jnp.einsum("rnd,rdf->rnf", inputs, w_gate, preferred_element_type=jnp.float32)
    up_out = jnp.einsum("rnd,rdf->rnf", inputs, w_up, preferred_element_type=jnp.float32)
    activated = (jax.nn.silu(gate_out) * up_out).astype(jnp.bfloat16)
    return jnp.einsum("rnf,rfd->rnd", activated, w_down, preferred_element_type=jnp.float32).astype(
        jnp.bfloat16
    )


def on_device_any_size(
    queries, keys, values, out_weight, resid, expert_ids, router_probs, w_gate, w_up, w_down
):
    rows_ctx = queries.shape[0]
    heads_here = queries.shape[1] // HEAD_DIMENSION
    group_width = QUERY_HEADS // KEY_VALUE_HEADS
    head_rank = lax.axis_index(("exp", "tp"))
    shared = head_rank * heads_here // group_width
    key_head = lax.dynamic_slice_in_dim(keys, shared * HEAD_DIMENSION, HEAD_DIMENSION, 1)
    value_head = lax.dynamic_slice_in_dim(values, shared * HEAD_DIMENSION, HEAD_DIMENSION, 1)
    cycle_rank = lax.axis_index("ctx")
    own_places = cycle_rank * rows_ctx + jnp.arange(rows_ctx, dtype=jnp.int32)
    attended = attend_blocks([(queries, own_places)], key_head, value_head, heads_here)[0]
    projected = lax.psum_scatter(
        jnp.dot(attended, out_weight, preferred_element_type=jnp.float32).astype(jnp.bfloat16),
        ("exp", "tp"),
        scatter_dimension=0,
        tiled=True,
    ).astype(jnp.float32)
    hidden = resid.astype(jnp.float32) + projected
    mean_square = jnp.mean(hidden * hidden, axis=1, keepdims=True)
    normed = (hidden * lax.rsqrt(mean_square + 1e-06)).astype(jnp.bfloat16)
    pair_rows = lax.all_gather(normed, "tp", axis=0, tiled=True)
    slot_count = min(8, expert_ids.shape[0])
    gate_weights = router_probs / jnp.sum(router_probs, axis=1, keepdims=True)
    flat_ids = expert_ids.reshape(-1)
    assigned = flat_ids.shape[0]
    onehot = (flat_ids[:, None] == jnp.arange(EXPERTS, dtype=jnp.int32)[None, :]).astype(jnp.int32)
    slots = jnp.sum(onehot * (jnp.cumsum(onehot, axis=0) - 1), axis=1)
    token_of = jnp.arange(assigned, dtype=jnp.int32) // TOPK
    peer_count = lax.axis_size(("ctx", "exp"))
    rows_here = w_gate.shape[0]
    cell_parts = []
    for half_index in range(2):
        half_rows_id = 2 * flat_ids + half_index
        target = half_rows_id // rows_here
        local_row = half_rows_id % rows_here
        cell_parts.append((local_row * slot_count + slots) * peer_count + target)
    cells = jnp.concatenate(cell_parts)
    table = (
        jnp.full((rows_here * slot_count * peer_count,), -1, jnp.int32)
        .at[cells]
        .set(jnp.concatenate([token_of, token_of]))
    )
    send_buffer = jnp.where(
        table[:, None] >= 0, pair_rows[jnp.maximum(table, 0)], jnp.zeros((), jnp.bfloat16)
    )
    model_width = pair_rows.shape[1]
    received = lax.all_to_all(
        send_buffer.reshape(rows_here * slot_count, peer_count, model_width),
        ("ctx", "exp"),
        split_axis=1,
        concat_axis=1,
        tiled=True,
    )
    expert_out = run_experts(
        received.reshape(rows_here, slot_count * peer_count, model_width), w_gate, w_up, w_down
    )
    returned = lax.all_to_all(
        expert_out.reshape(rows_here * slot_count, peer_count, model_width),
        ("ctx", "exp"),
        split_axis=1,
        concat_axis=1,
        tiled=True,
    )
    returned_flat = returned.reshape(rows_here * slot_count * peer_count, model_width)
    gathered = returned_flat[cells].reshape(2, expert_ids.shape[0], TOPK, model_width)
    routed_part = jnp.einsum(
        "hakd,ak->ad", gathered.astype(jnp.float32), gate_weights, precision=lax.Precision.HIGHEST
    )
    routed = lax.psum_scatter(
        routed_part.astype(jnp.bfloat16), "tp", scatter_dimension=0, tiled=True
    ).astype(jnp.float32)
    return (hidden + routed).astype(jnp.bfloat16)


def flip(x, axis, bit):
    return lax.ppermute(x, axis, [(i, i ^ bit) for i in range(lax.axis_size(axis))])


def flip_both(x):
    n_exp = lax.axis_size("exp")
    mask = n_exp + 1
    size = lax.axis_size("ctx") * n_exp
    return lax.ppermute(x, ("ctx", "exp"), [(i, i ^ mask) for i in range(size)])


def in_hbm(x):
    return pltpu.with_memory_space_constraint(x, pltpu.HBM)


def dot_rows(a, b):
    return lax.dot_general(a, b, (((1,), (1,)), ((), ())), preferred_element_type=F32)


KV_ORDER = (1, 2, 3)


def own_block_kernel(sizes, place, kv_ref, ids_hbm, probs_hbm, q_hbm, w_hbm, resid_hbm, *refs):
    n_exp, n_tp, heads, part = sizes
    rows = n_exp * n_tp * part
    q_ref, w_ref, resid_ref, out_ref, sum_ref, max_ref, routing_ref = refs[:7]
    v_ext, ids_ref, probs_ref, packed, q_sem, sems = refs[7:]
    fetch = [
        pltpu.make_async_copy(ids_hbm, ids_ref, sems.at[0]),
        pltpu.make_async_copy(probs_hbm, probs_ref, sems.at[1]),
        pltpu.make_async_copy(resid_hbm, resid_ref, sems.at[2]),
        pltpu.make_async_copy(w_hbm, w_ref, sems.at[3]),
    ]
    fetch_q = []
    for h in range(heads):
        columns = slice(h * HEAD_DIMENSION, (h + 1) * HEAD_DIMENSION)
        fetch_q.append(
            pltpu.make_async_copy(
                q_hbm.at[:, columns], q_ref.at[pl.ds(h * rows, rows)], q_sem.at[h]
            )
        )
        fetch_q[h].start()
    for copy in fetch:
        copy.start()
    tp = place[2]
    v_ext[:, :HEAD_DIMENSION] = kv_ref[:, HEAD_DIMENSION:]
    v_ext[:, HEAD_DIMENSION:] = jnp.ones((rows, HEAD_DIMENSION), BF)
    keys = kv_ref[:, :HEAD_DIMENSION]
    column = lax.broadcasted_iota(jnp.int32, (rows, rows), 1)
    allowed = column <= lax.broadcasted_iota(jnp.int32, (rows, rows), 0)
    scale = 1.0 / math.sqrt(HEAD_DIMENSION)
    for copy in fetch_q:
        copy.wait()
    s = dot_rows(q_ref[...], keys).reshape(heads, rows, rows)
    s = jnp.where(allowed, s * scale, -1e30).reshape(heads * rows, rows)
    top = jnp.max(s, axis=1, keepdims=True)
    out = jnp.dot(jnp.exp(s - top).astype(BF), v_ext[...], preferred_element_type=F32)
    out_ref[...] = out[:, :HEAD_DIMENSION]
    sum_ref[...] = out[:, HEAD_DIMENSION:]
    max_ref[...] = jnp.broadcast_to(top, max_ref.shape)

    fetch[0].wait()
    fetch[1].wait()
    block = n_tp * part
    ids = ids_ref[...]
    probs = probs_ref[...]
    expert = lax.broadcasted_iota(jnp.int32, (EXPERTS, block), 0)
    named = jnp.zeros((EXPERTS, block), F32)
    for k in range(TOPK):
        named = named + jnp.where(expert == ids[k : k + 1, :], 1.0, 0.0)
    before = lax.broadcasted_iota(jnp.int32, (block, block), 0) < lax.broadcasted_iota(
        jnp.int32, (block, block), 1
    )
    count = jnp.dot(
        named.astype(BF), jnp.where(before, 1.0, 0.0).astype(BF), preferred_element_type=F32
    )
    ranks = [
        jnp.sum(jnp.where(expert == ids[k : k + 1, :], count, 0.0), axis=0, keepdims=True)
        for k in range(TOPK)
    ]
    gates = probs / jnp.sum(probs, axis=0, keepdims=True)
    high = gates.astype(BF).astype(F32)
    fields = jnp.concatenate([ids.astype(F32)] + ranks + [high, gates - high], axis=0)
    packed[...] = jnp.zeros_like(packed)
    packed[: 4 * TOPK, :block] = fields
    packed[...] = packed[...].T
    routing_ref[...] = packed[pl.ds(pl.multiple_of(tp * part, part), part), :].astype(BF)
    fetch[2].wait()
    fetch[3].wait()


def own_block(place, kv, expert_ids, router_probs, queries, out_weight, resid, n_exp, n_tp):
    rows, width = queries.shape
    heads = width // HEAD_DIMENSION
    part, model = resid.shape
    block = expert_ids.shape[0]
    vmem = pl.BlockSpec(memory_space=pltpu.VMEM)
    hbm = pl.BlockSpec(memory_space=pltpu.HBM)
    return pl.pallas_call(
        functools.partial(own_block_kernel, (n_exp, n_tp, heads, part)),
        out_shape=(
            jax.ShapeDtypeStruct((heads * rows, HEAD_DIMENSION), BF),
            jax.ShapeDtypeStruct((width, model), BF),
            jax.ShapeDtypeStruct((part, model), BF),
            jax.ShapeDtypeStruct((heads * rows, HEAD_DIMENSION), F32),
            jax.ShapeDtypeStruct((heads * rows, HEAD_DIMENSION), F32),
            jax.ShapeDtypeStruct((heads * rows, LANES), F32),
            jax.ShapeDtypeStruct((part, LANES), BF),
        ),
        in_specs=[pl.BlockSpec(memory_space=pltpu.SMEM), vmem] + [hbm] * 5,
        out_specs=(vmem,) * 7,
        scratch_shapes=[
            pltpu.VMEM((rows, 2 * HEAD_DIMENSION), BF),
            pltpu.VMEM((TOPK, block), jnp.int32),
            pltpu.VMEM((TOPK, block), F32),
            pltpu.VMEM((LANES, LANES), F32),
            pltpu.SemaphoreType.DMA((heads,)),
            pltpu.SemaphoreType.DMA((4,)),
        ],
        compiler_params=pltpu.CompilerParams(vmem_limit_bytes=20 * MIB),
        cost_estimate=pl.CostEstimate(
            flops=6 * rows * width * rows,
            bytes_accessed=2 * (rows * width + width * model + rows * model),
            transcendentals=rows * rows * heads,
        ),
        name="own_block",
    )(place, kv, *map(in_hbm, (expert_ids.T, router_probs.T, queries, out_weight, resid)))


def dot_columns(a, b):
    return lax.dot_general(a, b, (((0,), (0,)), ((), ())), preferred_element_type=F32)


def attention_kernel(sizes, place, *refs):
    n_ctx, n_exp, n_tp, heads, part = sizes
    rows = n_exp * n_tp * part
    kv_refs, refs = refs[: n_ctx - 1], refs[n_ctx - 1 :]
    q_ref, w_ref, resid_ref, out_ref, sum_ref, max_ref = refs[:6]
    base_ref, across_ref, other_ref, other_across_ref = refs[6:10]
    k_all, v_all, att, att_rel = refs[10:]
    ctx, exp, tp = place[0], place[1], place[2]
    for i, kv_ref in enumerate(kv_refs):
        at = slice(i * rows, (i + 1) * rows)
        k_all[at, :] = kv_ref[:, :HEAD_DIMENSION]
        v_all[at, :HEAD_DIMENSION] = kv_ref[:, HEAD_DIMENSION:]
    v_all[:, HEAD_DIMENSION:] = jnp.ones(((n_ctx - 1) * rows, HEAD_DIMENSION), BF)
    piece = lax.broadcasted_iota(jnp.int32, (1, (n_ctx - 1) * rows), 1) // rows
    earlier = jnp.zeros_like(piece)
    for i, bits in enumerate(KV_ORDER):
        there = jnp.where(lax.bitwise_xor(ctx, bits) < ctx, 1, 0)
        earlier = earlier + jnp.where(piece == i, there, 0)
    allowed = earlier == 1
    scale = 1.0 / math.sqrt(HEAD_DIMENSION)
    s = jnp.where(allowed, dot_rows(q_ref[...], k_all[...]) * scale, -1e30)
    own_top = max_ref[...]
    top = jnp.maximum(own_top, jnp.max(s, axis=1, keepdims=True))
    keep = jnp.exp(own_top - top)
    out = jnp.dot(jnp.exp(s - top[:, :1]).astype(BF), v_all[...], preferred_element_type=F32)
    total = sum_ref[...] * keep + out[:, HEAD_DIMENSION:]
    out = out_ref[...] * keep + out[:, :HEAD_DIMENSION]
    att[...] = (out / total).astype(BF)
    for t in range(n_tp):
        for x in range(n_exp):
            owner = lax.rem(exp + x, n_exp) * n_tp + lax.rem(tp + t, n_tp)
            at = (t * n_exp + x) * part
            for h in range(heads):
                source = pl.ds(pl.multiple_of(h * rows + owner * part, part), part)
                columns = slice(h * HEAD_DIMENSION, (h + 1) * HEAD_DIMENSION)
                att_rel[at : at + part, columns] = att[source, :]
    projected = jnp.dot(att_rel[...], w_ref[...], preferred_element_type=F32)
    base_ref[...] = resid_ref[...].astype(F32) + projected[:part]
    across_ref[...] = projected[part : 2 * part].astype(BF)
    other_ref[...] = projected[2 * part : 3 * part].astype(BF)
    other_across_ref[...] = projected[3 * part :].astype(BF)


def attend_project(place, pieces, own, n_exp, n_tp):
    queries, out_weight, resid = own[:3]
    width, model = out_weight.shape
    n_ctx, heads = len(pieces) + 1, width // HEAD_DIMENSION
    rows = queries.shape[0] // heads
    part = resid.shape[0]
    vmem = pl.BlockSpec(memory_space=pltpu.VMEM)
    return pl.pallas_call(
        functools.partial(attention_kernel, (n_ctx, n_exp, n_tp, heads, part)),
        out_shape=(
            jax.ShapeDtypeStruct((part, model), F32),
            jax.ShapeDtypeStruct((part, model), BF),
            jax.ShapeDtypeStruct((part, model), BF),
            jax.ShapeDtypeStruct((part, model), BF),
        ),
        in_specs=[pl.BlockSpec(memory_space=pltpu.SMEM)] + [vmem] * (n_ctx - 1 + len(own)),
        out_specs=(vmem,) * 4,
        scratch_shapes=[
            pltpu.VMEM(((n_ctx - 1) * rows, HEAD_DIMENSION), BF),
            pltpu.VMEM(((n_ctx - 1) * rows, 2 * HEAD_DIMENSION), BF),
            pltpu.VMEM((heads * rows, HEAD_DIMENSION), BF),
            pltpu.VMEM((rows, width), BF),
        ],
        compiler_params=pltpu.CompilerParams(vmem_limit_bytes=20 * MIB),
        cost_estimate=pl.CostEstimate(
            flops=2 * rows * width * (3 * (n_ctx - 1) * rows + model),
            bytes_accessed=2 * (rows * width + width * model + rows * model),
            transcendentals=rows * n_ctx * rows * heads,
        ),
        name="attend_project",
    )(place, *pieces, *own)


def expert_kernel(n_pieces, depth, experts, first_ref, *refs):
    pieces, (wg_hbm, wu_hbm, wd_hbm) = refs[:n_pieces], refs[n_pieces : n_pieces + 3]
    outs = refs[n_pieces + 3 : n_pieces + 9]
    x_all, packed, pick_all, scale_all, out_all, wgu, wd, act, sems = refs[n_pieces + 9 :]
    sides, tokens, model = x_all.shape
    slots = pick_all.shape[1] // experts
    _, _, halves, hidden, _ = wgu.shape
    blocks = n_pieces // (2 * sides)
    part = tokens // (2 * blocks)

    def gate_up_copies(e):
        slot, rows = lax.rem(e, depth), pl.ds(e * halves, halves)
        return (
            pltpu.make_async_copy(wg_hbm.at[rows], wgu.at[slot, 0], sems.at[0, slot]),
            pltpu.make_async_copy(wu_hbm.at[rows], wgu.at[slot, 1], sems.at[1, slot]),
        )

    def down_copies(e):
        slot, rows = lax.rem(e, depth), pl.ds(e * halves, halves)
        return (pltpu.make_async_copy(wd_hbm.at[rows], wd.at[slot], sems.at[2, slot]),)

    def start(copies):
        for copy in copies:
            copy.start()

    def wait(copies):
        for copy in copies:
            copy.wait()

    def of_expert(e):
        return pl.ds(pl.multiple_of(e * slots, slots), slots)

    def gate_up(e):
        x = jnp.concatenate([out_all[side, of_expert(e), :] for side in range(sides)])
        weight = wgu[lax.rem(e, depth)].reshape(2 * halves * hidden, model)
        both = dot_rows(weight, x)
        gate, up = both[: halves * hidden], both[halves * hidden :]
        return (gate * jax.nn.sigmoid(gate) * up).astype(BF)

    def down(e):
        weight = wd[lax.rem(e, depth)].reshape(halves * hidden, model)
        out = dot_columns(act[lax.rem(e, 2)], weight)
        scale = jnp.concatenate([scale_all[side, of_expert(e), :] for side in range(sides)])
        return (out * scale).astype(BF)

    def keep(e, out):
        for side in range(sides):
            out_all[side, of_expert(e), :] = out[side * slots : (side + 1) * slots]

    for e in range(depth - 1):
        start(gate_up_copies(e))
        if e:
            start(down_copies(e - 1))
    for i, piece in enumerate(pieces):
        core, side, block = i // (sides * blocks), i // blocks % sides, i % blocks
        rows = slice((core * blocks + block) * part, (core * blocks + block + 1) * part)
        x_all[side, rows, :] = piece[:, :model]
        packed[side, rows, :] = piece[:, model:].astype(F32)
    slot = lax.broadcasted_iota(jnp.int32, (slots, tokens), 0)
    token = lax.broadcasted_iota(jnp.int32, (TOPK, tokens), 1)
    offset = lax.rem(token // part, blocks) * (slots // blocks)
    @pl.loop(0, sides)
    def _(side):
        fields = packed[side].T
        ids, ranks = fields[:TOPK].astype(jnp.int32), fields[TOPK : 2 * TOPK]
        gates = fields[2 * TOPK : 3 * TOPK] + fields[3 * TOPK : 4 * TOPK]
        places = ranks.astype(jnp.int32) + offset
        for e in range(experts):
            hit = ids == first_ref[0] + e
            chosen = slot == jnp.max(jnp.where(hit, places, -1), axis=0, keepdims=True)
            gate = jnp.sum(jnp.where(hit, gates, 0.0), axis=0, keepdims=True)
            here = slice(e * slots, (e + 1) * slots)
            pick_all[side, here, :] = jnp.where(chosen, 1.0, 0.0).astype(BF)
            scale_all[side, here, :] = jnp.sum(
                jnp.where(chosen, gate, 0.0), axis=1, keepdims=True
            )
        out_all[side] = jnp.dot(
            pick_all[side], x_all[side], preferred_element_type=F32
        ).astype(BF)
    wait(gate_up_copies(0))
    act[0] = gate_up(0)

    @pl.loop(0, experts - 1)
    def _(e):
        @pl.when(e + depth - 1 < experts)
        def _():
            start(gate_up_copies(e + depth - 1))

        @pl.when(e + depth - 2 < experts)
        def _():
            start(down_copies(e + depth - 2))

        wait(down_copies(e))
        wait(gate_up_copies(e + 1))
        following = gate_up(e + 1)
        out = down(e)
        act[lax.rem(e + 1, 2)] = following
        keep(e, out)

    wait(down_copies(experts - 1))
    keep(experts - 1, down(experts - 1))
    half = blocks * part // 2
    for side in (1, 0):
        routed = dot_columns(pick_all[side], out_all[side]).astype(BF)
        for core in range(2):
            near, far = routed[2 * core * half :][:half], routed[(2 * core + 1) * half :][:half]
            outs[3 * core + 1 - side][...] = far
            outs[3 * core + 2][(1 - side) * half : (2 - side) * half, :] = near


def cube_experts(first, pieces, w_gate, w_up, w_down, slots):
    rows, hidden, model = w_down.shape
    halves, sides = 2, 2
    experts = rows // halves
    tokens = len(pieces) * pieces[0].shape[0] // sides
    depth = 5
    vmem = pl.BlockSpec(memory_space=pltpu.VMEM)
    hbm = pl.BlockSpec(memory_space=pltpu.HBM)

    half = jax.ShapeDtypeStruct((tokens // 4, model), BF)
    whole = jax.ShapeDtypeStruct((tokens // 2, model), BF)
    return pl.pallas_call(
        functools.partial(expert_kernel, len(pieces), depth, experts),
        out_shape=(half, half, whole) * 2,
        in_specs=[pl.BlockSpec(memory_space=pltpu.SMEM)] + [vmem] * len(pieces) + [hbm] * 3,
        out_specs=(vmem,) * 6,
        scratch_shapes=[
            pltpu.VMEM((sides, tokens, model), BF),
            pltpu.VMEM((sides, tokens, LANES), F32),
            pltpu.VMEM((sides, experts * slots, tokens), BF),
            pltpu.VMEM((sides, experts * slots, 1), F32),
            pltpu.VMEM((sides, experts * slots, model), BF),
            pltpu.VMEM((depth, 2, halves, hidden, model), BF),
            pltpu.VMEM((depth, halves, hidden, model), BF),
            pltpu.VMEM((2, halves * hidden, sides * slots), BF),
            pltpu.SemaphoreType.DMA((3, depth)),
        ],
        compiler_params=pltpu.CompilerParams(vmem_limit_bytes=44 * MIB),
        cost_estimate=pl.CostEstimate(
            flops=2 * experts * sides * slots * model * (3 * halves * hidden + 2 * tokens),
            bytes_accessed=6 * rows * model * hidden + 4 * tokens * model,
            transcendentals=experts * sides * slots * halves * hidden,
        ),
        name="experts",
    )(
        first,
        *pieces,
        in_hbm(jnp.swapaxes(w_gate, 1, 2)),
        in_hbm(jnp.swapaxes(w_up, 1, 2)),
        in_hbm(w_down),
    )


def sums_back(mine, other, part):
    def add(a, *others):
        total = a.astype(F32)
        for b in others:
            total = total + b.astype(F32)
        return total.astype(BF)

    sums = [add(a, flip(b, "tp", 1)) for a, b in zip(mine, other)]
    sums[1], sums[2] = lax.optimization_barrier((sums[1], sums[2]))
    sums = [[x[at : at + part] for at in range(0, x.shape[0], part)] for x in sums]
    across = sums[2][:2] + sums[0]
    here = sums[2][2:] + sums[1]
    far_across = flip(across[2], "exp", 1)
    last_across = flip_both(across[3])
    last = flip(here[3], "ctx", 1)
    own = flip(across[0], "exp", 1)
    near = flip(here[1], "ctx", 1)
    near_across = flip_both(across[1])
    far = flip(add(here[2], last_across, far_across, last), "ctx", 2)
    total = here[0].astype(F32)
    for term in (far, near, near_across, own):
        total = total + term.astype(F32)
    return total


def on_device(
    queries, keys, values, out_weight, resid, expert_ids, router_probs, w_gate, w_up, w_down
):
    n_ctx, n_exp, n_tp = (lax.axis_size(a) for a in ("ctx", "exp", "tp"))
    part = resid.shape[0]
    rows_here = w_gate.shape[0]
    block = expert_ids.shape[0]
    cube = (n_ctx, n_exp, n_tp) == (4, 2, 2) and block == n_tp * part <= LANES
    if not cube or part % 16 or rows_here * n_ctx * n_exp != 2 * EXPERTS:
        return on_device_any_size(
            queries, keys, values, out_weight, resid, expert_ids, router_probs, w_gate, w_up, w_down
        )
    ctx, exp, tp = (lax.axis_index(a) for a in ("ctx", "exp", "tp"))
    place = jnp.stack([ctx, exp, tp]).astype(jnp.int32)
    heads_here = queries.shape[1] // HEAD_DIMENSION
    first = (ctx * n_exp + exp) * rows_here // 2
    slots = n_ctx * min(8, block)

    shared = (exp * n_tp + tp) * heads_here // (QUERY_HEADS // KEY_VALUE_HEADS)
    key_head = lax.dynamic_slice_in_dim(keys, shared * HEAD_DIMENSION, HEAD_DIMENSION, 1)
    value_head = lax.dynamic_slice_in_dim(values, shared * HEAD_DIMENSION, HEAD_DIMENSION, 1)
    kv = jnp.concatenate([key_head, value_head], axis=1)
    kv_pieces = [flip(kv, "ctx", bits) for bits in KV_ORDER]
    *own, routing = own_block(
        place, kv, expert_ids, router_probs, queries, out_weight, resid, n_exp, n_tp
    )
    base, across, other, other_across = attend_project(place, kv_pieces, own, n_exp, n_tp)

    other_across = flip(other_across, "tp", 1).astype(F32)
    across = (across.astype(F32) + other_across).astype(BF)
    across = flip(across, "exp", 1)
    other = flip(other, "tp", 1)
    hidden = base + other.astype(F32) + across.astype(F32)
    mean_square = jnp.mean(hidden * hidden, axis=1, keepdims=True)
    normed = (hidden * lax.rsqrt(mean_square + 1e-06)).astype(BF)
    normed = jnp.concatenate([normed, routing], axis=1)

    far = flip(normed, "ctx", 2)
    across = flip(normed, "exp", 1)
    near = flip(normed, "ctx", 1)
    near_across = flip_both(normed)
    far_across = flip(far, "exp", 1)
    last_across = flip_both(far)
    last = flip(far, "ctx", 1)
    early = (normed,) + lax.optimization_barrier((near, far, across, near_across))
    late = lax.optimization_barrier((far_across, last_across, last))
    pieces = [normed, near, far, last, across, near_across, far_across, last_across]
    pieces += [flip(piece, "tp", 1) for piece in early[:3] + late[2:] + early[3:] + late[:2]]
    sums = cube_experts(
        first.astype(jnp.int32).reshape(1), pieces, w_gate, w_up, w_down, slots
    )
    return (hidden + sums_back(sums[:3], sums[3:], part)).astype(BF)


def solution(mesh):
    in_specs = (
        P(("groups", "ctx"), ("exp", "tp")),
        P(("groups", "ctx"), None),
        P(("groups", "ctx"), None),
        P(("exp", "tp"), None),
        P(("groups", "ctx", "exp", "tp"), None),
        P(("groups", "ctx", "exp"), None),
        P(("groups", "ctx", "exp"), None),
        P(("ctx", "exp"), None, "tp"),
        P(("ctx", "exp"), None, "tp"),
        P(("ctx", "exp"), "tp", None),
    )
    out_specs = P(("groups", "ctx", "exp", "tp"), None)
    return jax.shard_map(
        on_device, mesh=mesh, in_specs=in_specs, out_specs=out_specs, check_vma=False
    )
```

```python
import functools
import math

import jax
import jax.numpy as jnp
from jax import lax
from jax.experimental import pallas as pl
from jax.experimental.pallas import tpu as pltpu
from jax.sharding import PartitionSpec as P

HEAD_DIMENSION = 128
QUERY_HEADS = 32
KEY_VALUE_HEADS = 4
EXPERTS = 64
TOPK = 8
MIB = 1 << 20
LANES = 128
BF = jnp.bfloat16
F32 = jnp.float32


def attend_blocks(blocks, key_head, value_head, heads_here):
    score_scale = 1.0 / math.sqrt(HEAD_DIMENSION)

    def make_state(query_rows):
        row_total = query_rows.shape[0]
        return (
            jnp.full((row_total, heads_here), -1e30, jnp.float32),
            jnp.zeros((row_total, heads_here), jnp.float32),
            jnp.zeros((row_total, heads_here, HEAD_DIMENSION), jnp.float32),
        )

    initial = tuple((make_state(query_rows) for query_rows, query_places in blocks))

    def fold_keys(carry, piece, first):
        key_piece, value_piece = piece
        key_places = jnp.arange(key_piece.shape[0], dtype=jnp.int32)
        updated = []
        for (query_rows, query_places), state in zip(blocks, carry):

            def refresh(state, query_rows=query_rows, query_places=query_places):
                running_max, running_sum, accum = state
                shaped = query_rows.reshape(query_rows.shape[0], heads_here, HEAD_DIMENSION)
                scores = (
                    jnp.einsum("qhd,kd->qhk", shaped, key_piece, preferred_element_type=jnp.float32)
                    * score_scale
                )
                allowed = key_places[None, None, :] <= query_places[:, None, None]
                scores = jnp.where(allowed, scores, -1e30)
                new_max = jnp.maximum(running_max, jnp.max(scores, axis=2))
                weights = jnp.where(allowed, jnp.exp(scores - new_max[:, :, None]), 0.0)
                running_sum = jnp.sum(weights, axis=2)
                accum = jnp.einsum(
                    "qhk,kd->qhd",
                    weights,
                    value_piece.astype(jnp.float32),
                    precision=lax.Precision.HIGHEST,
                )
                return (new_max, running_sum, accum)

            needed = first <= query_places[-1]
            updated.append(lax.cond(needed, refresh, lambda state: state, state))
        return tuple(updated)

    final = fold_keys(
        initial,
        (
            lax.all_gather(key_head, "ctx", axis=0, tiled=True),
            lax.all_gather(value_head, "ctx", axis=0, tiled=True),
        ),
        jnp.int32(0),
    )
    results = []
    for (query_rows, query_places), state in zip(blocks, final):
        running_max, running_sum, accum = state
        results.append(
            (accum / running_sum[:, :, None])
            .reshape(query_rows.shape[0], heads_here * HEAD_DIMENSION)
            .astype(jnp.bfloat16)
        )
    return results


def run_experts(inputs, w_gate, w_up, w_down):
    gate_out = jnp.einsum("rnd,rdf->rnf", inputs, w_gate, preferred_element_type=jnp.float32)
    up_out = jnp.einsum("rnd,rdf->rnf", inputs, w_up, preferred_element_type=jnp.float32)
    activated = (jax.nn.silu(gate_out) * up_out).astype(jnp.bfloat16)
    return jnp.einsum("rnf,rfd->rnd", activated, w_down, preferred_element_type=jnp.float32).astype(
        jnp.bfloat16
    )


def on_device_any_size(
    queries, keys, values, out_weight, resid, expert_ids, router_probs, w_gate, w_up, w_down
):
    rows_ctx = queries.shape[0]
    heads_here = queries.shape[1] // HEAD_DIMENSION
    group_width = QUERY_HEADS // KEY_VALUE_HEADS
    head_rank = lax.axis_index(("exp", "tp"))
    shared = head_rank * heads_here // group_width
    key_head = lax.dynamic_slice_in_dim(keys, shared * HEAD_DIMENSION, HEAD_DIMENSION, 1)
    value_head = lax.dynamic_slice_in_dim(values, shared * HEAD_DIMENSION, HEAD_DIMENSION, 1)
    cycle_rank = lax.axis_index("ctx")
    own_places = cycle_rank * rows_ctx + jnp.arange(rows_ctx, dtype=jnp.int32)
    attended = attend_blocks([(queries, own_places)], key_head, value_head, heads_here)[0]
    projected = lax.psum_scatter(
        jnp.dot(attended, out_weight, preferred_element_type=jnp.float32).astype(jnp.bfloat16),
        ("exp", "tp"),
        scatter_dimension=0,
        tiled=True,
    ).astype(jnp.float32)
    hidden = resid.astype(jnp.float32) + projected
    mean_square = jnp.mean(hidden * hidden, axis=1, keepdims=True)
    normed = (hidden * lax.rsqrt(mean_square + 1e-06)).astype(jnp.bfloat16)
    pair_rows = lax.all_gather(normed, "tp", axis=0, tiled=True)
    slot_count = min(8, expert_ids.shape[0])
    gate_weights = router_probs / jnp.sum(router_probs, axis=1, keepdims=True)
    flat_ids = expert_ids.reshape(-1)
    assigned = flat_ids.shape[0]
    onehot = (flat_ids[:, None] == jnp.arange(EXPERTS, dtype=jnp.int32)[None, :]).astype(jnp.int32)
    slots = jnp.sum(onehot * (jnp.cumsum(onehot, axis=0) - 1), axis=1)
    token_of = jnp.arange(assigned, dtype=jnp.int32) // TOPK
    peer_count = lax.axis_size(("ctx", "exp"))
    rows_here = w_gate.shape[0]
    cell_parts = []
    for half_index in range(2):
        half_rows_id = 2 * flat_ids + half_index
        target = half_rows_id // rows_here
        local_row = half_rows_id % rows_here
        cell_parts.append((local_row * slot_count + slots) * peer_count + target)
    cells = jnp.concatenate(cell_parts)
    table = (
        jnp.full((rows_here * slot_count * peer_count,), -1, jnp.int32)
        .at[cells]
        .set(jnp.concatenate([token_of, token_of]))
    )
    send_buffer = jnp.where(
        table[:, None] >= 0, pair_rows[jnp.maximum(table, 0)], jnp.zeros((), jnp.bfloat16)
    )
    model_width = pair_rows.shape[1]
    received = lax.all_to_all(
        send_buffer.reshape(rows_here * slot_count, peer_count, model_width),
        ("ctx", "exp"),
        split_axis=1,
        concat_axis=1,
        tiled=True,
    )
    expert_out = run_experts(
        received.reshape(rows_here, slot_count * peer_count, model_width), w_gate, w_up, w_down
    )
    returned = lax.all_to_all(
        expert_out.reshape(rows_here * slot_count, peer_count, model_width),
        ("ctx", "exp"),
        split_axis=1,
        concat_axis=1,
        tiled=True,
    )
    returned_flat = returned.reshape(rows_here * slot_count * peer_count, model_width)
    gathered = returned_flat[cells].reshape(2, expert_ids.shape[0], TOPK, model_width)
    routed_part = jnp.einsum(
        "hakd,ak->ad", gathered.astype(jnp.float32), gate_weights, precision=lax.Precision.HIGHEST
    )
    routed = lax.psum_scatter(
        routed_part.astype(jnp.bfloat16), "tp", scatter_dimension=0, tiled=True
    ).astype(jnp.float32)
    return (hidden + routed).astype(jnp.bfloat16)


def flip(x, axis, bit):
    return lax.ppermute(x, axis, [(i, i ^ bit) for i in range(lax.axis_size(axis))])


def flip_both(x):
    n_exp = lax.axis_size("exp")
    mask = n_exp + 1
    size = lax.axis_size("ctx") * n_exp
    return lax.ppermute(x, ("ctx", "exp"), [(i, i ^ mask) for i in range(size)])


def in_hbm(x):
    return pltpu.with_memory_space_constraint(x, pltpu.HBM)


def dot_rows(a, b):
    return lax.dot_general(a, b, (((1,), (1,)), ((), ())), preferred_element_type=F32)


KV_ORDER = ((1, 3), (2,))


def own_block_kernel(sizes, place, kv_ref, ids_hbm, probs_hbm, q_hbm, w_hbm, resid_hbm, *refs):
    n_exp, n_tp, heads, part = sizes
    rows = n_exp * n_tp * part
    q_ref, w_ref, resid_ref, out_ref, sum_ref, max_ref, routing_ref = refs[:7]
    v_ext, ids_ref, probs_ref, packed, q_sem, sems = refs[7:]
    fetch = [
        pltpu.make_async_copy(ids_hbm, ids_ref, sems.at[0]),
        pltpu.make_async_copy(probs_hbm, probs_ref, sems.at[1]),
        pltpu.make_async_copy(resid_hbm, resid_ref, sems.at[2]),
        pltpu.make_async_copy(w_hbm, w_ref, sems.at[3]),
    ]
    fetch_q = []
    for h in range(heads):
        columns = slice(h * HEAD_DIMENSION, (h + 1) * HEAD_DIMENSION)
        fetch_q.append(
            pltpu.make_async_copy(
                q_hbm.at[:, columns], q_ref.at[pl.ds(h * rows, rows)], q_sem.at[h]
            )
        )
        fetch_q[h].start()
    for copy in fetch:
        copy.start()
    tp = place[2]
    v_ext[:, :HEAD_DIMENSION] = kv_ref[:, HEAD_DIMENSION:]
    v_ext[:, HEAD_DIMENSION:] = jnp.ones((rows, HEAD_DIMENSION), BF)
    keys = kv_ref[:, :HEAD_DIMENSION]
    column = lax.broadcasted_iota(jnp.int32, (rows, rows), 1)
    allowed = column <= lax.broadcasted_iota(jnp.int32, (rows, rows), 0)
    scale = 1.0 / math.sqrt(HEAD_DIMENSION)
    for copy in fetch_q:
        copy.wait()
    s = dot_rows(q_ref[...], keys).reshape(heads, rows, rows)
    s = jnp.where(allowed, s * scale, -1e30).reshape(heads * rows, rows)
    top = jnp.max(s, axis=1, keepdims=True)
    out = jnp.dot(jnp.exp(s - top).astype(BF), v_ext[...], preferred_element_type=F32)
    out_ref[...] = out[:, :HEAD_DIMENSION]
    sum_ref[...] = out[:, HEAD_DIMENSION:]
    max_ref[...] = jnp.broadcast_to(top, max_ref.shape)

    fetch[0].wait()
    fetch[1].wait()
    block = n_tp * part
    ids = ids_ref[...]
    probs = probs_ref[...]
    expert = lax.broadcasted_iota(jnp.int32, (EXPERTS, block), 0)
    named = jnp.zeros((EXPERTS, block), F32)
    for k in range(TOPK):
        named = named + jnp.where(expert == ids[k : k + 1, :], 1.0, 0.0)
    before = lax.broadcasted_iota(jnp.int32, (block, block), 0) < lax.broadcasted_iota(
        jnp.int32, (block, block), 1
    )
    count = jnp.dot(
        named.astype(BF), jnp.where(before, 1.0, 0.0).astype(BF), preferred_element_type=F32
    )
    ranks = [
        jnp.sum(jnp.where(expert == ids[k : k + 1, :], count, 0.0), axis=0, keepdims=True)
        for k in range(TOPK)
    ]
    gates = probs / jnp.sum(probs, axis=0, keepdims=True)
    high = gates.astype(BF).astype(F32)
    fields = jnp.concatenate([ids.astype(F32)] + ranks + [high, gates - high], axis=0)
    packed[...] = jnp.zeros_like(packed)
    packed[: 4 * TOPK, :block] = fields
    packed[...] = packed[...].T
    routing_ref[...] = packed[pl.ds(pl.multiple_of(tp * part, part), part), :].astype(BF)
    fetch[2].wait()
    fetch[3].wait()


def own_block(place, kv, expert_ids, router_probs, queries, out_weight, resid, n_exp, n_tp):
    rows, width = queries.shape
    heads = width // HEAD_DIMENSION
    part, model = resid.shape
    block = expert_ids.shape[0]
    vmem = pl.BlockSpec(memory_space=pltpu.VMEM)
    hbm = pl.BlockSpec(memory_space=pltpu.HBM)
    return pl.pallas_call(
        functools.partial(own_block_kernel, (n_exp, n_tp, heads, part)),
        out_shape=(
            jax.ShapeDtypeStruct((heads * rows, HEAD_DIMENSION), BF),
            jax.ShapeDtypeStruct((width, model), BF),
            jax.ShapeDtypeStruct((part, model), BF),
            jax.ShapeDtypeStruct((heads * rows, HEAD_DIMENSION), F32),
            jax.ShapeDtypeStruct((heads * rows, HEAD_DIMENSION), F32),
            jax.ShapeDtypeStruct((heads * rows, LANES), F32),
            jax.ShapeDtypeStruct((part, LANES), BF),
        ),
        in_specs=[pl.BlockSpec(memory_space=pltpu.SMEM), vmem] + [hbm] * 5,
        out_specs=(vmem,) * 7,
        scratch_shapes=[
            pltpu.VMEM((rows, 2 * HEAD_DIMENSION), BF),
            pltpu.VMEM((TOPK, block), jnp.int32),
            pltpu.VMEM((TOPK, block), F32),
            pltpu.VMEM((LANES, LANES), F32),
            pltpu.SemaphoreType.DMA((heads,)),
            pltpu.SemaphoreType.DMA((4,)),
        ],
        compiler_params=pltpu.CompilerParams(vmem_limit_bytes=20 * MIB),
        cost_estimate=pl.CostEstimate(
            flops=6 * rows * width * rows,
            bytes_accessed=2 * (rows * width + width * model + rows * model),
            transcendentals=rows * rows * heads,
        ),
        name="own_block",
    )(place, kv, *map(in_hbm, (expert_ids.T, router_probs.T, queries, out_weight, resid)))


def dot_columns(a, b):
    return lax.dot_general(a, b, (((0,), (0,)), ((), ())), preferred_element_type=F32)


def fold_blocks(bits_of, ctx, kv_refs, q_ref, state, k_all, v_all):
    out_ref, sum_ref, max_ref = state
    rows = kv_refs[0].shape[0]
    for i, kv_ref in enumerate(kv_refs):
        at = slice(i * rows, (i + 1) * rows)
        k_all[at, :] = kv_ref[:, :HEAD_DIMENSION]
        v_all[at, :HEAD_DIMENSION] = kv_ref[:, HEAD_DIMENSION:]
    v_all[:, HEAD_DIMENSION:] = jnp.ones((len(kv_refs) * rows, HEAD_DIMENSION), BF)
    piece = lax.broadcasted_iota(jnp.int32, (1, len(kv_refs) * rows), 1) // rows
    earlier = jnp.zeros_like(piece)
    for i, bits in enumerate(bits_of):
        there = jnp.where(lax.bitwise_xor(ctx, bits) < ctx, 1, 0)
        earlier = earlier + jnp.where(piece == i, there, 0)
    scale = 1.0 / math.sqrt(HEAD_DIMENSION)
    s = jnp.where(earlier == 1, dot_rows(q_ref[...], k_all[...]) * scale, -1e30)
    old_top = max_ref[...]
    top = jnp.maximum(old_top, jnp.max(s, axis=1, keepdims=True))
    keep = jnp.exp(old_top - top)
    out = jnp.dot(jnp.exp(s - top[:, :1]).astype(BF), v_all[...], preferred_element_type=F32)
    total = sum_ref[...] * keep + out[:, HEAD_DIMENSION:]
    return out_ref[...] * keep + out[:, :HEAD_DIMENSION], total, top


def fold_kernel(bits_of, place, *refs):
    count = len(bits_of)
    kv_refs, (q_ref, *state), (k_all, v_all) = refs[:count], refs[count : count + 4], refs[-2:]
    folded = fold_blocks(bits_of, place[0], kv_refs, q_ref, state, k_all, v_all)
    for ref, value in zip(refs[count + 4 :], folded):
        ref[...] = value


def fold_earlier(bits_of, place, pieces, queries, state):
    rows, count = pieces[0].shape[0], len(pieces)
    vmem = pl.BlockSpec(memory_space=pltpu.VMEM)
    return pl.pallas_call(
        functools.partial(fold_kernel, bits_of),
        out_shape=tuple(jax.ShapeDtypeStruct(x.shape, x.dtype) for x in state),
        in_specs=[pl.BlockSpec(memory_space=pltpu.SMEM)] + [vmem] * (count + 4),
        out_specs=(vmem,) * 3,
        scratch_shapes=[
            pltpu.VMEM((count * rows, HEAD_DIMENSION), BF),
            pltpu.VMEM((count * rows, 2 * HEAD_DIMENSION), BF),
        ],
        compiler_params=pltpu.CompilerParams(vmem_limit_bytes=20 * MIB),
        cost_estimate=pl.CostEstimate(
            flops=6 * queries.size * count * rows,
            bytes_accessed=16 * queries.size,
            transcendentals=queries.shape[0] * count * rows,
        ),
        name="fold_earlier",
    )(place, *pieces, queries, *state)


def attention_kernel(sizes, place, *refs):
    bits_of, n_exp, n_tp, heads, part = sizes
    rows = n_exp * n_tp * part
    kv_refs, refs = refs[: len(bits_of)], refs[len(bits_of) :]
    q_ref, w_ref, resid_ref, *state = refs[:6]
    base_ref, across_ref, other_ref = refs[6:9]
    k_all, v_all, att, att_rel = refs[9:]
    ctx, exp, tp = place[0], place[1], place[2]
    out, total, _ = fold_blocks(bits_of, ctx, kv_refs, q_ref, state, k_all, v_all)
    att[...] = (out / total).astype(BF)
    for t in range(n_tp):
        for x in range(n_exp):
            owner = lax.rem(exp + x, n_exp) * n_tp + lax.rem(tp + t, n_tp)
            at = (t * n_exp + x) * part
            for h in range(heads):
                source = pl.ds(pl.multiple_of(h * rows + owner * part, part), part)
                columns = slice(h * HEAD_DIMENSION, (h + 1) * HEAD_DIMENSION)
                att_rel[at : at + part, columns] = att[source, :]
    projected = jnp.dot(att_rel[...], w_ref[...], preferred_element_type=F32)
    base_ref[...] = resid_ref[...].astype(F32) + projected[:part]
    across_ref[...] = projected[part : 2 * part].astype(BF)
    other_ref[...] = projected[2 * part :].astype(BF)


def attend_project(bits_of, place, pieces, own, n_exp, n_tp):
    queries, out_weight, resid = own[:3]
    width, model = out_weight.shape
    count, heads = len(pieces), width // HEAD_DIMENSION
    rows = queries.shape[0] // heads
    part = resid.shape[0]
    vmem = pl.BlockSpec(memory_space=pltpu.VMEM)
    return pl.pallas_call(
        functools.partial(attention_kernel, (bits_of, n_exp, n_tp, heads, part)),
        out_shape=(
            jax.ShapeDtypeStruct((part, model), F32),
            jax.ShapeDtypeStruct((part, model), BF),
            jax.ShapeDtypeStruct((2 * part, model), BF),
        ),
        in_specs=[pl.BlockSpec(memory_space=pltpu.SMEM)] + [vmem] * (count + len(own)),
        out_specs=(vmem,) * 3,
        scratch_shapes=[
            pltpu.VMEM((count * rows, HEAD_DIMENSION), BF),
            pltpu.VMEM((count * rows, 2 * HEAD_DIMENSION), BF),
            pltpu.VMEM((heads * rows, HEAD_DIMENSION), BF),
            pltpu.VMEM((rows, width), BF),
        ],
        compiler_params=pltpu.CompilerParams(vmem_limit_bytes=20 * MIB),
        cost_estimate=pl.CostEstimate(
            flops=2 * rows * width * (3 * count * rows + model),
            bytes_accessed=2 * (rows * width + width * model + rows * model),
            transcendentals=rows * count * rows * heads,
        ),
        name="attend_project",
    )(place, *pieces, *own)


def expert_kernel(n_pieces, depth, experts, first_ref, *refs):
    pieces, (wg_hbm, wu_hbm, wd_hbm) = refs[:n_pieces], refs[n_pieces : n_pieces + 3]
    outs = refs[n_pieces + 3 : n_pieces + 9]
    x_all, packed, pick_all, scale_all, out_all, wgu, wd, act, sems = refs[n_pieces + 9 :]
    sides, tokens, model = x_all.shape
    slots = pick_all.shape[1] // experts
    _, _, halves, hidden, _ = wgu.shape
    blocks = n_pieces // (2 * sides)
    part = tokens // (2 * blocks)

    def gate_up_copies(e):
        slot, rows = lax.rem(e, depth), pl.ds(e * halves, halves)
        return (
            pltpu.make_async_copy(wg_hbm.at[rows], wgu.at[slot, 0], sems.at[0, slot]),
            pltpu.make_async_copy(wu_hbm.at[rows], wgu.at[slot, 1], sems.at[1, slot]),
        )

    def down_copies(e):
        slot, rows = lax.rem(e, depth), pl.ds(e * halves, halves)
        return (pltpu.make_async_copy(wd_hbm.at[rows], wd.at[slot], sems.at[2, slot]),)

    def start(copies):
        for copy in copies:
            copy.start()

    def wait(copies):
        for copy in copies:
            copy.wait()

    def of_expert(e):
        return pl.ds(pl.multiple_of(e * slots, slots), slots)

    def gate_up(e):
        x = jnp.concatenate([out_all[side, of_expert(e), :] for side in range(sides)])
        weight = wgu[lax.rem(e, depth)].reshape(2 * halves * hidden, model)
        both = dot_rows(weight, x)
        gate, up = both[: halves * hidden], both[halves * hidden :]
        return (gate * jax.nn.sigmoid(gate) * up).astype(BF)

    def down(e):
        weight = wd[lax.rem(e, depth)].reshape(halves * hidden, model)
        out = dot_columns(act[lax.rem(e, 2)], weight)
        scale = jnp.concatenate([scale_all[side, of_expert(e), :] for side in range(sides)])
        return (out * scale).astype(BF)

    def keep(e, out):
        for side in range(sides):
            out_all[side, of_expert(e), :] = out[side * slots : (side + 1) * slots]

    for e in range(depth - 1):
        start(gate_up_copies(e))
        if e:
            start(down_copies(e - 1))
    for i, piece in enumerate(pieces):
        core, side, block = i // (sides * blocks), i // blocks % sides, i % blocks
        rows = slice((core * blocks + block) * part, (core * blocks + block + 1) * part)
        x_all[side, rows, :] = piece[:, :model]
        packed[side, rows, :] = piece[:, model:].astype(F32)
    slot = lax.broadcasted_iota(jnp.int32, (slots, tokens), 0)
    token = lax.broadcasted_iota(jnp.int32, (TOPK, tokens), 1)
    offset = lax.rem(token // part, blocks) * (slots // blocks)
    @pl.loop(0, sides)
    def _(side):
        fields = packed[side].T
        ids, ranks = fields[:TOPK].astype(jnp.int32), fields[TOPK : 2 * TOPK]
        gates = fields[2 * TOPK : 3 * TOPK] + fields[3 * TOPK : 4 * TOPK]
        places = ranks.astype(jnp.int32) + offset
        for e in range(experts):
            hit = ids == first_ref[0] + e
            chosen = slot == jnp.max(jnp.where(hit, places, -1), axis=0, keepdims=True)
            gate = jnp.sum(jnp.where(hit, gates, 0.0), axis=0, keepdims=True)
            here = slice(e * slots, (e + 1) * slots)
            pick_all[side, here, :] = jnp.where(chosen, 1.0, 0.0).astype(BF)
            scale_all[side, here, :] = jnp.sum(
                jnp.where(chosen, gate, 0.0), axis=1, keepdims=True
            )
        out_all[side] = jnp.dot(
            pick_all[side], x_all[side], preferred_element_type=F32
        ).astype(BF)
    wait(gate_up_copies(0))
    act[0] = gate_up(0)

    @pl.loop(0, experts - 1)
    def _(e):
        @pl.when(e + depth - 1 < experts)
        def _():
            start(gate_up_copies(e + depth - 1))

        @pl.when(e + depth - 2 < experts)
        def _():
            start(down_copies(e + depth - 2))

        wait(down_copies(e))
        wait(gate_up_copies(e + 1))
        following = gate_up(e + 1)
        out = down(e)
        act[lax.rem(e + 1, 2)] = following
        keep(e, out)

    wait(down_copies(experts - 1))
    keep(experts - 1, down(experts - 1))
    half = blocks * part // 2
    for side in (1, 0):
        routed = dot_columns(pick_all[side], out_all[side]).astype(BF)
        for core in range(2):
            near, far = routed[2 * core * half :][:half], routed[(2 * core + 1) * half :][:half]
            outs[3 * core + 1 - side][...] = far
            outs[3 * core + 2][(1 - side) * half : (2 - side) * half, :] = near


def cube_experts(first, pieces, w_gate, w_up, w_down, slots):
    rows, hidden, model = w_down.shape
    halves, sides = 2, 2
    experts = rows // halves
    tokens = len(pieces) * pieces[0].shape[0] // sides
    depth = 4
    vmem = pl.BlockSpec(memory_space=pltpu.VMEM)
    hbm = pl.BlockSpec(memory_space=pltpu.HBM)

    half = jax.ShapeDtypeStruct((tokens // 4, model), BF)
    whole = jax.ShapeDtypeStruct((tokens // 2, model), BF)
    return pl.pallas_call(
        functools.partial(expert_kernel, len(pieces), depth, experts),
        out_shape=(half, half, whole) * 2,
        in_specs=[pl.BlockSpec(memory_space=pltpu.SMEM)] + [vmem] * len(pieces) + [hbm] * 3,
        out_specs=(vmem,) * 6,
        scratch_shapes=[
            pltpu.VMEM((sides, tokens, model), BF),
            pltpu.VMEM((sides, tokens, LANES), F32),
            pltpu.VMEM((sides, experts * slots, tokens), BF),
            pltpu.VMEM((sides, experts * slots, 1), F32),
            pltpu.VMEM((sides, experts * slots, model), BF),
            pltpu.VMEM((depth, 2, halves, hidden, model), BF),
            pltpu.VMEM((depth, halves, hidden, model), BF),
            pltpu.VMEM((2, halves * hidden, sides * slots), BF),
            pltpu.SemaphoreType.DMA((3, depth)),
        ],
        compiler_params=pltpu.CompilerParams(vmem_limit_bytes=44 * MIB),
        cost_estimate=pl.CostEstimate(
            flops=2 * experts * sides * slots * model * (3 * halves * hidden + 2 * tokens),
            bytes_accessed=6 * rows * model * hidden + 4 * tokens * model,
            transcendentals=experts * sides * slots * halves * hidden,
        ),
        name="experts",
    )(
        first,
        *pieces,
        in_hbm(jnp.swapaxes(w_gate, 1, 2)),
        in_hbm(jnp.swapaxes(w_up, 1, 2)),
        in_hbm(w_down),
    )


def sums_back(mine, other, part):
    def add(a, *others):
        total = a.astype(F32)
        for b in others:
            total = total + b.astype(F32)
        return total.astype(BF)

    sums = [add(a, flip(b, "tp", 1)) for a, b in zip(mine, other)]
    sums[1], sums[2] = lax.optimization_barrier((sums[1], sums[2]))
    sums = [[x[at : at + part] for at in range(0, x.shape[0], part)] for x in sums]
    across = sums[2][:2] + sums[0]
    here = sums[2][2:] + sums[1]
    far_across = flip(across[2], "exp", 1)
    last_across = flip_both(across[3])
    last = flip(here[3], "ctx", 1)
    own = flip(across[0], "exp", 1)
    near = flip(here[1], "ctx", 1)
    near_across = flip_both(across[1])
    far = flip(add(here[2], last_across, far_across, last), "ctx", 2)
    total = here[0].astype(F32)
    for term in (far, near, near_across, own):
        total = total + term.astype(F32)
    return total


def on_device(
    queries, keys, values, out_weight, resid, expert_ids, router_probs, w_gate, w_up, w_down
):
    n_ctx, n_exp, n_tp = (lax.axis_size(a) for a in ("ctx", "exp", "tp"))
    part = resid.shape[0]
    rows_here = w_gate.shape[0]
    block = expert_ids.shape[0]
    cube = (n_ctx, n_exp, n_tp) == (4, 2, 2) and block == n_tp * part <= LANES
    if not cube or part % 16 or rows_here * n_ctx * n_exp != 2 * EXPERTS:
        return on_device_any_size(
            queries, keys, values, out_weight, resid, expert_ids, router_probs, w_gate, w_up, w_down
        )
    ctx, exp, tp = (lax.axis_index(a) for a in ("ctx", "exp", "tp"))
    place = jnp.stack([ctx, exp, tp]).astype(jnp.int32)
    heads_here = queries.shape[1] // HEAD_DIMENSION
    first = (ctx * n_exp + exp) * rows_here // 2
    slots = n_ctx * min(8, block)

    shared = (exp * n_tp + tp) * heads_here // (QUERY_HEADS // KEY_VALUE_HEADS)
    key_head = lax.dynamic_slice_in_dim(keys, shared * HEAD_DIMENSION, HEAD_DIMENSION, 1)
    value_head = lax.dynamic_slice_in_dim(values, shared * HEAD_DIMENSION, HEAD_DIMENSION, 1)
    kv = jnp.concatenate([key_head, value_head], axis=1)
    early, late = KV_ORDER
    early_pieces = [flip(kv, "ctx", bits) for bits in early]
    late_pieces = [flip(kv, "ctx", bits) for bits in late]
    *own, routing = own_block(
        place, kv, expert_ids, router_probs, queries, out_weight, resid, n_exp, n_tp
    )
    own[3:] = fold_earlier(early, place, early_pieces, own[0], own[3:])
    base, across, other = attend_project(late, place, late_pieces, own, n_exp, n_tp)

    other = flip(other, "tp", 1).astype(F32)
    across = flip((across.astype(F32) + other[part:]).astype(BF), "exp", 1)
    hidden = base + other[:part] + across.astype(F32)
    mean_square = jnp.mean(hidden * hidden, axis=1, keepdims=True)
    normed = (hidden * lax.rsqrt(mean_square + 1e-06)).astype(BF)
    normed = jnp.concatenate([normed, routing], axis=1)

    far = flip(normed, "ctx", 2)
    across = flip(normed, "exp", 1)
    near = flip(normed, "ctx", 1)
    near_across = flip_both(normed)
    far_across = flip(far, "exp", 1)
    last_across = flip_both(far)
    last = flip(far, "ctx", 1)
    early = lax.optimization_barrier((normed, near, far, across, near_across))
    late = lax.optimization_barrier((far_across, last_across, last))
    pieces = [normed, near, far, last, across, near_across, far_across, last_across]
    pieces += [flip(piece, "tp", 1) for piece in early[:3] + late[2:] + early[3:] + late[:2]]
    sums = cube_experts(
        first.astype(jnp.int32).reshape(1), pieces, w_gate, w_up, w_down, slots
    )
    return (hidden + sums_back(sums[:3], sums[3:], part)).astype(BF)


def solution(mesh):
    in_specs = (
        P(("groups", "ctx"), ("exp", "tp")),
        P(("groups", "ctx"), None),
        P(("groups", "ctx"), None),
        P(("exp", "tp"), None),
        P(("groups", "ctx", "exp", "tp"), None),
        P(("groups", "ctx", "exp"), None),
        P(("groups", "ctx", "exp"), None),
        P(("ctx", "exp"), None, "tp"),
        P(("ctx", "exp"), None, "tp"),
        P(("ctx", "exp"), "tp", None),
    )
    out_specs = P(("groups", "ctx", "exp", "tp"), None)
    return jax.shard_map(
        on_device, mesh=mesh, in_specs=in_specs, out_specs=out_specs, check_vma=False
    )
```
